32 devices in a mesh: row: 8 (over z, x), col: 4 (over y, core).
Axes of the slice: x: 2, y: 2, z: 4, core: 2. Of those that a mesh axis runs over, the one named last changes fastest.
Arguments:
- tokens: bfloat16 [8192, 2048], P('row', 'col'), may hold values from -6 to 6
- lengths: int32 [8], P('row'), may hold values from 512 to 1024, as said below
- norm_in: float32 [2048], replicated, may hold values from 0.25 to 2.9
- q_weight: bfloat16 [2048, 2048], P('row', 'col'), may hold values from -0.125 to 0.125
- k_weight: bfloat16 [2048, 2048], P('row', 'col'), may hold values from -0.125 to 0.125
- v_weight: bfloat16 [2048, 2048], P('row', 'col'), may hold values from -0.125 to 0.125
- conv_q: float32 [4, 2048], P(None, 'col'), may hold values from -3 to 3
- conv_k: float32 [4, 2048], P(None, 'col'), may hold values from -3 to 3
- conv_v: float32 [4, 2048], P(None, 'col'), may hold values from -3 to 3
- beta_weight: bfloat16 [2048, 16], P('row', 'col'), may hold values from -0.125 to 0.125
- head_gain: float32 [128], replicated, may hold values from 0.5 to 1.5
- out_weight: bfloat16 [2048, 2048], P('col', 'row'), may hold values from -0.125 to 0.125
- norm_mid: float32 [2048], replicated, may hold values from 0.25 to 2.9
- gate_weight: bfloat16 [2048, 5632], P('row', 'col'), may hold values from -0.125 to 0.125
- up_weight: bfloat16 [2048, 5632], P('row', 'col'), may hold values from -0.125 to 0.125
- down_weight: bfloat16 [5632, 2048], P('col', 'row'), may hold values from -0.078125 to 0.078125
- cotangent: bfloat16 [8192, 2048], P('row', 'col'), may hold values from -6 to 6
Outputs:
- layer_out: bfloat16 [8192, 2048], P('row', 'col')
- grad_tokens: float32 [8192, 2048], P('row', 'col')
- grad_norm_in: float32 [2048], replicated
- grad_q: float32 [2048, 2048], P('row', 'col')
- grad_k: float32 [2048, 2048], P('row', 'col')
- grad_v: float32 [2048, 2048], P('row', 'col')
- grad_conv_q: float32 [4, 2048], P(None, 'col')
- grad_conv_k: float32 [4, 2048], P(None, 'col')
- grad_conv_v: float32 [4, 2048], P(None, 'col')
- grad_beta: float32 [2048, 16], P('row', 'col')
- grad_head_gain: float32 [128], replicated
- grad_out: float32 [2048, 2048], P('col', 'row')
- grad_norm_mid: float32 [2048], replicated
- grad_gate: float32 [2048, 5632], P('row', 'col')
- grad_up: float32 [2048, 5632], P('row', 'col')
- grad_down: float32 [5632, 2048], P('col', 'row')
The draws below stay inside these ranges and needn't reach their ends.
Inputs may be any that keep to these rules, and one draw needn't show every extreme that they name: `lengths`: each slot's live rows come first. Some slot is full and some slot holds exactly 512 live rows.
All inputs are finite; a program needn't handle non-finite values.
Results may differ from the reference program's by a relative error of at most 0.015.
Values may be sent and summed in bfloat16 or wider, within the bound.
No kernel may reach another device: no remote copies, remote signals or barrier semaphores. Data moves between devices by JAX's collectives and lax.ppermute only.
A program may use at most 320 MiB of HBM per device.

```python
import jax
import jax.numpy as jnp
from jax import lax

D = 2048
H = 16
DH = 128
FF = 5632
BLOCK = 64
CONV = 4
SLOT = 1024
HD = 2048
SEQS = 8
TOKENS = 8192


def draw_lengths(key, part):
    key = jax.random.fold_in(key, 7)
    first_key, second_key = jax.random.split(key)
    drawn_lengths = jax.random.randint(first_key, (SEQS,), SLOT // 2, SLOT + 1)
    full_slot = jax.random.randint(second_key, (), 0, SEQS)
    slot_ids = jnp.arange(SEQS)
    drawn_lengths = jnp.where(slot_ids == full_slot, SLOT, drawn_lengths)
    drawn_lengths = jnp.where(slot_ids == (full_slot + 1) % SEQS, SLOT // 2, drawn_lengths)
    return drawn_lengths.astype(jnp.int32)


def rising_gain(key, start, end, rough):
    place = jnp.arange(D, dtype=jnp.float32) / (D - 1)
    trend = start * (end / start) ** place
    factor = jax.random.uniform(key, (D,), jnp.float32, 1.0 - rough, 1.0 + rough)
    return (trend * factor).astype(jnp.float32)


def draw_norm_in(key, part):
    key = jax.random.fold_in(key, 11)
    return rising_gain(key, 0.4, 2.0, 0.2)


def draw_norm_mid(key, part):
    key = jax.random.fold_in(key, 13)
    return rising_gain(key, 0.4, 2.0, 0.2)


def block_scale(rng, shape, cuts, smallest, largest):
    level = 1.0
    for position, parts in cuts:
        steps = jax.random.uniform(jax.random.fold_in(jax.random.fold_in(rng, 6), position), (parts,), jnp.float32, smallest / len(cuts), largest / len(cuts))
        level = level * jnp.repeat(jnp.exp(steps), shape[position] // parts).reshape((-1,) + (1,) * (len(shape) - 1 - position))
    return level


def noise(stream_key, extent, spread, reach, cuts=(), kind=jnp.bfloat16):
    gain = block_scale(stream_key, extent, cuts, -0.22, 0.18) if cuts else 1.0
    values = jax.random.normal(stream_key, extent, jnp.float32) * spread * gain
    return jnp.minimum(jnp.maximum(values, -reach), reach).astype(kind)


def setup_inputs(seed: int = 0) -> dict:
    key_of = jax.random.split(jax.random.key(seed), 18)
    tokens = noise(key_of[0], (TOKENS, D), 1.0, 6.0, ((0, 8), (1, 4)))
    lengths = draw_lengths(jax.random.fold_in(key_of[17], 71), 0)
    norm_in = draw_norm_in(jax.random.fold_in(key_of[17], 71), 0)
    q_weight = noise(key_of[3], (D, HD), D ** -0.5, 0.125, ((0, 8), (1, 4)))
    k_weight = noise(key_of[4], (D, HD), D ** -0.5, 0.125, ((0, 8), (1, 4)))
    v_weight = noise(key_of[5], (D, HD), D ** -0.5, 0.125, ((0, 8), (1, 4)))
    conv_q = noise(key_of[6], (CONV, HD), 0.5, 3.0, ((1, 4),), jnp.float32)
    conv_k = noise(key_of[7], (CONV, HD), 0.5, 3.0, ((1, 4),), jnp.float32)
    conv_v = noise(key_of[8], (CONV, HD), 0.5, 3.0, ((1, 4),), jnp.float32)
    beta_weight = noise(key_of[9], (D, H), D ** -0.5, 0.125, ((0, 8), (1, 4)))
    head_gain = jnp.clip(1.0 + 0.1 * jax.random.normal(key_of[10], (DH,), jnp.float32), 0.5, 1.5)
    out_weight = noise(key_of[11], (HD, D), HD ** -0.5, 0.125, ((0, 4), (1, 8)))
    norm_mid = draw_norm_mid(jax.random.fold_in(key_of[17], 71), 0)
    gate_weight = noise(key_of[13], (D, FF), D ** -0.5, 0.125, ((0, 8), (1, 4)))
    up_weight = noise(key_of[14], (D, FF), D ** -0.5, 0.125, ((0, 8), (1, 4)))
    down_weight = noise(key_of[15], (FF, D), FF ** -0.5, 0.078125, ((0, 4), (1, 8)))
    cotangent = noise(key_of[16], (TOKENS, D), 1.0, 6.0, ((0, 8), (1, 4)))
    return dict(tokens=tokens, lengths=lengths, norm_in=norm_in, q_weight=q_weight, k_weight=k_weight, v_weight=v_weight, conv_q=conv_q, conv_k=conv_k, conv_v=conv_v, beta_weight=beta_weight, head_gain=head_gain, out_weight=out_weight, norm_mid=norm_mid, gate_weight=gate_weight, up_weight=up_weight, down_weight=down_weight, cotangent=cotangent)


epsilon = 1e-06
highest = lax.Precision.HIGHEST

@jax.custom_vjp
def low(v):
    return lax.optimization_barrier(v.astype(jnp.bfloat16)).astype(jnp.float32)

@jax.custom_vjp
def low_back(v):
    return v

def low_keep(v):
    return (low(v), None)

def low_pass(kept, grad):
    return (grad,)

def back_keep(v):
    return (v, None)

def back_low(kept, grad):
    return (low(grad),)
low.defvjp(low_keep, low_pass)
low_back.defvjp(back_keep, back_low)

def causal_conv(projected, kernel):
    length = projected.shape[0]
    padded = jnp.pad(projected, ((3, 0), (0, 0)))
    summed = kernel[0] * padded[0:length]
    for offset in range(1, 4):
        summed = summed + kernel[offset] * padded[offset:offset + length]
    return summed

def delta_block(states, blocks):
    queries, keys_in, values_in, strength = blocks
    block_len = keys_in.shape[1]
    key_width = keys_in.shape[2]
    row_ids = lax.broadcasted_iota(jnp.int32, (block_len, block_len), 0)
    col_ids = lax.broadcasted_iota(jnp.int32, (block_len, block_len), 1)
    strict_lower = (row_ids > col_ids).astype(jnp.float32)
    upto_lower = (row_ids >= col_ids).astype(jnp.float32)
    key_gram = jnp.einsum('hcd,hed->hce', keys_in, keys_in, precision=highest)
    system = jnp.eye(block_len, dtype=jnp.float32) + strength[:, :, None] * key_gram * strict_lower
    right_side = strength[:, :, None] * jnp.concatenate([keys_in, values_in], axis=2)
    solved = lax.linalg.triangular_solve(system, right_side, left_side=True, lower=True, unit_diagonal=True)
    w_factors = solved[:, :, :key_width]
    u_factors = solved[:, :, key_width:]
    fresh_vals = u_factors - jnp.einsum('hcd,hde->hce', w_factors, states, precision=highest)
    scores = jnp.einsum('hcd,hed->hce', queries, keys_in, precision=highest) * upto_lower
    output = jnp.einsum('hcd,hde->hce', queries, states, precision=highest)
    output = output + jnp.einsum('hce,hed->hcd', scores, fresh_vals, precision=highest)
    states = states + jnp.einsum('hcd,hce->hde', keys_in, fresh_vals, precision=highest)
    return (states, output)

def delta_mixer(q_proj, k_proj, v_proj, beta_logit, conv_q, conv_k, conv_v, head_gain):
    head_dim = head_gain.shape[0]
    head_count = beta_logit.shape[1]
    length = q_proj.shape[0]
    block_count = length // BLOCK
    queries = jax.nn.silu(causal_conv(q_proj, conv_q)) * head_dim ** (-0.5)
    keys_raw = jax.nn.silu(causal_conv(k_proj, conv_k)).reshape(length, head_count, head_dim)
    keys_unit = keys_raw * lax.rsqrt(lax.optimization_barrier(jnp.sum(keys_raw * keys_raw, axis=2, keepdims=True)) + epsilon)
    values = jax.nn.silu(causal_conv(v_proj, conv_v))
    strength = jax.nn.sigmoid(beta_logit)

    def split_blocks(tensor):
        return tensor.reshape(block_count, BLOCK, head_count, head_dim).transpose(0, 2, 1, 3)
    blocks = (split_blocks(queries), split_blocks(keys_unit), split_blocks(values), strength.reshape(block_count, BLOCK, head_count).transpose(0, 2, 1))
    start_state = jnp.zeros((head_count, head_dim, head_dim), jnp.float32)
    final_state, pieces = lax.scan(jax.checkpoint(delta_block), start_state, blocks)
    merged = pieces.transpose(0, 2, 1, 3).reshape(length, head_count, head_dim)
    normed = merged * lax.rsqrt(lax.optimization_barrier(jnp.mean(merged * merged, axis=2, keepdims=True)) + epsilon) * head_gain
    return normed.reshape(length, head_count * head_dim)

def rms_scale(rows_in, gain_vec):
    return rows_in * lax.rsqrt(lax.optimization_barrier(jnp.mean(rows_in * rows_in, axis=1, keepdims=True)) + epsilon) * gain_vec

def matmul(left, right):
    return jnp.dot(left.astype(jnp.float32), right.astype(jnp.float32), precision=highest, preferred_element_type=jnp.float32)

def layer_forward(x_rows, weights, live_rows):
    norm_in, q_weight, k_weight, v_weight, conv_q, conv_k, conv_v, beta_weight, head_gain, out_weight, norm_mid, gate_weight, up_weight, down_weight = weights
    normed = low(rms_scale(x_rows, norm_in))
    q_proj = low_back(matmul(normed, q_weight))
    k_proj = low_back(matmul(normed, k_weight))
    v_proj = low_back(matmul(normed, v_weight))
    beta_logit = low_back(matmul(normed, beta_weight))
    mixed = low(delta_mixer(q_proj, k_proj, v_proj, beta_logit, conv_q, conv_k, conv_v, head_gain))
    branch = low_back(matmul(mixed, out_weight))
    middle = x_rows + live_rows * branch
    normed_mid = low(rms_scale(low(middle), norm_mid))
    gate_val = low_back(matmul(normed_mid, gate_weight))
    up_val = low_back(matmul(normed_mid, up_weight))
    hidden = low(jax.nn.silu(gate_val) * up_val)
    return middle + live_rows * matmul(hidden, down_weight)

def reference(tokens, lengths, norm_in, q_weight, k_weight, v_weight, conv_q, conv_k, conv_v, beta_weight, head_gain, out_weight, norm_mid, gate_weight, up_weight, down_weight, cotangent):
    params = tuple((weight.astype(jnp.float32) for weight in (norm_in, q_weight, k_weight, v_weight, conv_q, conv_k, conv_v, beta_weight, head_gain, out_weight, norm_mid, gate_weight, up_weight, down_weight)))
    token_seqs = tokens.astype(jnp.float32).reshape(SEQS, SLOT, D)
    cot_seqs = cotangent.astype(jnp.float32).reshape(SEQS, SLOT, D)
    positions = jnp.arange(SLOT, dtype=jnp.int32)

    def per_sequence(grad_sums, inputs):
        x_rows, cot_rows, seq_length = inputs
        live_rows = (positions < seq_length).astype(jnp.float32)[:, None]

        def apply_layer(rows_in, weights):
            return layer_forward(rows_in, weights, live_rows)
        result, pullback = jax.vjp(apply_layer, x_rows, params)
        grad_rows, grad_weights = pullback(cot_rows)
        grad_sums = jax.tree.map(jnp.add, grad_sums, grad_weights)
        return (grad_sums, (result.astype(jnp.bfloat16), grad_rows))
    zero_sums = jax.tree.map(jnp.zeros_like, params)
    grad_sums, (outputs, grad_rows) = lax.scan(per_sequence, zero_sums, (token_seqs, cot_seqs, lengths.astype(jnp.int32)))
    g_norm_in, g_query, g_key, g_value, g_conv_q, g_conv_k, g_conv_v, g_beta, g_head, g_out, g_norm_mid, g_gate, g_up, g_down = grad_sums
    return (outputs.reshape(TOKENS, D), grad_rows.reshape(TOKENS, D), g_norm_in, g_query, g_key, g_value, g_conv_q, g_conv_k, g_conv_v, g_beta, g_head, g_out, g_norm_mid, g_gate, g_up, g_down)
```

```python
import functools
import jax
import jax.numpy as jnp
from jax import lax
from jax.experimental import pallas as pl
from jax.experimental.pallas import tpu as pltpu
from jax.sharding import PartitionSpec as P

CHUNK = 128
EPS = 1e-6
bf16 = jnp.bfloat16
f32 = jnp.float32


def split(x):
    high = x.astype(bf16)
    return high, (x - high.astype(f32)).astype(bf16)


def mm(a, b, ca=1, cb=0):
    def dg(u, v):
        return lax.dot_general(u, v, (((ca,), (cb,)), ((), ())), preferred_element_type=f32)

    return dg(a[0], b[0]) + (dg(a[0], b[1]) + dg(a[1], b[0]))


def sigmoid(x):
    return 1.0 / (1.0 + jnp.exp(-x))


def masks(n):
    r = lax.broadcasted_iota(jnp.int32, (n, n), 0)
    c = lax.broadcasted_iota(jnp.int32, (n, n), 1)
    return r, c


def unit_lower_inverse(lows, r, c):
    n = lows[0].shape[0]
    eye = jnp.where(r == c, 1.0, 0.0)
    invs = [eye - jnp.where(r // 2 == c // 2, low, 0.0) for low in lows]
    size = 2
    while size < n:
        mask = (r // (2 * size) == c // (2 * size)) & (r // size != c // size)
        offs = [split(jnp.where(mask, low, 0.0)) for low in lows]
        parts = [split(inv) for inv in invs]
        right = [split(mm(off, part)) for off, part in zip(offs, parts)]
        invs = [inv - mm(part, x) for inv, part, x in zip(invs, parts, right)]
        size *= 2
    return invs


def conv_rows(padded, taps, first):
    out = taps[0:1] * padded[first : first + CHUNK]
    for j in range(1, 4):
        out = out + taps[j : j + 1] * padded[first + j : first + j + CHUNK]
    return out


def fwd_kernel(heads, dh, x_ref, conv_ref, gain_ref, mixed_ref, o_ref, n_ref, t_ref, s_ref, state, halo):
    hd = heads * dh

    @pl.when(pl.program_id(0) == 0)
    def _():
        state[...] = jnp.zeros_like(state)
        halo[...] = jnp.zeros_like(halo)

    r, c = masks(CHUNK)
    each = range(heads)
    acts = []
    for p in range(3):
        for h in each:
            cols = slice(p * hd + h * dh, p * hd + (h + 1) * dh)
            y = conv_rows(jnp.concatenate([halo[:, cols], x_ref[:, cols]], 0), conv_ref[:, cols], 5)
            acts.append(y * sigmoid(y))
    qs = [split(acts[h] * dh ** -0.5) for h in each]
    ks = []
    for h in each:
        k = acts[heads + h]
        ks.append(split(k * lax.rsqrt(jnp.sum(k * k, axis=1, keepdims=True) + EPS)))
    b = [sigmoid(x_ref[:, 3 * hd + h : 3 * hd + h + 1]) for h in each]
    lows = [jnp.where(r > c, b[h] * mm(ks[h], ks[h], 1, 1), 0.0) for h in each]
    invs = unit_lower_inverse(lows, r, c)
    scores = [split(jnp.where(r >= c, mm(qs[h], ks[h], 1, 1), 0.0)) for h in each]
    s = [state[h] for h in each]
    ss = [split(s[h]) for h in each]
    right = [split(b[h] * (acts[2 * heads + h] - mm(ks[h], ss[h]))) for h in each]
    fresh = [mm(split(invs[h]), right[h]) for h in each]
    fs = [split(fresh[h]) for h in each]
    outs = [mm(qs[h], ss[h]) + mm(scores[h], fs[h]) for h in each]
    for h in each:
        state[h] = s[h] + mm(ks[h], fs[h], 0, 0)
        cols = slice(h * dh, (h + 1) * dh)
        s_ref[0, h] = s[h]
        t_ref[0, h] = invs[h]
        n_ref[:, cols] = fresh[h]
        o = outs[h]
        o_ref[:, cols] = o
        norm = lax.rsqrt(jnp.mean(o * o, axis=1, keepdims=True) + EPS)
        mixed_ref[:, cols] = (o * norm * gain_ref[...]).astype(bf16)
    halo[...] = x_ref[CHUNK - 8 :, : 3 * hd]


def bwd_kernel(heads, dh, x_ref, prev_ref, conv_ref, gain_ref, m_ref, o_ref, n_ref, t_ref, s_ref,
               low_ref, gconv_ref, ggain_ref, inner_ref, dstate, ghead):
    hd = heads * dh
    step = pl.program_id(0)

    @pl.when(step == 0)
    def _():
        dstate[...] = jnp.zeros_like(dstate)
        ghead[...] = jnp.zeros_like(ghead)
        gconv_ref[...] = jnp.zeros_like(gconv_ref)
        ggain_ref[...] = jnp.zeros_like(ggain_ref)

    has_prev = jnp.where(step == pl.num_programs(0) - 1, 0.0, 1.0)
    r, c = masks(CHUNK)
    lane = lax.broadcasted_iota(jnp.int32, (CHUNK, 128), 1)
    each = range(heads)
    scale = dh ** -0.5
    cuts = [slice(h * dh, (h + 1) * dh) for h in each]
    ys, sigs = [], []
    for p in range(3):
        for h in each:
            cols = slice(p * hd + h * dh, p * hd + (h + 1) * dh)
            padded = jnp.concatenate([prev_ref[:, cols] * has_prev, x_ref[:, cols]], 0)
            y = conv_rows(padded, conv_ref[:, cols], 5)
            ys.append(y)
            sigs.append(sigmoid(y))
    qs = [split(ys[h] * sigs[h] * scale) for h in each]
    kr = [ys[heads + h] * sigs[heads + h] for h in each]
    kinv = [lax.rsqrt(jnp.sum(kr[h] * kr[h], axis=1, keepdims=True) + EPS) for h in each]
    ks = [split(kr[h] * kinv[h]) for h in each]
    b = [sigmoid(x_ref[:, 3 * hd + h : 3 * hd + h + 1]) for h in each]
    dos = []
    ggain = jnp.zeros((1, dh), f32)
    for h in each:
        o = o_ref[:, cuts[h]]
        mc = m_ref[:, cuts[h]]
        norm = lax.rsqrt(jnp.mean(o * o, axis=1, keepdims=True) + EPS)
        ggain = ggain + jnp.sum(mc * (o * norm), axis=0, keepdims=True)
        dn_ = mc * gain_ref[...]
        do = norm * dn_ - o * (norm * norm * norm * jnp.mean(dn_ * o, axis=1, keepdims=True))
        dos.append(split(do))
    scores = [split(jnp.where(r >= c, mm(qs[h], ks[h], 1, 1), 0.0)) for h in each]
    part = [mm(scores[h], dos[h], 0, 0) for h in each]
    d = [dstate[h] for h in each]
    ds = [split(d[h]) for h in each]
    dfresh = [split(part[h] + mm(ks[h], ds[h])) for h in each]
    db_ = [mm(split(t_ref[0, h]), dfresh[h], 0, 0) for h in each]
    dr = [b[h] * db_[h] for h in each]
    drs = [split(dr[h]) for h in each]
    for h in each:
        dstate[h] = d[h] + (mm(qs[h], dos[h], 0, 0) - mm(ks[h], drs[h], 0, 0))
    ss = [split(s_ref[0, h]) for h in each]
    fs = [split(n_ref[:, cuts[h]]) for h in each]
    resid = [ys[2 * heads + h] * sigs[2 * heads + h] - mm(ks[h], ss[h]) for h in each]
    gram = [mm(ks[h], ks[h], 1, 1) for h in each]
    da = [jnp.where(r > c, -mm(split(db_[h]), fs[h], 1, 1), 0.0) for h in each]
    dsc = [split(jnp.where(r >= c, mm(dos[h], fs[h], 1, 1), 0.0)) for h in each]
    dq = [mm(dos[h], ss[h], 1, 1) + mm(dsc[h], ks[h]) for h in each]
    dgs = [split(b[h] * da[h]) for h in each]
    dk = [mm(dsc[h], qs[h], 0, 0) + mm(fs[h], ds[h], 1, 1) for h in each]
    dk = [dk[h] - mm(drs[h], ss[h], 1, 1) for h in each]
    dk = [dk[h] + (mm(dgs[h], ks[h]) + mm(dgs[h], ks[h], 0, 0)) for h in each]
    beta_low = jnp.zeros((CHUNK, 128), f32)
    inner = jnp.zeros((CHUNK, dh), f32)
    for h in each:
        dbeta = jnp.sum(db_[h] * resid[h], axis=1, keepdims=True) + jnp.sum(da[h] * gram[h], axis=1, keepdims=True)
        beta_low = jnp.where(lane == h, dbeta * b[h] * (1.0 - b[h]), beta_low)
    dkr = [kinv[h] * dk[h] - kr[h] * (kinv[h] * kinv[h] * kinv[h] * jnp.sum(dk[h] * kr[h], axis=1, keepdims=True)) for h in each]
    cots = [dq[h] * scale for h in each] + dkr + dr
    for p in range(3):
        for h in each:
            i = p * heads + h
            cols = slice(p * hd + h * dh, p * hd + (h + 1) * dh)
            g = cots[i] * sigs[i] * (1.0 + ys[i] * (1.0 - sigs[i]))
            taps = conv_ref[:, cols]
            gp = jnp.concatenate([g, ghead[:, cols]], 0)
            padded = jnp.concatenate([prev_ref[:, cols] * has_prev, x_ref[:, cols]], 0)
            out = taps[3:4] * g
            for j in range(3):
                out = out + taps[j : j + 1] * gp[3 - j : 3 - j + CHUNK]
            low_ref[:, cols] = out.astype(bf16)
            inner = inner + out * x_ref[:, cols]
            for j in range(4):
                gconv_ref[j : j + 1, cols] += jnp.sum(g * padded[5 + j : 5 + j + CHUNK], axis=0, keepdims=True)
            ghead[:, cols] = g[0:8]
    low_ref[:, 3 * hd :] = beta_low.astype(bf16)
    inner = inner + beta_low * x_ref[:, 3 * hd :]
    inner_ref[...] = jnp.sum(inner, axis=1, keepdims=True)
    ggain_ref[...] += ggain


def mixer_forward(proj, conv, gain, heads, dh):
    rows, width = proj.shape
    hd = heads * dh
    steps = rows // CHUNK
    square = pl.BlockSpec((1, heads, dh, dh), lambda i: (i, 0, 0, 0))
    wide = pl.BlockSpec((CHUNK, hd), lambda i: (i, 0))
    flops = rows * heads * (20 * 3 * 2 * 128 * 128)
    return pl.pallas_call(
        functools.partial(fwd_kernel, heads, dh),
        grid=(steps,),
        in_specs=[
            pl.BlockSpec((CHUNK, width), lambda i: (i, 0)),
            pl.BlockSpec((4, 3 * hd), lambda i: (0, 0)),
            pl.BlockSpec((1, dh), lambda i: (0, 0)),
        ],
        out_specs=[wide, wide, wide, pl.BlockSpec((1, heads, CHUNK, CHUNK), lambda i: (i, 0, 0, 0)), square],
        out_shape=[
            jax.ShapeDtypeStruct((rows, hd), bf16),
            jax.ShapeDtypeStruct((rows, hd), f32),
            jax.ShapeDtypeStruct((rows, hd), f32),
            jax.ShapeDtypeStruct((steps, heads, CHUNK, CHUNK), f32),
            jax.ShapeDtypeStruct((steps, heads, dh, dh), f32),
        ],
        scratch_shapes=[pltpu.VMEM((heads, dh, dh), f32), pltpu.VMEM((8, 3 * hd), f32)],
        compiler_params=pltpu.CompilerParams(vmem_limit_bytes=40 * 2**20),
        cost_estimate=pl.CostEstimate(flops=flops, bytes_accessed=rows * (width * 4 + hd * 18), transcendentals=0),
        name="mixer_forward",
    )(proj, conv, gain)


def mixer_backward(proj, conv, gain, mixed_cot, kept, heads, dh):
    o, fresh, inv, states = kept
    rows, width = proj.shape
    hd = heads * dh
    steps = rows // CHUNK
    last = steps - 1
    per = CHUNK // 8
    square = pl.BlockSpec((1, heads, dh, dh), lambda i: (last - i, 0, 0, 0))
    wide = pl.BlockSpec((CHUNK, hd), lambda i: (last - i, 0))
    flops = rows * heads * (15 * 3 * 2 * 128 * 128)
    return pl.pallas_call(
        functools.partial(bwd_kernel, heads, dh),
        grid=(steps,),
        in_specs=[
            pl.BlockSpec((CHUNK, width), lambda i: (last - i, 0)),
            pl.BlockSpec((8, width), lambda i: (jnp.maximum((last - i) * per - 1, 0), 0)),
            pl.BlockSpec((4, 3 * hd), lambda i: (0, 0)),
            pl.BlockSpec((1, dh), lambda i: (0, 0)),
            wide, wide, wide,
            pl.BlockSpec((1, heads, CHUNK, CHUNK), lambda i: (last - i, 0, 0, 0)),
            square,
        ],
        out_specs=[
            pl.BlockSpec((CHUNK, width), lambda i: (last - i, 0)),
            pl.BlockSpec((4, 3 * hd), lambda i: (0, 0)),
            pl.BlockSpec((1, dh), lambda i: (0, 0)),
            pl.BlockSpec((CHUNK, 1), lambda i: (last - i, 0)),
        ],
        out_shape=[
            jax.ShapeDtypeStruct((rows, width), bf16),
            jax.ShapeDtypeStruct((4, 3 * hd), f32),
            jax.ShapeDtypeStruct((1, dh), f32),
            jax.ShapeDtypeStruct((rows, 1), f32),
        ],
        scratch_shapes=[pltpu.VMEM((heads, dh, dh), f32), pltpu.VMEM((8, 3 * hd), f32)],
        compiler_params=pltpu.CompilerParams(vmem_limit_bytes=40 * 2**20),
        cost_estimate=pl.CostEstimate(flops=flops, bytes_accessed=rows * (width * 6 + hd * 18), transcendentals=0),
        name="mixer_backward",
    )(proj, proj, conv, gain, mixed_cot, o, fresh, inv, states)


def live_column(length, rows):
    return (lax.broadcasted_iota(jnp.int32, (rows, 1), 0) < length).astype(f32)


def swap(x, axis, bit):
    n = lax.axis_size(axis)
    return lax.ppermute(x, axis, [(i, i ^ bit) for i in range(n)])


def bits_down(n):
    bits = []
    while n > 1:
        n //= 2
        bits.append(n)
    return bits


def sum_all(x, axis):
    for bit in bits_down(lax.axis_size(axis)):
        x = x + swap(x, axis, bit)
    return x


def spread_cols(shard):
    n = lax.axis_size("col")
    pieces = {0: shard}
    for bit in bits_down(n):
        for j in list(pieces):
            pieces[j | bit] = swap(pieces[j], "col", bit)
    return [pieces[j] for j in range(n)]


def sum_cols(piece):
    n = lax.axis_size("col")
    away = {}
    bit = 1
    kept = list(range(n))
    got = {}
    while bit < n:
        for j in [j for j in kept if j & bit]:
            mine = piece(j) + got[j] if j in got else piece(j)
            got_j = swap(mine.astype(bf16), "col", bit).astype(f32)
            base = j ^ bit
            got[base] = got[base] + got_j if base in got else got_j
        kept = [j for j in kept if not j & bit]
        bit *= 2
    return piece(0) + got[0]


def norm_kernel(width, me_ref, *refs):
    pieces, (gain_ref, normed_ref, factor_ref) = refs[:-3], refs[-3:]
    total = len(pieces) * width
    values = [p[...].astype(f32) for p in pieces]
    square = values[0] * values[0]
    for v in values[1:]:
        square = square + v * v
    factor = lax.rsqrt(jnp.sum(square, axis=1, keepdims=True) / total + EPS)
    factor_ref[...] = factor
    for j, v in enumerate(values):
        cols = pl.ds(pl.multiple_of((me_ref[0] ^ j) * width, width), width)
        normed_ref[:, cols] = (v * factor * gain_ref[:, cols]).astype(bf16)


def join_kernel(width, me_ref, *refs):
    pieces, out_ref = refs[:-1], refs[-1]
    for j, p in enumerate(pieces):
        out_ref[:, pl.ds(pl.multiple_of((me_ref[0] ^ j) * width, width), width)] = p[...]


TILE = 256


def join_call(kernel, pieces, extra, outs, name):
    rows, width = pieces[0].shape
    me = lax.axis_index("col").astype(jnp.int32).reshape(1)
    return pl.pallas_call(
        functools.partial(kernel, width),
        grid_spec=pltpu.PrefetchScalarGridSpec(
            num_scalar_prefetch=1,
            grid=(rows // TILE,),
            in_specs=[pl.BlockSpec((TILE, width), lambda i, m: (i, 0))] * len(pieces)
            + [pl.BlockSpec(e.shape, lambda i, m: (0, 0)) for e in extra],
            out_specs=[pl.BlockSpec((TILE, o.shape[1]), lambda i, m: (i, 0)) for o in outs],
        ),
        out_shape=outs,
        compiler_params=pltpu.CompilerParams(vmem_limit_bytes=24 * 2**20),
        cost_estimate=pl.CostEstimate(flops=rows * width * 16, bytes_accessed=rows * width * len(pieces) * 4, transcendentals=0),
        name=name,
    )(me, *pieces, *extra)


def join_norm(pieces, gain):
    rows, width = pieces[0].shape
    outs = [jax.ShapeDtypeStruct((rows, width * len(pieces)), bf16), jax.ShapeDtypeStruct((rows, 1), f32)]
    return join_call(norm_kernel, pieces, [gain.reshape(1, -1)], outs, "join_norm")


def join(pieces):
    rows, width = pieces[0].shape
    return join_call(join_kernel, pieces, [], [jax.ShapeDtypeStruct((rows, width * len(pieces)), bf16)], "join")[0]


def dot(a, b, ca=1, cb=0):
    return lax.dot_general(a, b, (((ca,), (cb,)), ((), ())), preferred_element_type=f32)


def gather_rows(shard):
    return lax.all_gather(shard, "row", axis=0, tiled=True)


def scatter_rows(grad):
    return lax.psum_scatter(grad.astype(bf16), "row", scatter_dimension=0, tiled=True)


def per_device(tokens, lengths, norm_in, q_weight, k_weight, v_weight, conv_q, conv_k, conv_v, beta_weight,
               head_gain, out_weight, norm_mid, gate_weight, up_weight, down_weight, cotangent):
    rows, width = tokens.shape
    dh = head_gain.shape[0]
    hd = q_weight.shape[1]
    heads = hd // dh
    ff = gate_weight.shape[1]
    col = lax.axis_index("col")
    feat = lax.axis_size("col") * width
    live = live_column(lengths[0], rows)
    live_low = live.astype(bf16)
    beta_pad = jnp.pad(beta_weight, ((0, 0), (0, 128 - beta_weight.shape[1])))
    w_in = gather_rows(jnp.concatenate([q_weight, k_weight, v_weight, beta_pad], 1))
    w_out = gather_rows(out_weight.T)
    w_ff = gather_rows(jnp.concatenate([gate_weight, up_weight], 1))
    w_down = gather_rows(down_weight.T)
    conv = jnp.concatenate([conv_q, conv_k, conv_v], 1)
    gain = head_gain.reshape(1, dh)
    gain_in = lax.dynamic_slice_in_dim(norm_in, col * width, width)
    gain_mid = lax.dynamic_slice_in_dim(norm_mid, col * width, width)
    tokens32 = tokens.astype(f32)

    def block(w, j):
        return lax.dynamic_slice_in_dim(w, (col ^ j) * width, width, 0)

    normed, factor_in = join_norm(spread_cols(tokens), norm_in)
    ffn_cot = join(spread_cols(cotangent * live_low))
    proj = dot(normed, w_in)
    mixed, *kept = mixer_forward(proj, conv, gain, heads, dh)
    branch = sum_cols(lambda j: dot(mixed, block(w_out, j), 1, 1))
    middle = tokens32 + live * branch
    mid_low = middle.astype(bf16)
    normed_mid, factor_mid = join_norm(spread_cols(mid_low), norm_mid)
    gate = dot(normed_mid, w_ff[:, :ff])
    up = dot(normed_mid, w_ff[:, ff:])
    gate_sig = jax.nn.sigmoid(gate)
    hidden = (gate * gate_sig * up).astype(bf16)
    grad_down = scatter_rows(dot(ffn_cot, hidden, 0, 0))
    hidden_cot = dot(ffn_cot, w_down)
    gate_cot = (hidden_cot * up * gate_sig * (1.0 + gate * (1.0 - gate_sig))).astype(bf16)
    up_cot = (hidden_cot * gate * gate_sig).astype(bf16)
    grad_gate = scatter_rows(dot(normed_mid, gate_cot, 0, 0))
    grad_up = scatter_rows(dot(normed_mid, up_cot, 0, 0))
    inner_mid = jnp.sum(gate_cot.astype(f32) * gate + up_cot.astype(f32) * up, axis=1, keepdims=True)
    inner_mid = sum_all(inner_mid.reshape(rows // 128, 128), "col").reshape(rows, 1) / factor_mid
    both_cot = jnp.concatenate([gate_cot, up_cot], 1)
    mid_cot = sum_cols(lambda j: dot(both_cot, block(w_ff, j), 1, 1))
    result = sum_cols(lambda j: dot(hidden, block(w_down, j), 1, 1))
    layer_out = (middle + live * result).astype(bf16)

    mid32 = mid_low.astype(f32)
    gmid_part = jnp.sum(mid_cot * mid32 * factor_mid, axis=0)
    middle_cot = cotangent.astype(f32) + factor_mid * gain_mid * mid_cot - mid32 * (factor_mid**3 * inner_mid / feat)
    branch_cot = join(spread_cols((live * middle_cot).astype(bf16)))
    mixed_cot = dot(branch_cot, w_out)
    grad_out = scatter_rows(dot(branch_cot, mixed, 0, 0))
    low, gconv, ghead, inner_in = mixer_backward(proj, conv, gain, mixed_cot, kept, heads, dh)
    grad_in = scatter_rows(dot(normed, low, 0, 0))
    inner_in = sum_all(inner_in.reshape(rows // 128, 128), "col").reshape(rows, 1) / factor_in
    in_cot = sum_cols(lambda j: dot(low, block(w_in, j), 1, 1))
    gin_part = jnp.sum(in_cot * tokens32 * factor_in, axis=0)
    grad_tokens = middle_cot + factor_in * gain_in * in_cot - tokens32 * (factor_in**3 * inner_in / feat)

    def own_cols(part):
        return lax.dynamic_update_slice_in_dim(jnp.zeros((feat,), f32), part, col * width, 0)

    sizes = [feat, feat, dh]
    wide = sum_all(jnp.concatenate([own_cols(gin_part), own_cols(gmid_part), ghead[0]]).reshape(-1, 128), "col")
    small = sum_all(jnp.concatenate([wide, gconv.reshape(-1, 128)], 0), "row")
    wide, gconv = small[: wide.shape[0]].reshape(-1), small[wide.shape[0] :].reshape(gconv.shape)
    g_in = grad_in.astype(f32)
    return (
        layer_out,
        grad_tokens,
        wide[:feat],
        g_in[:, :hd],
        g_in[:, hd : 2 * hd],
        g_in[:, 2 * hd : 3 * hd],
        gconv[:, :hd],
        gconv[:, hd : 2 * hd],
        gconv[:, 2 * hd :],
        g_in[:, 3 * hd : 3 * hd + beta_weight.shape[1]],
        wide[2 * feat :],
        grad_out.astype(f32).T,
        wide[feat : 2 * feat],
        grad_gate.astype(f32),
        grad_up.astype(f32),
        grad_down.astype(f32).T,
    )


def solution(mesh):
    split_both, features, turned = P("row", "col"), P(None, "col"), P("col", "row")
    return jax.shard_map(
        per_device,
        mesh=mesh,
        in_specs=(split_both, P("row"), P(), split_both, split_both, split_both, features, features, features,
                  split_both, P(), turned, P(), split_both, split_both, turned, split_both),
        out_specs=(split_both, split_both, P(), split_both, split_both, split_both, features, features, features,
                   split_both, P(), turned, P(), split_both, split_both, turned),
        check_vma=False,
    )
```

```python
import functools
import jax
import jax.numpy as jnp
from jax import lax
from jax.experimental import pallas as pl
from jax.experimental.pallas import tpu as pltpu
from jax.sharding import PartitionSpec as P

CHUNK = 128
EPS = 1e-6
FREE = pl.CostEstimate(flops=0, bytes_accessed=0, transcendentals=0)
bf16 = jnp.bfloat16
f32 = jnp.float32


def split(x):
    high = x.astype(bf16)
    return high, (x - high.astype(f32)).astype(bf16)


def mm(a, b, ca=1, cb=0):
    def dg(u, v):
        return lax.dot_general(u, v, (((ca,), (cb,)), ((), ())), preferred_element_type=f32)

    return dg(a[0], b[0]) + (dg(a[0], b[1]) + dg(a[1], b[0]))


def sigmoid(x):
    return 1.0 / (1.0 + jnp.exp(-x))


def masks(n):
    r = lax.broadcasted_iota(jnp.int32, (n, n), 0)
    c = lax.broadcasted_iota(jnp.int32, (n, n), 1)
    return r, c


def unit_lower_inverse(lows, r, c):
    n = lows[0].shape[0]
    eye = jnp.where(r == c, 1.0, 0.0)
    invs = [eye - jnp.where(r // 2 == c // 2, low, 0.0) for low in lows]
    size = 2
    while size < n:
        mask = (r // (2 * size) == c // (2 * size)) & (r // size != c // size)
        offs = [split(jnp.where(mask, low, 0.0)) for low in lows]
        parts = [split(inv) for inv in invs]
        right = [split(mm(off, part)) for off, part in zip(offs, parts)]
        invs = [inv - mm(part, x) for inv, part, x in zip(invs, parts, right)]
        size *= 2
    return invs


def conv_rows(padded, taps, first):
    out = taps[0:1] * padded[first : first + CHUNK]
    for j in range(1, 4):
        out = out + taps[j : j + 1] * padded[first + j : first + j + CHUNK]
    return out


def fwd_kernel(heads, dh, x_ref, conv_ref, gain_ref, mixed_ref, o_ref, n_ref, t_ref, s_ref, state, halo):
    hd = heads * dh

    @pl.when(pl.program_id(0) == 0)
    def _():
        state[...] = jnp.zeros_like(state)
        halo[...] = jnp.zeros_like(halo)

    r, c = masks(CHUNK)
    each = range(heads)
    acts = []
    for p in range(3):
        for h in each:
            cols = slice(p * hd + h * dh, p * hd + (h + 1) * dh)
            y = conv_rows(jnp.concatenate([halo[:, cols], x_ref[:, cols]], 0), conv_ref[:, cols], 5)
            acts.append(y * sigmoid(y))
    qs = [split(acts[h] * dh ** -0.5) for h in each]
    ks = []
    for h in each:
        k = acts[heads + h]
        ks.append(split(k * lax.rsqrt(jnp.sum(k * k, axis=1, keepdims=True) + EPS)))
    b = [sigmoid(x_ref[:, 3 * hd + h : 3 * hd + h + 1]) for h in each]
    lows = [jnp.where(r > c, b[h] * mm(ks[h], ks[h], 1, 1), 0.0) for h in each]
    invs = unit_lower_inverse(lows, r, c)
    scores = [split(jnp.where(r >= c, mm(qs[h], ks[h], 1, 1), 0.0)) for h in each]
    s = [state[h] for h in each]
    ss = [split(s[h]) for h in each]
    right = [split(b[h] * (acts[2 * heads + h] - mm(ks[h], ss[h]))) for h in each]
    fresh = [mm(split(invs[h]), right[h]) for h in each]
    fs = [split(fresh[h]) for h in each]
    outs = [mm(qs[h], ss[h]) + mm(scores[h], fs[h]) for h in each]
    for h in each:
        state[h] = s[h] + mm(ks[h], fs[h], 0, 0)
        cols = slice(h * dh, (h + 1) * dh)
        s_ref[0, h] = s[h]
        t_ref[0, h] = invs[h]
        n_ref[:, cols] = fresh[h]
        o = outs[h]
        o_ref[:, cols] = o
        norm = lax.rsqrt(jnp.mean(o * o, axis=1, keepdims=True) + EPS)
        mixed_ref[:, cols] = (o * norm * gain_ref[...]).astype(bf16)
    halo[...] = x_ref[CHUNK - 8 :, : 3 * hd]


def bwd_kernel(heads, dh, x_ref, prev_ref, conv_ref, gain_ref, m_ref, o_ref, n_ref, t_ref, s_ref,
               low_ref, gconv_ref, ggain_ref, inner_ref, dstate, ghead):
    hd = heads * dh
    step = pl.program_id(0)

    @pl.when(step == 0)
    def _():
        dstate[...] = jnp.zeros_like(dstate)
        ghead[...] = jnp.zeros_like(ghead)
        gconv_ref[...] = jnp.zeros_like(gconv_ref)
        ggain_ref[...] = jnp.zeros_like(ggain_ref)

    has_prev = jnp.where(step == pl.num_programs(0) - 1, 0.0, 1.0)
    r, c = masks(CHUNK)
    lane = lax.broadcasted_iota(jnp.int32, (CHUNK, 128), 1)
    each = range(heads)
    scale = dh ** -0.5
    cuts = [slice(h * dh, (h + 1) * dh) for h in each]
    ys, sigs = [], []
    for p in range(3):
        for h in each:
            cols = slice(p * hd + h * dh, p * hd + (h + 1) * dh)
            padded = jnp.concatenate([prev_ref[:, cols] * has_prev, x_ref[:, cols]], 0)
            y = conv_rows(padded, conv_ref[:, cols], 5)
            ys.append(y)
            sigs.append(sigmoid(y))
    qs = [split(ys[h] * sigs[h] * scale) for h in each]
    kr = [ys[heads + h] * sigs[heads + h] for h in each]
    kinv = [lax.rsqrt(jnp.sum(kr[h] * kr[h], axis=1, keepdims=True) + EPS) for h in each]
    ks = [split(kr[h] * kinv[h]) for h in each]
    b = [sigmoid(x_ref[:, 3 * hd + h : 3 * hd + h + 1]) for h in each]
    dos = []
    ggain = jnp.zeros((1, dh), f32)
    for h in each:
        o = o_ref[:, cuts[h]]
        mc = m_ref[:, cuts[h]]
        norm = lax.rsqrt(jnp.mean(o * o, axis=1, keepdims=True) + EPS)
        ggain = ggain + jnp.sum(mc * (o * norm), axis=0, keepdims=True)
        dn_ = mc * gain_ref[...]
        do = norm * dn_ - o * (norm * norm * norm * jnp.mean(dn_ * o, axis=1, keepdims=True))
        dos.append(split(do))
    scores = [split(jnp.where(r >= c, mm(qs[h], ks[h], 1, 1), 0.0)) for h in each]
    part = [mm(scores[h], dos[h], 0, 0) for h in each]
    d = [dstate[h] for h in each]
    ds = [split(d[h]) for h in each]
    dfresh = [split(part[h] + mm(ks[h], ds[h])) for h in each]
    db_ = [mm(split(t_ref[0, h]), dfresh[h], 0, 0) for h in each]
    dr = [b[h] * db_[h] for h in each]
    drs = [split(dr[h]) for h in each]
    for h in each:
        dstate[h] = d[h] + (mm(qs[h], dos[h], 0, 0) - mm(ks[h], drs[h], 0, 0))
    ss = [split(s_ref[0, h]) for h in each]
    fs = [split(n_ref[:, cuts[h]]) for h in each]
    resid = [ys[2 * heads + h] * sigs[2 * heads + h] - mm(ks[h], ss[h]) for h in each]
    gram = [mm(ks[h], ks[h], 1, 1) for h in each]
    da = [jnp.where(r > c, -mm(split(db_[h]), fs[h], 1, 1), 0.0) for h in each]
    dsc = [split(jnp.where(r >= c, mm(dos[h], fs[h], 1, 1), 0.0)) for h in each]
    dq = [mm(dos[h], ss[h], 1, 1) + mm(dsc[h], ks[h]) for h in each]
    dgs = [split(b[h] * da[h]) for h in each]
    dk = [mm(dsc[h], qs[h], 0, 0) + mm(fs[h], ds[h], 1, 1) for h in each]
    dk = [dk[h] - mm(drs[h], ss[h], 1, 1) for h in each]
    dk = [dk[h] + (mm(dgs[h], ks[h]) + mm(dgs[h], ks[h], 0, 0)) for h in each]
    beta_low = jnp.zeros((CHUNK, 128), f32)
    inner = jnp.zeros((CHUNK, dh), f32)
    for h in each:
        dbeta = jnp.sum(db_[h] * resid[h], axis=1, keepdims=True) + jnp.sum(da[h] * gram[h], axis=1, keepdims=True)
        beta_low = jnp.where(lane == h, dbeta * b[h] * (1.0 - b[h]), beta_low)
    dkr = [kinv[h] * dk[h] - kr[h] * (kinv[h] * kinv[h] * kinv[h] * jnp.sum(dk[h] * kr[h], axis=1, keepdims=True)) for h in each]
    cots = [dq[h] * scale for h in each] + dkr + dr
    for p in range(3):
        for h in each:
            i = p * heads + h
            cols = slice(p * hd + h * dh, p * hd + (h + 1) * dh)
            g = cots[i] * sigs[i] * (1.0 + ys[i] * (1.0 - sigs[i]))
            taps = conv_ref[:, cols]
            gp = jnp.concatenate([g, ghead[:, cols]], 0)
            padded = jnp.concatenate([prev_ref[:, cols] * has_prev, x_ref[:, cols]], 0)
            out = taps[3:4] * g
            for j in range(3):
                out = out + taps[j : j + 1] * gp[3 - j : 3 - j + CHUNK]
            low_ref[:, cols] = out.astype(bf16)
            inner = inner + out * x_ref[:, cols]
            for j in range(4):
                gconv_ref[j : j + 1, cols] += jnp.sum(g * padded[5 + j : 5 + j + CHUNK], axis=0, keepdims=True)
            ghead[:, cols] = g[0:8]
    low_ref[:, 3 * hd :] = beta_low.astype(bf16)
    inner = inner + beta_low * x_ref[:, 3 * hd :]
    inner_ref[...] = jnp.sum(inner, axis=1, keepdims=True)
    ggain_ref[...] += ggain


def mixer_forward(proj, conv, gain, heads, dh):
    rows, width = proj.shape
    hd = heads * dh
    steps = rows // CHUNK
    square = pl.BlockSpec((1, heads, dh, dh), lambda i: (i, 0, 0, 0))
    wide = pl.BlockSpec((CHUNK, hd), lambda i: (i, 0))
    return pl.pallas_call(
        functools.partial(fwd_kernel, heads, dh),
        grid=(steps,),
        in_specs=[
            pl.BlockSpec((CHUNK, width), lambda i: (i, 0)),
            pl.BlockSpec((4, 3 * hd), lambda i: (0, 0)),
            pl.BlockSpec((1, dh), lambda i: (0, 0)),
        ],
        out_specs=[wide, wide, wide, pl.BlockSpec((1, heads, CHUNK, CHUNK), lambda i: (i, 0, 0, 0)), square],
        out_shape=[
            jax.ShapeDtypeStruct((rows, hd), bf16),
            jax.ShapeDtypeStruct((rows, hd), f32),
            jax.ShapeDtypeStruct((rows, hd), f32),
            jax.ShapeDtypeStruct((steps, heads, CHUNK, CHUNK), f32),
            jax.ShapeDtypeStruct((steps, heads, dh, dh), f32),
        ],
        scratch_shapes=[pltpu.VMEM((heads, dh, dh), f32), pltpu.VMEM((8, 3 * hd), f32)],
        compiler_params=pltpu.CompilerParams(vmem_limit_bytes=40 * 2**20),
        cost_estimate=FREE,
        name="mixer_forward",
    )(proj, conv, gain)


def mixer_backward(proj, conv, gain, mixed_cot, kept, heads, dh):
    o, fresh, inv, states = kept
    rows, width = proj.shape
    hd = heads * dh
    steps = rows // CHUNK
    last = steps - 1
    per = CHUNK // 8
    square = pl.BlockSpec((1, heads, dh, dh), lambda i: (last - i, 0, 0, 0))
    wide = pl.BlockSpec((CHUNK, hd), lambda i: (last - i, 0))
    return pl.pallas_call(
        functools.partial(bwd_kernel, heads, dh),
        grid=(steps,),
        in_specs=[
            pl.BlockSpec((CHUNK, width), lambda i: (last - i, 0)),
            pl.BlockSpec((8, width), lambda i: (jnp.maximum((last - i) * per - 1, 0), 0)),
            pl.BlockSpec((4, 3 * hd), lambda i: (0, 0)),
            pl.BlockSpec((1, dh), lambda i: (0, 0)),
            wide, wide, wide,
            pl.BlockSpec((1, heads, CHUNK, CHUNK), lambda i: (last - i, 0, 0, 0)),
            square,
        ],
        out_specs=[
            pl.BlockSpec((CHUNK, width), lambda i: (last - i, 0)),
            pl.BlockSpec((4, 3 * hd), lambda i: (0, 0)),
            pl.BlockSpec((1, dh), lambda i: (0, 0)),
            pl.BlockSpec((CHUNK, 1), lambda i: (last - i, 0)),
        ],
        out_shape=[
            jax.ShapeDtypeStruct((rows, width), bf16),
            jax.ShapeDtypeStruct((4, 3 * hd), f32),
            jax.ShapeDtypeStruct((1, dh), f32),
            jax.ShapeDtypeStruct((rows, 1), f32),
        ],
        scratch_shapes=[pltpu.VMEM((heads, dh, dh), f32), pltpu.VMEM((8, 3 * hd), f32)],
        compiler_params=pltpu.CompilerParams(vmem_limit_bytes=40 * 2**20),
        cost_estimate=FREE,
        name="mixer_backward",
    )(proj, proj, conv, gain, mixed_cot, o, fresh, inv, states)


def live_column(length, rows):
    return (lax.broadcasted_iota(jnp.int32, (rows, 1), 0) < length).astype(f32)


def swap(x, axis, bit):
    n = lax.axis_size(axis)
    return lax.ppermute(x, axis, [(i, i ^ bit) for i in range(n)])


def bits_down(n):
    bits = []
    while n > 1:
        n //= 2
        bits.append(n)
    return bits


def sum_all(x, axis):
    for bit in bits_down(lax.axis_size(axis)):
        x = x + swap(x, axis, bit)
    return x


def spread_cols(shard):
    n = lax.axis_size("col")
    pieces = {0: shard}
    for bit in bits_down(n):
        for j in list(pieces):
            pieces[j | bit] = swap(pieces[j], "col", bit)
    return [pieces[j] for j in range(n)]


class ColSum:
    def __init__(self, terms, block):
        self.terms, self.block = terms, block
        self.kept, self.got = list(range(lax.axis_size("col"))), {}

    def pieces(self, js, dtype, earlier):
        (left, pair), rest = self.terms[0], self.terms[1:]
        gots = [self.got.get(j) for j in js]
        return piece_call([(after(left, *earlier), pair)] + rest, self.block, js, gots, dtype)

    def send(self, bit, *earlier):
        js = [j for j in self.kept if j & bit]
        sent = self.pieces(js, bf16, earlier)
        for j, low in zip(js, sent):
            got, base = swap(low, "col", bit), j ^ bit
            self.got[base] = got if base not in self.got else self.got[base].astype(f32) + got.astype(f32)
        self.kept = [j for j in self.kept if not j & bit]
        return sent

    def send_last(self, *earlier):
        bit = 2
        while 2 * bit < lax.axis_size("col"):
            earlier = self.send(bit, *earlier)
            bit *= 2
        first = self.got.pop(0)
        sent = self.send(bit, *earlier)
        self.last = self.got[0]
        self.got[0] = first
        return sent

    def set_base(self, *earlier):
        self.base = self.pieces([0], f32, earlier)[0]
        return self.base

    def total(self):
        return self.base + self.last.astype(f32)


def norm_kernel(width, me_ref, *refs):
    pieces, (gain_ref, normed_ref, factor_ref) = refs[:-3], refs[-3:]
    total = len(pieces) * width
    values = [p[...].astype(f32) for p in pieces]
    square = values[0] * values[0]
    for v in values[1:]:
        square = square + v * v
    factor = lax.rsqrt(jnp.sum(square, axis=1, keepdims=True) / total + EPS)
    factor_ref[...] = factor
    half = width // 2
    for j, v in enumerate(values):
        for p in range(2):
            start = p * (total // 2) + (me_ref[0] ^ j) * half
            cols = pl.ds(pl.multiple_of(start, half), half)
            normed_ref[:, cols] = (v[:, p * half : (p + 1) * half] * factor * gain_ref[:, cols]).astype(bf16)


def join_kernel(width, me_ref, *refs):
    pieces, out_ref = refs[:-1], refs[-1]
    half = width // 2
    for j, piece in enumerate(pieces):
        for p in range(2):
            start = p * len(pieces) * half + (me_ref[0] ^ j) * half
            out_ref[:, pl.ds(pl.multiple_of(start, half), half)] = piece[:, p * half : (p + 1) * half]


TILE = 256


def join_call(kernel, pieces, extra, outs, name):
    rows, width = pieces[0].shape
    me = lax.axis_index("col").astype(jnp.int32).reshape(1)
    return pl.pallas_call(
        functools.partial(kernel, width),
        grid_spec=pltpu.PrefetchScalarGridSpec(
            num_scalar_prefetch=1,
            grid=(rows // TILE,),
            in_specs=[pl.BlockSpec((TILE, width), lambda i, m: (i, 0))] * len(pieces)
            + [pl.BlockSpec(e.shape, lambda i, m: (0, 0)) for e in extra],
            out_specs=[pl.BlockSpec((TILE, o.shape[1]), lambda i, m: (i, 0)) for o in outs],
        ),
        out_shape=outs,
        compiler_params=pltpu.CompilerParams(vmem_limit_bytes=24 * 2**20),
        cost_estimate=FREE,
        name=name,
    )(me, *pieces, *extra)


def join_norm(pieces, gain):
    rows, width = pieces[0].shape
    outs = [jax.ShapeDtypeStruct((rows, width * len(pieces)), bf16), jax.ShapeDtypeStruct((rows, 1), f32)]
    return join_call(norm_kernel, pieces, [gain.reshape(1, -1)], outs, "join_norm")


def join(pieces):
    rows, width = pieces[0].shape
    return join_call(join_kernel, pieces, [], [jax.ShapeDtypeStruct((rows, width * len(pieces)), bf16)], "join")[0]


def dot(a, b, ca=1, cb=0):
    return lax.dot_general(a, b, (((ca,), (cb,)), ((), ())), preferred_element_type=f32)


FREE = pl.CostEstimate(flops=0, bytes_accessed=0, transcendentals=0)


def tile_call(kernel, arrays, specs, outs, out_specs, grid, name, me=None):
    params = dict(
        compiler_params=pltpu.CompilerParams(vmem_limit_bytes=56 * 2**20), cost_estimate=FREE, name=name
    )
    if me is None:
        return pl.pallas_call(kernel, grid=grid, in_specs=specs, out_specs=out_specs, out_shape=outs, **params)(*arrays)
    grid_spec = pltpu.PrefetchScalarGridSpec(
        num_scalar_prefetch=1, grid=grid, in_specs=specs, out_specs=out_specs
    )
    return pl.pallas_call(kernel, grid_spec=grid_spec, out_shape=outs, **params)(me, *arrays)


def row_tile(width):
    return pl.BlockSpec((TILE, width), lambda i, *_: (i, 0))


def half_tile(width, which):
    return pl.BlockSpec((TILE, width), lambda i, *_: (i, which))


def whole(shape):
    return pl.BlockSpec(shape, lambda i, *_: (0, 0))


def halves_kernel(count, *refs):
    out = refs[-1]
    total = dot(refs[0][...], refs[1][...])
    for i in range(1, count):
        total = total + dot(refs[2 * i][...], refs[2 * i + 1][...])
    out[...] = total.astype(out.dtype)


def halves(left, pairs, dtype=f32):
    rows, half, width = left.shape[0], left.shape[1] // 2, pairs[0][1].shape[1]
    arrays, specs = [], []
    for which, weight in pairs:
        arrays += [left, weight]
        specs += [half_tile(half, which), whole(weight.shape)]
    return tile_call(functools.partial(halves_kernel, len(pairs)), arrays, specs,
                     jax.ShapeDtypeStruct((rows, width), dtype), row_tile(width), (rows // TILE,), "halves")


def both(refs):
    return dot(refs[0][...], refs[2][...]) + dot(refs[1][...], refs[3][...])


def hidden_kernel(*refs):
    gate_ref, up_ref, hidden_ref = refs[4:]
    up = both(refs)
    gate = gate_ref[...].astype(f32)
    up_ref[...] = up.astype(bf16)
    hidden_ref[...] = (gate * sigmoid(gate) * up).astype(bf16)


def both_specs(left, pair):
    half = left.shape[1] // 2
    return [left, left, *pair], [half_tile(half, 0), half_tile(half, 1), whole(pair[0].shape), whole(pair[1].shape)]


def hidden_call(left, pair, gate):
    rows, width = gate.shape
    tile = row_tile(width)
    arrays, specs = both_specs(left, pair)
    outs = [jax.ShapeDtypeStruct((rows, width), bf16)] * 2
    return tile_call(hidden_kernel, arrays + [gate], specs + [tile], outs, [tile, tile], (rows // TILE,), "hidden")


def cots_kernel(*refs):
    gate_ref, up_ref, gate_cot_ref, up_cot_ref, inner_ref = refs[4:]
    cot = both(refs)
    gate, up = gate_ref[...].astype(f32), up_ref[...].astype(f32)
    sig = sigmoid(gate)
    silu = gate * sig
    gate_cot = cot * up * (sig + silu * (1.0 - sig))
    up_cot = cot * silu
    gate_cot_ref[...] = gate_cot.astype(bf16)
    up_cot_ref[...] = up_cot.astype(bf16)
    inner_ref[...] = jnp.sum(gate_cot * gate + up_cot * up, axis=1, keepdims=True)


def cots_call(left, pair, gate, up):
    rows, width = gate.shape
    tile = row_tile(width)
    arrays, specs = both_specs(left, pair)
    outs = [jax.ShapeDtypeStruct((rows, width), bf16)] * 2 + [jax.ShapeDtypeStruct((rows, 1), f32)]
    return tile_call(cots_kernel, arrays + [gate, up], specs + [tile, tile], outs, [tile, tile, row_tile(1)],
                     (rows // TILE,), "cots")


def piece_kernel(count, pieces, has_got, me_ref, *refs):
    outs = refs[-pieces:]
    stride = 1 + 2 * pieces
    for n, out in enumerate(outs):
        width = out.shape[1] // 2
        for p in range(2):
            total = None
            for i in range(count):
                term = dot(refs[stride * i][...], refs[stride * i + 1 + 2 * n + p][...], 1, 1)
                total = term if total is None else total + term
            if has_got:
                total = total + refs[stride * count + n][:, p * width : (p + 1) * width].astype(f32)
            out[:, p * width : (p + 1) * width] = total.astype(out.dtype)


def piece_call(terms, block, js, gots, dtype):
    rows = terms[0][0].shape[0]
    me = jnp.stack([lax.axis_index("col") ^ j for j in js]).astype(jnp.int32)
    arrays, specs = [], []
    for left, pair in terms:
        arrays.append(left)
        specs.append(row_tile(left.shape[1]))
        for n in range(len(js)):
            arrays += pair
            specs += [pl.BlockSpec((block, w.shape[1]), lambda i, m, n=n: (m[n], 0)) for w in pair]
    has_got = gots[0] is not None
    if has_got:
        arrays += gots
        specs += [row_tile(2 * block)] * len(js)
    kernel = functools.partial(piece_kernel, len(terms), len(js), has_got)
    outs = [jax.ShapeDtypeStruct((rows, 2 * block), dtype)] * len(js)
    return tile_call(kernel, arrays, specs, outs, [row_tile(2 * block)] * len(js), (rows // TILE,), "piece", me)


def rows_kernel(left_ref, right_ref, *refs):
    total = dot(left_ref[...], right_ref[...], 0, 0)
    if len(refs) > 1:
        total = total + refs[0][...].astype(f32)
    refs[-1][...] = total.astype(bf16)


def rows_call(left, right, which, got=None):
    rows, half, width = left.shape[0], left.shape[1] // 2, right.shape[1]
    tile = 2 * TILE
    steps = half // tile
    arrays = [left, right] + ([] if got is None else [got])
    specs = [pl.BlockSpec((rows, tile), lambda i: (0, which * steps + i)), whole(right.shape)]
    out = pl.BlockSpec((tile, width), lambda i: (i, 0))
    specs += [] if got is None else [out]
    return tile_call(rows_kernel, arrays, specs, jax.ShapeDtypeStruct((half, width), bf16), out,
                     (steps,), "rows")


def parity_groups():
    n = lax.axis_size("row")
    return [list(range(p, n, 2)) for p in range(2)]


def after(x, *earlier):
    return lax.optimization_barrier((x,) + earlier)[0]


def gather_parity(shard):
    return lax.all_gather(shard, "row", axis=0, tiled=True, axis_index_groups=parity_groups())


def scatter_parity(part):
    return lax.psum_scatter(part, "row", scatter_dimension=0, tiled=True, axis_index_groups=parity_groups())


def other_rows(left, right):
    return rows_call(left, right, 1)


def own_rows(left, right, got):
    return rows_call(left, right, 0, got)


def flip(first, second):
    odd = (lax.axis_index("row") & 1) == 1
    return jnp.where(odd, second, first), jnp.where(odd, first, second)


def by_parity(x, chunk):
    lead, width = x.shape
    parts = x.reshape(lead, width // (2 * chunk), 2, chunk)
    first, second = flip(parts[:, :, 0], parts[:, :, 1])
    return jnp.concatenate([first.reshape(lead, width // 2), second.reshape(lead, width // 2)], 1)


def by_place(x, chunk):
    lead, width = x.shape
    shape = (lead, width // (2 * chunk), chunk)
    first, second = flip(x[:, : width // 2].reshape(shape), x[:, width // 2 :].reshape(shape))
    return jnp.stack([first, second], 2).reshape(lead, width)


def per_device(tokens, lengths, norm_in, q_weight, k_weight, v_weight, conv_q, conv_k, conv_v, beta_weight,
               head_gain, out_weight, norm_mid, gate_weight, up_weight, down_weight, cotangent):
    rows, width = tokens.shape
    dh = head_gain.shape[0]
    hd = q_weight.shape[1]
    heads = hd // dh
    ff = gate_weight.shape[1]
    col = lax.axis_index("col")
    feat = lax.axis_size("col") * width
    live = live_column(lengths[0], rows)
    live_low = live.astype(bf16)
    beta_pad = jnp.pad(beta_weight, ((0, 0), (0, 128 - beta_weight.shape[1])))
    in_mine = gather_parity(jnp.concatenate([q_weight, k_weight, v_weight, beta_pad], 1))
    out_mine = gather_parity(out_weight.T)
    gate_mine = gather_parity(gate_weight)
    up_mine = gather_parity(up_weight)
    down_turned = down_weight.T
    down_side = swap(down_turned, "row", 1)
    down_mine = gather_parity(down_turned)
    down_other = gather_parity(down_side)
    conv = jnp.concatenate([conv_q, conv_k, conv_v], 1)
    gain = head_gain.reshape(1, dh)
    gain_in = lax.dynamic_slice_in_dim(norm_in, col * width, width)
    gain_mid = lax.dynamic_slice_in_dim(norm_mid, col * width, width)
    chunk = q_weight.shape[0]
    tokens, cotangent = by_parity(tokens, chunk), by_parity(cotangent, chunk)
    gain_in, gain_mid = by_parity(gain_in[None], chunk), by_parity(gain_mid[None], chunk)
    norm_in, norm_mid = by_parity(norm_in[None], chunk), by_parity(norm_mid[None], chunk)
    tokens32 = tokens.astype(f32)

    block = width // 2

    half = feat // 2
    normed, factor_in = join_norm(spread_cols(tokens), norm_in)
    ffn_cot = join(spread_cols(cotangent * live_low))
    in_mine = after(in_mine, normed, ffn_cot, down_side)
    in_other, out_other = swap(in_mine, "row", 1), swap(out_mine, "row", 1)
    proj = halves(after(normed, out_mine), [(0, in_mine), (1, in_other)])
    gate_mine = after(gate_mine, proj)
    gate_other = swap(gate_mine, "row", 1)
    proj = after(proj, gate_mine)
    out_other = after(out_other, proj)
    w_in, w_out = (in_mine, in_other), (out_mine, out_other)
    mixed, *kept = mixer_forward(proj, conv, gain, heads, dh)
    branch = ColSum([(mixed, w_out)], block)
    sent = branch.send(1)
    sent = branch.send_last(*sent)
    up_mine = after(up_mine, *sent)
    up_other = swap(up_mine, "row", 1)
    branch.set_base(*sent)
    middle = tokens32 + live * after(branch.total(), gate_other)
    mid_low = middle.astype(bf16)
    normed_mid, factor_mid = join_norm(spread_cols(mid_low), after(norm_mid, up_mine))
    w_gate, w_up = (gate_mine, gate_other), (up_mine, up_other)
    gate = halves(normed_mid, [(0, gate_mine), (1, gate_other)], bf16)
    up, hidden = hidden_call(after(normed_mid, gate), w_up, gate)
    down_sent = other_rows(ffn_cot, hidden)
    down_got = swap(down_sent, "row", 1)
    w_down = after(down_mine, down_sent), after(down_other, down_sent)
    gate_cot, up_cot, inner_mid = cots_call(ffn_cot, w_down, gate, up)
    inner_mid = sum_all(inner_mid.reshape(rows // 128, 128), "col").reshape(rows, 1) / factor_mid
    mid_sum = ColSum([(gate_cot, w_gate), (up_cot, w_up)], block)
    sent = mid_sum.send(1)
    gate_sent = other_rows(after(normed_mid, *sent), gate_cot)
    gate_got = swap(gate_sent, "row", 1)
    sent = mid_sum.send_last(gate_sent)
    up_sent = other_rows(after(normed_mid, *sent), up_cot)
    up_got = swap(up_sent, "row", 1)
    mid_sum.set_base(up_sent)
    down_rows = own_rows(ffn_cot, hidden, after(down_got, mid_sum.base))
    grad_down = scatter_parity(down_rows)
    mid_cot = after(mid_sum.total(), down_rows)

    mid32 = mid_low.astype(f32)
    gmid_part = jnp.sum(mid_cot * mid32 * factor_mid, axis=0)
    middle_cot = cotangent.astype(f32) + factor_mid * gain_mid * mid_cot - mid32 * (factor_mid**3 * inner_mid / feat)
    branch_low = (live * middle_cot).astype(bf16)
    pieces = spread_cols(branch_low)
    result = ColSum([(hidden, w_down)], block)
    sent = result.send(1, branch_low)
    pieces[0] = after(pieces[0], *sent)
    branch_cot = join(pieces)
    mixed_cot = halves(branch_cot, [(0, out_mine), (1, out_other)])
    out_sent = other_rows(after(branch_cot, mixed_cot), mixed)
    out_got = swap(out_sent, "row", 1)
    gate_rows = own_rows(normed_mid, gate_cot, after(gate_got, out_sent, down_rows))
    grad_gate = scatter_parity(gate_rows)
    mixed_cot = after(mixed_cot, out_sent, gate_rows)
    low, gconv, ghead, inner_in = mixer_backward(proj, conv, gain, mixed_cot, kept, heads, dh)
    cut = 2 * hd
    qk, vb = low[:, :cut], low[:, cut:]
    qk_sent, vb_sent = other_rows(normed, qk), other_rows(normed, vb)
    qk_got, vb_got = swap(qk_sent, "row", 1), swap(vb_sent, "row", 1)
    up_rows = own_rows(normed_mid, up_cot, after(up_got, qk_sent, vb_sent, grad_down))
    grad_up = scatter_parity(up_rows)
    in_sum = ColSum([(low, w_in)], block)
    sent = in_sum.send(1, up_rows)
    sent = in_sum.send_last(*sent)
    out_rows = own_rows(branch_cot, mixed, after(out_got, grad_gate, *sent))
    grad_out = scatter_parity(out_rows)
    in_sum.set_base(out_rows)
    result.send_last(in_sum.base)
    result.set_base(in_sum.base)
    inner_in = sum_all(inner_in.reshape(rows // 128, 128), "col").reshape(rows, 1) / factor_in
    in_cot = in_sum.total()
    gin_part = jnp.sum(in_cot * tokens32 * factor_in, axis=0)
    grad_tokens = middle_cot + factor_in * gain_in * in_cot - tokens32 * (factor_in**3 * inner_in / feat)
    qk_rows = own_rows(normed, qk, after(qk_got, out_rows, gin_part, grad_up))
    grad_qk = scatter_parity(qk_rows)
    layer_out = (middle + live * result.total()).astype(bf16)

    def own_cols(part):
        part = by_place(part[None], chunk)[0]
        return lax.dynamic_update_slice_in_dim(jnp.zeros((feat,), f32), part, col * width, 0)

    sizes = [feat, feat, dh]
    wide = sum_all(jnp.concatenate([own_cols(gin_part), own_cols(gmid_part), ghead[0]]).reshape(-1, 128), "col")
    small = sum_all(jnp.concatenate([wide, gconv.reshape(-1, 128)], 0), "row")
    wide, gconv = small[: wide.shape[0]].reshape(-1), small[wide.shape[0] :].reshape(gconv.shape)
    vb_rows = own_rows(normed, vb, after(vb_got, qk_rows, small, layer_out, grad_tokens, grad_out))
    grad_vb = scatter_parity(vb_rows)
    g_qk, g_vb = grad_qk.astype(f32), grad_vb.astype(f32)
    return (
        by_place(layer_out, chunk),
        by_place(grad_tokens, chunk),
        wide[:feat],
        g_qk[:, :hd],
        g_qk[:, hd:],
        g_vb[:, :hd],
        gconv[:, :hd],
        gconv[:, hd : 2 * hd],
        gconv[:, 2 * hd :],
        g_vb[:, hd : hd + beta_weight.shape[1]],
        wide[2 * feat :],
        grad_out.astype(f32).T,
        wide[feat : 2 * feat],
        grad_gate.astype(f32),
        grad_up.astype(f32),
        grad_down.astype(f32).T,
    )


def solution(mesh):
    split_both, features, turned = P("row", "col"), P(None, "col"), P("col", "row")
    return jax.shard_map(
        per_device,
        mesh=mesh,
        in_specs=(split_both, P("row"), P(), split_both, split_both, split_both, features, features, features,
                  split_both, P(), turned, P(), split_both, split_both, turned, split_both),
        out_specs=(split_both, split_both, P(), split_both, split_both, split_both, features, features, features,
                   split_both, P(), turned, P(), split_both, split_both, turned),
        check_vma=False,
    )
```

```python
import functools
import jax
import jax.numpy as jnp
from jax import lax
from jax.experimental import pallas as pl
from jax.experimental.pallas import tpu as pltpu
from jax.sharding import PartitionSpec as P

CHUNK = 128
EPS = 1e-6
FREE = pl.CostEstimate(flops=2**20, bytes_accessed=2**18, transcendentals=0)
bf16 = jnp.bfloat16
f32 = jnp.float32


def split(x):
    high = x.astype(bf16)
    return high, (x - high.astype(f32)).astype(bf16)


def mm(a, b, ca=1, cb=0):
    def dg(u, v):
        return lax.dot_general(u, v, (((ca,), (cb,)), ((), ())), preferred_element_type=f32)

    return dg(a[0], b[0]) + (dg(a[0], b[1]) + dg(a[1], b[0]))


def sigmoid(x):
    return 0.5 * jnp.tanh(0.5 * x) + 0.5


def masks(n):
    r = lax.broadcasted_iota(jnp.int32, (n, n), 0)
    c = lax.broadcasted_iota(jnp.int32, (n, n), 1)
    return r, c


def unit_lower_inverse(lows, r, c):
    n = lows[0].shape[0]
    eye = jnp.where(r == c, 1.0, 0.0)
    invs = [eye - jnp.where(r // 2 == c // 2, low, 0.0) for low in lows]
    size = 2
    while size < n:
        mask = (r // (2 * size) == c // (2 * size)) & (r // size != c // size)
        offs = [split(jnp.where(mask, low, 0.0)) for low in lows]
        parts = [split(inv) for inv in invs]
        right = [split(mm(off, part)) for off, part in zip(offs, parts)]
        invs = [inv - mm(part, x) for inv, part, x in zip(invs, parts, right)]
        size *= 2
    return invs


def conv_rows(padded, taps, first):
    out = taps[0:1] * padded[first : first + CHUNK]
    for j in range(1, 4):
        out = out + taps[j : j + 1] * padded[first + j : first + j + CHUNK]
    return out


def fwd_kernel(heads, dh, x_ref, conv_ref, gain_ref, mixed_ref, o_ref, n_ref, t_ref, s_ref, state, halo):
    hd = heads * dh

    @pl.when(pl.program_id(0) == 0)
    def _():
        state[...] = jnp.zeros_like(state)
        halo[...] = jnp.zeros_like(halo)

    r, c = masks(CHUNK)
    each = range(heads)
    acts = []
    for p in range(3):
        for h in each:
            cols = slice(p * hd + h * dh, p * hd + (h + 1) * dh)
            y = conv_rows(jnp.concatenate([halo[:, cols], x_ref[:, cols]], 0), conv_ref[:, cols], 5)
            acts.append(y * sigmoid(y))
    qs = [split(acts[h] * dh ** -0.5) for h in each]
    ks = []
    for h in each:
        k = acts[heads + h]
        ks.append(split(k * lax.rsqrt(jnp.sum(k * k, axis=1, keepdims=True) + EPS)))
    b = [sigmoid(x_ref[:, 3 * hd + h : 3 * hd + h + 1]) for h in each]
    lows = [jnp.where(r > c, b[h] * mm(ks[h], ks[h], 1, 1), 0.0) for h in each]
    invs = unit_lower_inverse(lows, r, c)
    scores = [split(jnp.where(r >= c, mm(qs[h], ks[h], 1, 1), 0.0)) for h in each]
    s = [state[h] for h in each]
    ss = [split(s[h]) for h in each]
    right = [split(b[h] * (acts[2 * heads + h] - mm(ks[h], ss[h]))) for h in each]
    fresh = [mm(split(invs[h]), right[h]) for h in each]
    fs = [split(fresh[h]) for h in each]
    outs = [mm(qs[h], ss[h]) + mm(scores[h], fs[h]) for h in each]
    for h in each:
        state[h] = s[h] + mm(ks[h], fs[h], 0, 0)
        cols = slice(h * dh, (h + 1) * dh)
        s_ref[0, h] = s[h]
        t_ref[0, h] = invs[h]
        n_ref[:, cols] = fresh[h]
        o = outs[h]
        o_ref[:, cols] = o
        norm = lax.rsqrt(jnp.mean(o * o, axis=1, keepdims=True) + EPS)
        mixed_ref[:, cols] = (o * norm * gain_ref[...]).astype(bf16)
    halo[...] = x_ref[CHUNK - 8 :, : 3 * hd]


def bwd_kernel(heads, dh, x_ref, prev_ref, conv_ref, gain_ref, m_ref, o_ref, n_ref, t_ref, s_ref,
               low_ref, gconv_ref, ggain_ref, inner_ref, dstate, ghead):
    hd = heads * dh
    step = pl.program_id(0)

    @pl.when(step == 0)
    def _():
        dstate[...] = jnp.zeros_like(dstate)
        ghead[...] = jnp.zeros_like(ghead)
        gconv_ref[...] = jnp.zeros_like(gconv_ref)
        ggain_ref[...] = jnp.zeros_like(ggain_ref)

    has_prev = jnp.where(step == pl.num_programs(0) - 1, 0.0, 1.0)
    r, c = masks(CHUNK)
    lane = lax.broadcasted_iota(jnp.int32, (CHUNK, 128), 1)
    each = range(heads)
    scale = dh ** -0.5
    cuts = [slice(h * dh, (h + 1) * dh) for h in each]
    ys, sigs = [], []
    for p in range(3):
        for h in each:
            cols = slice(p * hd + h * dh, p * hd + (h + 1) * dh)
            padded = jnp.concatenate([prev_ref[:, cols] * has_prev, x_ref[:, cols]], 0)
            y = conv_rows(padded, conv_ref[:, cols], 5)
            ys.append(y)
            sigs.append(sigmoid(y))
    qs = [split(ys[h] * sigs[h] * scale) for h in each]
    kr = [ys[heads + h] * sigs[heads + h] for h in each]
    kinv = [lax.rsqrt(jnp.sum(kr[h] * kr[h], axis=1, keepdims=True) + EPS) for h in each]
    ks = [split(kr[h] * kinv[h]) for h in each]
    b = [sigmoid(x_ref[:, 3 * hd + h : 3 * hd + h + 1]) for h in each]
    dos = []
    ggain = jnp.zeros((1, dh), f32)
    for h in each:
        o = o_ref[:, cuts[h]]
        mc = m_ref[:, cuts[h]]
        norm = lax.rsqrt(jnp.mean(o * o, axis=1, keepdims=True) + EPS)
        ggain = ggain + jnp.sum(mc * (o * norm), axis=0, keepdims=True)
        dn_ = mc * gain_ref[...]
        do = norm * dn_ - o * (norm * norm * norm * jnp.mean(dn_ * o, axis=1, keepdims=True))
        dos.append(split(do))
    scores = [split(jnp.where(r >= c, mm(qs[h], ks[h], 1, 1), 0.0)) for h in each]
    part = [mm(scores[h], dos[h], 0, 0) for h in each]
    d = [dstate[h] for h in each]
    ds = [split(d[h]) for h in each]
    dfresh = [split(part[h] + mm(ks[h], ds[h])) for h in each]
    db_ = [mm(split(t_ref[0, h]), dfresh[h], 0, 0) for h in each]
    dr = [b[h] * db_[h] for h in each]
    drs = [split(dr[h]) for h in each]
    for h in each:
        dstate[h] = d[h] + (mm(qs[h], dos[h], 0, 0) - mm(ks[h], drs[h], 0, 0))
    ss = [split(s_ref[0, h]) for h in each]
    fs = [split(n_ref[:, cuts[h]]) for h in each]
    resid = [ys[2 * heads + h] * sigs[2 * heads + h] - mm(ks[h], ss[h]) for h in each]
    gram = [mm(ks[h], ks[h], 1, 1) for h in each]
    da = [jnp.where(r > c, -mm(split(db_[h]), fs[h], 1, 1), 0.0) for h in each]
    dsc = [split(jnp.where(r >= c, mm(dos[h], fs[h], 1, 1), 0.0)) for h in each]
    dq = [mm(dos[h], ss[h], 1, 1) + mm(dsc[h], ks[h]) for h in each]
    dgs = [split(b[h] * da[h]) for h in each]
    dk = [mm(dsc[h], qs[h], 0, 0) + mm(fs[h], ds[h], 1, 1) for h in each]
    dk = [dk[h] - mm(drs[h], ss[h], 1, 1) for h in each]
    dk = [dk[h] + (mm(dgs[h], ks[h]) + mm(dgs[h], ks[h], 0, 0)) for h in each]
    beta_low = jnp.zeros((CHUNK, 128), f32)
    inner = jnp.zeros((CHUNK, dh), f32)
    for h in each:
        dbeta = jnp.sum(db_[h] * resid[h], axis=1, keepdims=True) + jnp.sum(da[h] * gram[h], axis=1, keepdims=True)
        beta_low = jnp.where(lane == h, dbeta * b[h] * (1.0 - b[h]), beta_low)
    dkr = [kinv[h] * dk[h] - kr[h] * (kinv[h] * kinv[h] * kinv[h] * jnp.sum(dk[h] * kr[h], axis=1, keepdims=True)) for h in each]
    cots = [dq[h] * scale for h in each] + dkr + dr
    for p in range(3):
        for h in each:
            i = p * heads + h
            cols = slice(p * hd + h * dh, p * hd + (h + 1) * dh)
            g = cots[i] * sigs[i] * (1.0 + ys[i] * (1.0 - sigs[i]))
            taps = conv_ref[:, cols]
            gp = jnp.concatenate([g, ghead[:, cols]], 0)
            padded = jnp.concatenate([prev_ref[:, cols] * has_prev, x_ref[:, cols]], 0)
            out = taps[3:4] * g
            for j in range(3):
                out = out + taps[j : j + 1] * gp[3 - j : 3 - j + CHUNK]
            low_ref[:, cols] = out.astype(bf16)
            inner = inner + out * x_ref[:, cols]
            for j in range(4):
                gconv_ref[j : j + 1, cols] += jnp.sum(g * padded[5 + j : 5 + j + CHUNK], axis=0, keepdims=True)
            ghead[:, cols] = g[0:8]
    low_ref[:, 3 * hd :] = beta_low.astype(bf16)
    inner = inner + beta_low * x_ref[:, 3 * hd :]
    inner_ref[...] = jnp.sum(inner, axis=1, keepdims=True)
    ggain_ref[...] += ggain


def mixer_forward(proj, conv, gain, heads, dh):
    rows, width = proj.shape
    hd = heads * dh
    steps = rows // CHUNK
    square = pl.BlockSpec((1, heads, dh, dh), lambda i: (i, 0, 0, 0))
    wide = pl.BlockSpec((CHUNK, hd), lambda i: (i, 0))
    return pl.pallas_call(
        functools.partial(fwd_kernel, heads, dh),
        grid=(steps,),
        in_specs=[
            pl.BlockSpec((CHUNK, width), lambda i: (i, 0)),
            pl.BlockSpec((4, 3 * hd), lambda i: (0, 0)),
            pl.BlockSpec((1, dh), lambda i: (0, 0)),
        ],
        out_specs=[wide, wide, wide, pl.BlockSpec((1, heads, CHUNK, CHUNK), lambda i: (i, 0, 0, 0)), square],
        out_shape=[
            jax.ShapeDtypeStruct((rows, hd), bf16),
            jax.ShapeDtypeStruct((rows, hd), f32),
            jax.ShapeDtypeStruct((rows, hd), f32),
            jax.ShapeDtypeStruct((steps, heads, CHUNK, CHUNK), f32),
            jax.ShapeDtypeStruct((steps, heads, dh, dh), f32),
        ],
        scratch_shapes=[pltpu.VMEM((heads, dh, dh), f32), pltpu.VMEM((8, 3 * hd), f32)],
        compiler_params=pltpu.CompilerParams(vmem_limit_bytes=60 * 2**20),
        cost_estimate=FREE,
        name="mixer_forward",
    )(proj, conv, gain)


def mixer_backward(proj, conv, gain, mixed_cot, kept, heads, dh):
    o, fresh, inv, states = kept
    rows, width = proj.shape
    hd = heads * dh
    steps = rows // CHUNK
    last = steps - 1
    per = CHUNK // 8
    square = pl.BlockSpec((1, heads, dh, dh), lambda i: (last - i, 0, 0, 0))
    wide = pl.BlockSpec((CHUNK, hd), lambda i: (last - i, 0))
    return pl.pallas_call(
        functools.partial(bwd_kernel, heads, dh),
        grid=(steps,),
        in_specs=[
            pl.BlockSpec((CHUNK, width), lambda i: (last - i, 0)),
            pl.BlockSpec((8, width), lambda i: (jnp.maximum((last - i) * per - 1, 0), 0)),
            pl.BlockSpec((4, 3 * hd), lambda i: (0, 0)),
            pl.BlockSpec((1, dh), lambda i: (0, 0)),
            wide, wide, wide,
            pl.BlockSpec((1, heads, CHUNK, CHUNK), lambda i: (last - i, 0, 0, 0)),
            square,
        ],
        out_specs=[
            pl.BlockSpec((CHUNK, width), lambda i: (last - i, 0)),
            pl.BlockSpec((4, 3 * hd), lambda i: (0, 0)),
            pl.BlockSpec((1, dh), lambda i: (0, 0)),
            pl.BlockSpec((CHUNK, 1), lambda i: (last - i, 0)),
        ],
        out_shape=[
            jax.ShapeDtypeStruct((rows, width), bf16),
            jax.ShapeDtypeStruct((4, 3 * hd), f32),
            jax.ShapeDtypeStruct((1, dh), f32),
            jax.ShapeDtypeStruct((rows, 1), f32),
        ],
        scratch_shapes=[pltpu.VMEM((heads, dh, dh), f32), pltpu.VMEM((8, 3 * hd), f32)],
        compiler_params=pltpu.CompilerParams(vmem_limit_bytes=60 * 2**20),
        cost_estimate=FREE,
        name="mixer_backward",
    )(proj, proj, conv, gain, mixed_cot, o, fresh, inv, states)


def live_column(length, rows):
    return (lax.broadcasted_iota(jnp.int32, (rows, 1), 0) < length).astype(f32)


def swap(x, axis, bit):
    n = lax.axis_size(axis)
    return lax.ppermute(x, axis, [(i, i ^ bit) for i in range(n)])


def bits_down(n):
    bits = []
    while n > 1:
        n //= 2
        bits.append(n)
    return bits


def sum_all(x, axis):
    for bit in bits_down(lax.axis_size(axis)):
        x = x + swap(x, axis, bit)
    return x


def spread_cols(shard):
    n = lax.axis_size("col")
    pieces = {0: shard}
    for bit in bits_down(n):
        for j in list(pieces):
            pieces[j | bit] = swap(pieces[j], "col", bit)
    return [pieces[j] for j in range(n)]


class ColSum:
    def __init__(self, terms, block):
        self.terms, self.block = terms, block
        self.kept, self.got = list(range(lax.axis_size("col"))), {}

    def pieces(self, js, dtypes, earlier):
        (left, pair), rest = self.terms[0], self.terms[1:]
        gots = [self.got.pop(j, None) for j in js]
        return piece_call([(after(left, *earlier), pair)] + rest, self.block, js, gots, dtypes)

    def send(self, bit, *earlier):
        js = [j for j in self.kept if j & bit]
        last = bit > 1 and 2 * bit == lax.axis_size("col")
        sent = list(self.pieces(js + [0] * last, [bf16] * len(js) + [f32] * last, earlier))
        if last:
            self.base = sent.pop()
        for j, low in zip(js, sent):
            got, base = swap(low, "col", bit), j ^ bit
            self.got[base] = got if base not in self.got else self.got[base].astype(f32) + got.astype(f32)
        self.kept = [j for j in self.kept if not j & bit]
        return sent

    def send_last(self, *earlier):
        bit = 2
        while bit < lax.axis_size("col"):
            earlier = self.send(bit, *earlier)
            bit *= 2
        return earlier

    def total(self):
        return self.base + self.got[0].astype(f32)


def norm_kernel(width, me_ref, *refs):
    pieces, (gain_ref, normed_ref, factor_ref) = refs[:-3], refs[-3:]
    total = len(pieces) * width
    values = [p[...].astype(f32) for p in pieces]
    square = values[0] * values[0]
    for v in values[1:]:
        square = square + v * v
    factor = lax.rsqrt(jnp.sum(square, axis=1, keepdims=True) / total + EPS)
    factor_ref[...] = factor
    half = width // 2
    for j, v in enumerate(values):
        for p in range(2):
            start = p * (total // 2) + (me_ref[0] ^ j) * half
            cols = pl.ds(pl.multiple_of(start, half), half)
            normed_ref[:, cols] = (v[:, p * half : (p + 1) * half] * factor * gain_ref[:, cols]).astype(bf16)


def join_kernel(width, me_ref, *refs):
    pieces, out_ref = refs[:-1], refs[-1]
    half = width // 2
    for j, piece in enumerate(pieces):
        for p in range(2):
            start = p * len(pieces) * half + (me_ref[0] ^ j) * half
            out_ref[:, pl.ds(pl.multiple_of(start, half), half)] = piece[:, p * half : (p + 1) * half]


TILE = 256


def join_call(kernel, pieces, extra, outs, name):
    rows, width = pieces[0].shape
    me = lax.axis_index("col").astype(jnp.int32).reshape(1)
    return pl.pallas_call(
        functools.partial(kernel, width),
        grid_spec=pltpu.PrefetchScalarGridSpec(
            num_scalar_prefetch=1,
            grid=(rows // TILE,),
            in_specs=[pl.BlockSpec((TILE, width), lambda i, m: (i, 0))] * len(pieces)
            + [pl.BlockSpec(e.shape, lambda i, m: (0, 0)) for e in extra],
            out_specs=[pl.BlockSpec((TILE, o.shape[1]), lambda i, m: (i, 0)) for o in outs],
        ),
        out_shape=outs,
        compiler_params=pltpu.CompilerParams(vmem_limit_bytes=60 * 2**20),
        cost_estimate=FREE,
        name=name,
    )(me, *pieces, *extra)


def join_norm(pieces, gain):
    rows, width = pieces[0].shape
    outs = [jax.ShapeDtypeStruct((rows, width * len(pieces)), bf16), jax.ShapeDtypeStruct((rows, 1), f32)]
    return join_call(norm_kernel, pieces, [gain.reshape(1, -1)], outs, "join_norm")


def join(pieces):
    rows, width = pieces[0].shape
    return join_call(join_kernel, pieces, [], [jax.ShapeDtypeStruct((rows, width * len(pieces)), bf16)], "join")[0]


def dot(a, b, ca=1, cb=0):
    return lax.dot_general(a, b, (((ca,), (cb,)), ((), ())), preferred_element_type=f32)


FREE = pl.CostEstimate(flops=2**20, bytes_accessed=2**18, transcendentals=0)


def tile_call(kernel, arrays, specs, outs, out_specs, grid, name, me=None):
    params = dict(
        compiler_params=pltpu.CompilerParams(vmem_limit_bytes=48 * 2**20), cost_estimate=FREE, name=name
    )
    if me is None:
        return pl.pallas_call(kernel, grid=grid, in_specs=specs, out_specs=out_specs, out_shape=outs, **params)(*arrays)
    grid_spec = pltpu.PrefetchScalarGridSpec(
        num_scalar_prefetch=1, grid=grid, in_specs=specs, out_specs=out_specs
    )
    return pl.pallas_call(kernel, grid_spec=grid_spec, out_shape=outs, **params)(me, *arrays)


def row_tile(width):
    return pl.BlockSpec((TILE, width), lambda i, *_: (i, 0))


def half_tile(width, which):
    return pl.BlockSpec((TILE, width), lambda i, *_: (i, which))


def whole(shape):
    return pl.BlockSpec(shape, lambda i, *_: (0, 0))


def halves_kernel(count, *refs):
    out = refs[-1]
    total = dot(refs[0][...], refs[1][...])
    for i in range(1, count):
        total = total + dot(refs[2 * i][...], refs[2 * i + 1][...])
    out[...] = total.astype(out.dtype)


def halves(left, pairs, dtype=f32):
    rows, half, width = left.shape[0], left.shape[1] // 2, pairs[0][1].shape[1]
    arrays, specs = [], []
    for which, weight in pairs:
        arrays += [left, weight]
        specs += [half_tile(half, which), whole(weight.shape)]
    return tile_call(functools.partial(halves_kernel, len(pairs)), arrays, specs,
                     jax.ShapeDtypeStruct((rows, width), dtype), row_tile(width), (rows // TILE,), "halves")


def both(refs):
    return dot(refs[0][...], refs[2][...]) + dot(refs[1][...], refs[3][...])


def hidden_kernel(*refs):
    gate_ref, up_ref, hidden_ref = refs[4:]
    up = both(refs)
    gate = gate_ref[...].astype(f32)
    up_ref[...] = up.astype(bf16)
    hidden_ref[...] = (gate * sigmoid(gate) * up).astype(bf16)


def both_specs(left, pair):
    half = left.shape[1] // 2
    return [left, left, *pair], [half_tile(half, 0), half_tile(half, 1), whole(pair[0].shape), whole(pair[1].shape)]


def hidden_call(left, pair, gate):
    rows, width = gate.shape
    tile = row_tile(width)
    arrays, specs = both_specs(left, pair)
    outs = [jax.ShapeDtypeStruct((rows, width), bf16)] * 2
    return tile_call(hidden_kernel, arrays + [gate], specs + [tile], outs, [tile, tile], (rows // TILE,), "hidden")


def cots_kernel(*refs):
    gate_ref, up_ref, gate_cot_ref, up_cot_ref, inner_ref = refs[4:]
    cot = both(refs)
    gate, up = gate_ref[...].astype(f32), up_ref[...].astype(f32)
    sig = sigmoid(gate)
    silu = gate * sig
    gate_cot = cot * up * (sig + silu * (1.0 - sig))
    up_cot = cot * silu
    gate_cot_ref[...] = gate_cot.astype(bf16)
    up_cot_ref[...] = up_cot.astype(bf16)
    inner_ref[...] = jnp.sum(gate_cot * gate + up_cot * up, axis=1, keepdims=True)


def cots_call(left, pair, gate, up):
    rows, width = gate.shape
    tile = row_tile(width)
    arrays, specs = both_specs(left, pair)
    outs = [jax.ShapeDtypeStruct((rows, width), bf16)] * 2 + [jax.ShapeDtypeStruct((rows, 1), f32)]
    return tile_call(cots_kernel, arrays + [gate, up], specs + [tile, tile], outs, [tile, tile, row_tile(1)],
                     (rows // TILE,), "cots")


def piece_kernel(count, pieces, has_got, me_ref, *refs):
    outs = refs[-pieces:]
    stride = 1 + 2 * pieces
    for n, out in enumerate(outs):
        width = out.shape[1] // 2
        for p in range(2):
            total = None
            for i in range(count):
                term = dot(refs[stride * i][...], refs[stride * i + 1 + 2 * n + p][...], 1, 1)
                total = term if total is None else total + term
            if has_got:
                total = total + refs[stride * count + n][:, p * width : (p + 1) * width].astype(f32)
            out[:, p * width : (p + 1) * width] = total.astype(out.dtype)


def piece_call(terms, block, js, gots, dtypes):
    rows = terms[0][0].shape[0]
    me = jnp.stack([lax.axis_index("col") ^ j for j in js]).astype(jnp.int32)
    arrays, specs = [], []
    for left, pair in terms:
        arrays.append(left)
        specs.append(row_tile(left.shape[1]))
        for n in range(len(js)):
            arrays += pair
            specs += [pl.BlockSpec((block, w.shape[1]), lambda i, m, n=n: (m[n], 0)) for w in pair]
    has_got = gots[0] is not None
    if has_got:
        arrays += gots
        specs += [row_tile(2 * block)] * len(js)
    kernel = functools.partial(piece_kernel, len(terms), len(js), has_got)
    outs = [jax.ShapeDtypeStruct((rows, 2 * block), dtype) for dtype in dtypes]
    return tile_call(kernel, arrays, specs, outs, [row_tile(2 * block)] * len(js), (rows // TILE,), "piece", me)


def rows_kernel(left_ref, right_ref, *refs):
    total = dot(left_ref[...], right_ref[...], 0, 0)
    gots, out = refs[:-1], refs[-1]
    if len(gots) < 2:
        out[...] = (total + gots[0][...].astype(f32) if gots else total).astype(bf16)
        return
    for n, got in enumerate(gots):

        @pl.when(pl.program_id(0) == n)
        def _(got=got):
            out[...] = (total + got[...].astype(f32)).astype(bf16)


def rows_call(left, right, first, count, gots=()):
    rows, tile, width = left.shape[0], left.shape[1] // 4, right.shape[1]
    specs = [pl.BlockSpec((rows, tile), lambda i: (0, first + i)), whole(right.shape)]
    out = pl.BlockSpec((tile, width), lambda i: (i, 0))
    specs += [out] if len(gots) == 1 else [whole((tile, width))] * len(gots)
    return tile_call(rows_kernel, [left, right, *gots], specs, jax.ShapeDtypeStruct((count * tile, width), bf16), out,
                     (count,), "rows")


def parity_groups():
    n = lax.axis_size("row")
    return [list(range(p, n, 2)) for p in range(2)]


def after(x, *earlier):
    return lax.optimization_barrier((x,) + earlier)[0]


def gather_parity(shard):
    return lax.all_gather(shard, "row", axis=0, tiled=True, axis_index_groups=parity_groups())


def scatter_parity(part):
    return lax.psum_scatter(part, "row", scatter_dimension=0, tiled=True, axis_index_groups=parity_groups())


def trade_rows(left, right, parts=1):
    count = 2 // parts
    sent = [rows_call(left, right, 2 + part * count, count) for part in range(parts)]
    return sent, [swap(part, "row", 1) for part in sent]


def own_rows(left, right, gots, *earlier):
    first = after(gots[0], *gots[1:], *earlier)
    return rows_call(left, right, 0, 2, [first, *gots[1:]])


def flip(first, second):
    odd = (lax.axis_index("row") & 1) == 1
    return jnp.where(odd, second, first), jnp.where(odd, first, second)


def by_parity(x, chunk):
    lead, width = x.shape
    parts = x.reshape(lead, width // (2 * chunk), 2, chunk)
    first, second = flip(parts[:, :, 0], parts[:, :, 1])
    return jnp.concatenate([first.reshape(lead, width // 2), second.reshape(lead, width // 2)], 1)


def by_place(x, chunk):
    lead, width = x.shape
    shape = (lead, width // (2 * chunk), chunk)
    first, second = flip(x[:, : width // 2].reshape(shape), x[:, width // 2 :].reshape(shape))
    return jnp.stack([first, second], 2).reshape(lead, width)


def per_device(tokens, lengths, norm_in, q_weight, k_weight, v_weight, conv_q, conv_k, conv_v, beta_weight,
               head_gain, out_weight, norm_mid, gate_weight, up_weight, down_weight, cotangent):
    rows, width = tokens.shape
    dh = head_gain.shape[0]
    hd = q_weight.shape[1]
    heads = hd // dh
    ff = gate_weight.shape[1]
    col = lax.axis_index("col")
    feat = lax.axis_size("col") * width
    live = live_column(lengths[0], rows)
    live_low = live.astype(bf16)
    beta_pad = jnp.pad(beta_weight, ((0, 0), (0, 128 - beta_weight.shape[1])))
    in_mine = gather_parity(jnp.concatenate([q_weight, k_weight, v_weight, beta_pad], 1))
    out_mine = gather_parity(out_weight.T)
    gate_mine = gather_parity(gate_weight)
    up_mine = gather_parity(up_weight)
    down_turned = down_weight.T
    down_side = swap(down_turned, "row", 1)
    down_mine = gather_parity(down_turned)
    down_other = gather_parity(down_side)
    conv = jnp.concatenate([conv_q, conv_k, conv_v], 1)
    gain = head_gain.reshape(1, dh)
    gain_in = lax.dynamic_slice_in_dim(norm_in, col * width, width)
    gain_mid = lax.dynamic_slice_in_dim(norm_mid, col * width, width)
    chunk = q_weight.shape[0]
    tokens, cotangent = by_parity(tokens, chunk), by_parity(cotangent, chunk)
    gain_in, gain_mid = by_parity(gain_in[None], chunk), by_parity(gain_mid[None], chunk)
    norm_in, norm_mid = by_parity(norm_in[None], chunk), by_parity(norm_mid[None], chunk)
    tokens32 = tokens.astype(f32)

    block = width // 2

    half = feat // 2
    normed, factor_in = join_norm(spread_cols(tokens), norm_in)
    ffn_cot = join(spread_cols(after(cotangent * live_low, down_side)))
    in_mine = after(in_mine, normed, ffn_cot)
    in_other, out_other = swap(in_mine, "row", 1), swap(out_mine, "row", 1)
    proj = halves(after(normed, out_mine), [(0, in_mine), (1, in_other)])
    gate_mine = after(gate_mine, proj)
    gate_other = swap(gate_mine, "row", 1)
    proj = after(proj, gate_mine)
    out_other = after(out_other, proj)
    w_in, w_out = (in_mine, in_other), (out_mine, out_other)
    mixed, *kept = mixer_forward(proj, conv, gain, heads, dh)
    branch = ColSum([(mixed, w_out)], block)
    sent = branch.send(1)
    sent = branch.send_last(*sent)
    up_mine = after(up_mine, *sent)
    up_other = swap(up_mine, "row", 1)
    middle = tokens32 + live * after(branch.total(), gate_other)
    mid_low = middle.astype(bf16)
    normed_mid, factor_mid = join_norm(spread_cols(mid_low), after(norm_mid, up_mine))
    w_gate, w_up = (gate_mine, gate_other), (up_mine, up_other)
    gate = halves(normed_mid, [(0, gate_mine), (1, gate_other)], bf16)
    up, hidden = hidden_call(after(normed_mid, gate), w_up, gate)
    down_sent, down_got = trade_rows(ffn_cot, hidden)
    down_sent = down_sent[0]
    w_down = after(down_mine, down_sent), after(down_other, down_sent)
    gate_cot, up_cot, inner_mid = cots_call(ffn_cot, w_down, gate, up)
    inner_mid = sum_all(inner_mid.reshape(rows // 128, 128), "col").reshape(rows, 1) / factor_mid
    mid_sum = ColSum([(gate_cot, w_gate), (up_cot, w_up)], block)
    sent = mid_sum.send(1)
    gate_sent, gate_got = trade_rows(after(normed_mid, *sent), gate_cot, 2)
    mid_sum.send_last(inner_mid, gate_sent[0])
    up_sent, up_got = trade_rows(after(normed_mid, gate_got[0]), up_cot)
    mid_sum.got[0] = after(mid_sum.got[0], *up_sent)
    down_rows = own_rows(ffn_cot, hidden, down_got, mid_sum.got[0])
    grad_down = scatter_parity(down_rows)
    mid_cot = mid_sum.total()

    mid32 = mid_low.astype(f32)
    gmid_part = jnp.sum(mid_cot * mid32 * factor_mid, axis=0)
    middle_cot = cotangent.astype(f32) + factor_mid * gain_mid * mid_cot - mid32 * (factor_mid**3 * inner_mid / feat)
    branch_low = (live * middle_cot).astype(bf16)
    pieces = spread_cols(branch_low)
    gate_rows = own_rows(normed_mid, gate_cot, gate_got, pieces[2])
    grad_gate = scatter_parity(gate_rows)
    branch_cot = join(pieces)
    mixed_cot = halves(branch_cot, [(0, out_mine), (1, out_other)])
    out_sent, out_got = trade_rows(after(branch_cot, mixed_cot), mixed)
    mixed_cot = after(mixed_cot, *out_sent)
    low, gconv, ghead, inner_in = mixer_backward(proj, conv, gain, mixed_cot, kept, heads, dh)
    low_sent, low_got = trade_rows(normed, low, 2)
    inner_in = sum_all(inner_in.reshape(rows // 128, 128), "col").reshape(rows, 1) / factor_in
    in_sum = ColSum([(low, w_in)], block)
    sent = in_sum.send(1, *low_sent)
    in_sum.send_last(inner_in, *sent)
    up_rows = own_rows(normed_mid, up_cot, up_got, *out_got, in_sum.base, grad_down)
    grad_up = scatter_parity(up_rows)
    out_rows = own_rows(branch_cot, mixed, out_got, grad_gate, up_rows, low_got[0], in_sum.got[0])
    grad_out = scatter_parity(out_rows)
    in_cot = in_sum.total()
    gin_part = jnp.sum(in_cot * tokens32 * factor_in, axis=0)
    grad_tokens = middle_cot + factor_in * gain_in * in_cot - tokens32 * (factor_in**3 * inner_in / feat)

    def own_cols(part):
        part = by_place(part[None], chunk)[0]
        return lax.dynamic_update_slice_in_dim(jnp.zeros((feat,), f32), part, col * width, 0)

    sizes = [feat, feat, dh]
    wide = sum_all(jnp.concatenate([own_cols(gin_part), own_cols(gmid_part), ghead[0]]).reshape(-1, 128), "col")
    small = jnp.concatenate([wide, gconv.reshape(-1, 128)], 0)
    bits = bits_down(lax.axis_size("row"))
    for bit in bits[:-1]:
        small = small + swap(small, "row", bit)
    low_rows = own_rows(normed, low, low_got, out_rows, grad_up, small, grad_tokens)
    grad_low = scatter_parity(low_rows)
    in_cot = in_sum.total()
    gin_part = jnp.sum(in_cot * tokens32 * factor_in, axis=0)
    grad_tokens = middle_cot + factor_in * gain_in * in_cot - tokens32 * (factor_in**3 * inner_in / feat)

    def own_cols(part):
        part = by_place(part[None], chunk)[0]
        return lax.dynamic_update_slice_in_dim(jnp.zeros((feat,), f32), part, col * width, 0)

    sizes = [feat, feat, dh]
    wide = sum_all(jnp.concatenate([own_cols(gin_part), own_cols(gmid_part), ghead[0]]).reshape(-1, 128), "col")
    small = jnp.concatenate([wide, gconv.reshape(-1, 128)], 0)
    bits = bits_down(lax.axis_size("row"))
    for bit in bits[:-1]:
        small = small + swap(small, "row", bit)
    low_rows = own_rows(normed, low, low_got, out_rows, grad_up, small, grad_tokens)
    grad_low = scatter_parity(low_rows)
    result = ColSum([(hidden, w_down)], block)
    sent = result.send(1, low_rows)
    result.send_last(*sent)
    layer_out = (middle + live * result.total()).astype(bf16)
    small = small + swap(small, "row", bits[-1])
    wide, gconv = small[: wide.shape[0]].reshape(-1), small[wide.shape[0] :].reshape(gconv.shape)
    g_low = grad_low.astype(f32)
    return (
        by_place(layer_out, chunk),
        by_place(grad_tokens, chunk),
        wide[:feat],
        g_low[:, :hd],
        g_low[:, hd : 2 * hd],
        g_low[:, 2 * hd : 3 * hd],
        gconv[:, :hd],
        gconv[:, hd : 2 * hd],
        gconv[:, 2 * hd :],
        g_low[:, 3 * hd : 3 * hd + beta_weight.shape[1]],
        wide[2 * feat :],
        grad_out.astype(f32).T,
        wide[feat : 2 * feat],
        grad_gate.astype(f32),
        grad_up.astype(f32),
        grad_down.astype(f32).T,
    )


def solution(mesh):
    split_both, features, turned = P("row", "col"), P(None, "col"), P("col", "row")
    return jax.shard_map(
        per_device,
        mesh=mesh,
        in_specs=(split_both, P("row"), P(), split_both, split_both, split_both, features, features, features,
                  split_both, P(), turned, P(), split_both, split_both, turned, split_both),
        out_specs=(split_both, split_both, P(), split_both, split_both, split_both, features, features, features,
                   split_both, P(), turned, P(), split_both, split_both, turned),
        check_vma=False,
    )
```

```python
import functools
import jax
import jax.numpy as jnp
from jax import lax
from jax.experimental import pallas as pl
from jax.experimental.pallas import tpu as pltpu
from jax.sharding import PartitionSpec as P

CHUNK = 128
EPS = 1e-6
FREE = pl.CostEstimate(flops=2**20, bytes_accessed=2**18, transcendentals=0)
bf16 = jnp.bfloat16
f32 = jnp.float32


def split(x):
    high = x.astype(bf16)
    return high, (x - high.astype(f32)).astype(bf16)


def mm(a, b, ca=1, cb=0):
    def dg(u, v):
        return lax.dot_general(u, v, (((ca,), (cb,)), ((), ())), preferred_element_type=f32)

    return dg(a[0], b[0]) + (dg(a[0], b[1]) + dg(a[1], b[0]))


def sigmoid(x):
    return 0.5 * jnp.tanh(0.5 * x) + 0.5


def masks(n):
    r = lax.broadcasted_iota(jnp.int32, (n, n), 0)
    c = lax.broadcasted_iota(jnp.int32, (n, n), 1)
    return r, c


def unit_lower_inverse(lows, r, c):
    n = lows[0].shape[0]
    eye = jnp.where(r == c, 1.0, 0.0)
    invs = [eye - jnp.where(r // 2 == c // 2, low, 0.0) for low in lows]
    size = 2
    while size < n:
        mask = (r // (2 * size) == c // (2 * size)) & (r // size != c // size)
        offs = [split(jnp.where(mask, low, 0.0)) for low in lows]
        parts = [split(inv) for inv in invs]
        right = [split(mm(off, part)) for off, part in zip(offs, parts)]
        invs = [inv - mm(part, x) for inv, part, x in zip(invs, parts, right)]
        size *= 2
    return invs


def conv_rows(padded, taps, first):
    out = taps[0:1] * padded[first : first + CHUNK]
    for j in range(1, 4):
        out = out + taps[j : j + 1] * padded[first + j : first + j + CHUNK]
    return out


def fwd_kernel(heads, dh, x_ref, conv_ref, gain_ref, mixed_ref, o_ref, n_ref, t_ref, s_ref, state, halo):
    hd = heads * dh

    @pl.when(pl.program_id(0) == 0)
    def _():
        state[...] = jnp.zeros_like(state)
        halo[...] = jnp.zeros_like(halo)

    r, c = masks(CHUNK)
    each = range(heads)
    acts = []
    for p in range(3):
        for h in each:
            cols = slice(p * hd + h * dh, p * hd + (h + 1) * dh)
            y = conv_rows(jnp.concatenate([halo[:, cols], x_ref[:, cols]], 0), conv_ref[:, cols], 5)
            acts.append(y * sigmoid(y))
    qs = [split(acts[h] * dh ** -0.5) for h in each]
    ks = []
    for h in each:
        k = acts[heads + h]
        ks.append(split(k * lax.rsqrt(jnp.sum(k * k, axis=1, keepdims=True) + EPS)))
    b = [sigmoid(x_ref[:, 3 * hd + h : 3 * hd + h + 1]) for h in each]
    lows = [jnp.where(r > c, b[h] * mm(ks[h], ks[h], 1, 1), 0.0) for h in each]
    invs = unit_lower_inverse(lows, r, c)
    scores = [split(jnp.where(r >= c, mm(qs[h], ks[h], 1, 1), 0.0)) for h in each]
    s = [state[h] for h in each]
    ss = [split(s[h]) for h in each]
    right = [split(b[h] * (acts[2 * heads + h] - mm(ks[h], ss[h]))) for h in each]
    fresh = [mm(split(invs[h]), right[h]) for h in each]
    fs = [split(fresh[h]) for h in each]
    outs = [mm(qs[h], ss[h]) + mm(scores[h], fs[h]) for h in each]
    for h in each:
        state[h] = s[h] + mm(ks[h], fs[h], 0, 0)
        cols = slice(h * dh, (h + 1) * dh)
        s_ref[0, h] = s[h]
        t_ref[0, h] = invs[h]
        n_ref[:, cols] = fresh[h]
        o = outs[h]
        o_ref[:, cols] = o
        norm = lax.rsqrt(jnp.mean(o * o, axis=1, keepdims=True) + EPS)
        mixed_ref[:, cols] = (o * norm * gain_ref[...]).astype(bf16)
    halo[...] = x_ref[CHUNK - 8 :, : 3 * hd]


def bwd_kernel(heads, dh, x_ref, prev_ref, conv_ref, gain_ref, m_ref, o_ref, n_ref, t_ref, s_ref,
               low_ref, gconv_ref, ggain_ref, inner_ref, dstate, ghead):
    hd = heads * dh
    step = pl.program_id(0)

    @pl.when(step == 0)
    def _():
        dstate[...] = jnp.zeros_like(dstate)
        ghead[...] = jnp.zeros_like(ghead)
        gconv_ref[...] = jnp.zeros_like(gconv_ref)
        ggain_ref[...] = jnp.zeros_like(ggain_ref)

    has_prev = jnp.where(step == pl.num_programs(0) - 1, 0.0, 1.0)
    r, c = masks(CHUNK)
    lane = lax.broadcasted_iota(jnp.int32, (CHUNK, 128), 1)
    each = range(heads)
    scale = dh ** -0.5
    cuts = [slice(h * dh, (h + 1) * dh) for h in each]
    ys, sigs = [], []
    for p in range(3):
        for h in each:
            cols = slice(p * hd + h * dh, p * hd + (h + 1) * dh)
            padded = jnp.concatenate([prev_ref[:, cols] * has_prev, x_ref[:, cols]], 0)
            y = conv_rows(padded, conv_ref[:, cols], 5)
            ys.append(y)
            sigs.append(sigmoid(y))
    qs = [split(ys[h] * sigs[h] * scale) for h in each]
    kr = [ys[heads + h] * sigs[heads + h] for h in each]
    kinv = [lax.rsqrt(jnp.sum(kr[h] * kr[h], axis=1, keepdims=True) + EPS) for h in each]
    ks = [split(kr[h] * kinv[h]) for h in each]
    b = [sigmoid(x_ref[:, 3 * hd + h : 3 * hd + h + 1]) for h in each]
    dos = []
    ggain = jnp.zeros((1, dh), f32)
    for h in each:
        o = o_ref[:, cuts[h]]
        mc = m_ref[:, cuts[h]]
        norm = lax.rsqrt(jnp.mean(o * o, axis=1, keepdims=True) + EPS)
        ggain = ggain + jnp.sum(mc * (o * norm), axis=0, keepdims=True)
        dn_ = mc * gain_ref[...]
        do = norm * dn_ - o * (norm * norm * norm * jnp.mean(dn_ * o, axis=1, keepdims=True))
        dos.append(split(do))
    scores = [split(jnp.where(r >= c, mm(qs[h], ks[h], 1, 1), 0.0)) for h in each]
    part = [mm(scores[h], dos[h], 0, 0) for h in each]
    d = [dstate[h] for h in each]
    ds = [split(d[h]) for h in each]
    dfresh = [split(part[h] + mm(ks[h], ds[h])) for h in each]
    db_ = [mm(split(t_ref[0, h]), dfresh[h], 0, 0) for h in each]
    dr = [b[h] * db_[h] for h in each]
    drs = [split(dr[h]) for h in each]
    for h in each:
        dstate[h] = d[h] + (mm(qs[h], dos[h], 0, 0) - mm(ks[h], drs[h], 0, 0))
    ss = [split(s_ref[0, h]) for h in each]
    fs = [split(n_ref[:, cuts[h]]) for h in each]
    resid = [ys[2 * heads + h] * sigs[2 * heads + h] - mm(ks[h], ss[h]) for h in each]
    gram = [mm(ks[h], ks[h], 1, 1) for h in each]
    da = [jnp.where(r > c, -mm(split(db_[h]), fs[h], 1, 1), 0.0) for h in each]
    dsc = [split(jnp.where(r >= c, mm(dos[h], fs[h], 1, 1), 0.0)) for h in each]
    dq = [mm(dos[h], ss[h], 1, 1) + mm(dsc[h], ks[h]) for h in each]
    dgs = [split(b[h] * da[h]) for h in each]
    dk = [mm(dsc[h], qs[h], 0, 0) + mm(fs[h], ds[h], 1, 1) for h in each]
    dk = [dk[h] - mm(drs[h], ss[h], 1, 1) for h in each]
    dk = [dk[h] + (mm(dgs[h], ks[h]) + mm(dgs[h], ks[h], 0, 0)) for h in each]
    beta_low = jnp.zeros((CHUNK, 128), f32)
    inner = jnp.zeros((CHUNK, dh), f32)
    for h in each:
        dbeta = jnp.sum(db_[h] * resid[h], axis=1, keepdims=True) + jnp.sum(da[h] * gram[h], axis=1, keepdims=True)
        beta_low = jnp.where(lane == h, dbeta * b[h] * (1.0 - b[h]), beta_low)
    dkr = [kinv[h] * dk[h] - kr[h] * (kinv[h] * kinv[h] * kinv[h] * jnp.sum(dk[h] * kr[h], axis=1, keepdims=True)) for h in each]
    cots = [dq[h] * scale for h in each] + dkr + dr
    for p in range(3):
        for h in each:
            i = p * heads + h
            cols = slice(p * hd + h * dh, p * hd + (h + 1) * dh)
            g = cots[i] * sigs[i] * (1.0 + ys[i] * (1.0 - sigs[i]))
            taps = conv_ref[:, cols]
            gp = jnp.concatenate([g, ghead[:, cols]], 0)
            padded = jnp.concatenate([prev_ref[:, cols] * has_prev, x_ref[:, cols]], 0)
            out = taps[3:4] * g
            for j in range(3):
                out = out + taps[j : j + 1] * gp[3 - j : 3 - j + CHUNK]
            low_ref[:, cols] = out.astype(bf16)
            inner = inner + out * x_ref[:, cols]
            for j in range(4):
                gconv_ref[j : j + 1, cols] += jnp.sum(g * padded[5 + j : 5 + j + CHUNK], axis=0, keepdims=True)
            ghead[:, cols] = g[0:8]
    low_ref[:, 3 * hd :] = beta_low.astype(bf16)
    inner = inner + beta_low * x_ref[:, 3 * hd :]
    inner_ref[...] = jnp.sum(inner, axis=1, keepdims=True)
    ggain_ref[...] += ggain


def mixer_forward(proj, conv, gain, heads, dh):
    rows, width = proj.shape
    hd = heads * dh
    steps = rows // CHUNK
    square = pl.BlockSpec((1, heads, dh, dh), lambda i: (i, 0, 0, 0))
    wide = pl.BlockSpec((CHUNK, hd), lambda i: (i, 0))
    return pl.pallas_call(
        functools.partial(fwd_kernel, heads, dh),
        grid=(steps,),
        in_specs=[
            pl.BlockSpec((CHUNK, width), lambda i: (i, 0)),
            pl.BlockSpec((4, 3 * hd), lambda i: (0, 0)),
            pl.BlockSpec((1, dh), lambda i: (0, 0)),
        ],
        out_specs=[wide, wide, wide, pl.BlockSpec((1, heads, CHUNK, CHUNK), lambda i: (i, 0, 0, 0)), square],
        out_shape=[
            jax.ShapeDtypeStruct((rows, hd), bf16),
            jax.ShapeDtypeStruct((rows, hd), f32),
            jax.ShapeDtypeStruct((rows, hd), f32),
            jax.ShapeDtypeStruct((steps, heads, CHUNK, CHUNK), f32),
            jax.ShapeDtypeStruct((steps, heads, dh, dh), f32),
        ],
        scratch_shapes=[pltpu.VMEM((heads, dh, dh), f32), pltpu.VMEM((8, 3 * hd), f32)],
        compiler_params=pltpu.CompilerParams(vmem_limit_bytes=60 * 2**20),
        cost_estimate=FREE,
        name="mixer_forward",
    )(proj, conv, gain)


def mixer_backward(proj, conv, gain, mixed_cot, kept, heads, dh):
    o, fresh, inv, states = kept
    rows, width = proj.shape
    hd = heads * dh
    steps = rows // CHUNK
    last = steps - 1
    per = CHUNK // 8
    square = pl.BlockSpec((1, heads, dh, dh), lambda i: (last - i, 0, 0, 0))
    wide = pl.BlockSpec((CHUNK, hd), lambda i: (last - i, 0))
    return pl.pallas_call(
        functools.partial(bwd_kernel, heads, dh),
        grid=(steps,),
        in_specs=[
            pl.BlockSpec((CHUNK, width), lambda i: (last - i, 0)),
            pl.BlockSpec((8, width), lambda i: (jnp.maximum((last - i) * per - 1, 0), 0)),
            pl.BlockSpec((4, 3 * hd), lambda i: (0, 0)),
            pl.BlockSpec((1, dh), lambda i: (0, 0)),
            wide, wide, wide,
            pl.BlockSpec((1, heads, CHUNK, CHUNK), lambda i: (last - i, 0, 0, 0)),
            square,
        ],
        out_specs=[
            pl.BlockSpec((CHUNK, width), lambda i: (last - i, 0)),
            pl.BlockSpec((4, 3 * hd), lambda i: (0, 0)),
            pl.BlockSpec((1, dh), lambda i: (0, 0)),
            pl.BlockSpec((CHUNK, 1), lambda i: (last - i, 0)),
        ],
        out_shape=[
            jax.ShapeDtypeStruct((rows, width), bf16),
            jax.ShapeDtypeStruct((4, 3 * hd), f32),
            jax.ShapeDtypeStruct((1, dh), f32),
            jax.ShapeDtypeStruct((rows, 1), f32),
        ],
        scratch_shapes=[pltpu.VMEM((heads, dh, dh), f32), pltpu.VMEM((8, 3 * hd), f32)],
        compiler_params=pltpu.CompilerParams(vmem_limit_bytes=60 * 2**20),
        cost_estimate=FREE,
        name="mixer_backward",
    )(proj, proj, conv, gain, mixed_cot, o, fresh, inv, states)


def live_column(length, rows):
    return (lax.broadcasted_iota(jnp.int32, (rows, 1), 0) < length).astype(f32)


def swap(x, axis, bit):
    n = lax.axis_size(axis)
    return lax.ppermute(x, axis, [(i, i ^ bit) for i in range(n)])


def bits_down(n):
    bits = []
    while n > 1:
        n //= 2
        bits.append(n)
    return bits


def sum_all(x, axis):
    for bit in bits_down(lax.axis_size(axis)):
        x = x + swap(x, axis, bit)
    return x


def spread_cols(shard):
    n = lax.axis_size("col")
    pieces = {0: shard}
    for bit in bits_down(n):
        for j in list(pieces):
            pieces[j | bit] = swap(pieces[j], "col", bit)
    return [pieces[j] for j in range(n)]


class ColSum:
    def __init__(self, terms, block):
        self.terms, self.block = terms, block
        self.kept, self.got = list(range(lax.axis_size("col"))), {}

    def pieces(self, js, dtypes, earlier):
        (left, pair), rest = self.terms[0], self.terms[1:]
        gots = [self.got.pop(j, None) for j in js]
        return piece_call([(after(left, *earlier), pair)] + rest, self.block, js, gots, dtypes)

    def send(self, bit, *earlier):
        js = [j for j in self.kept if j & bit]
        last = bit > 1 and 2 * bit == lax.axis_size("col")
        sent = list(self.pieces(js + [0] * last, [bf16] * len(js) + [f32] * last, earlier))
        if last:
            self.base = sent.pop()
        for j, low in zip(js, sent):
            got, base = swap(low, "col", bit), j ^ bit
            self.got[base] = got if base not in self.got else self.got[base].astype(f32) + got.astype(f32)
        self.kept = [j for j in self.kept if not j & bit]
        return sent

    def send_last(self, *earlier):
        bit = 2
        while bit < lax.axis_size("col"):
            earlier = self.send(bit, *earlier)
            bit *= 2
        return earlier

    def total(self):
        return self.base + self.got[0].astype(f32)


def norm_kernel(width, me_ref, *refs):
    pieces, (gain_ref, normed_ref, factor_ref) = refs[:-3], refs[-3:]
    total = len(pieces) * width
    values = [p[...].astype(f32) for p in pieces]
    square = values[0] * values[0]
    for v in values[1:]:
        square = square + v * v
    factor = lax.rsqrt(jnp.sum(square, axis=1, keepdims=True) / total + EPS)
    factor_ref[...] = factor
    half = width // 2
    for j, v in enumerate(values):
        for p in range(2):
            start = p * (total // 2) + (me_ref[0] ^ j) * half
            cols = pl.ds(pl.multiple_of(start, half), half)
            normed_ref[:, cols] = (v[:, p * half : (p + 1) * half] * factor * gain_ref[:, cols]).astype(bf16)


def join_kernel(width, me_ref, *refs):
    pieces, out_ref = refs[:-1], refs[-1]
    half = width // 2
    for j, piece in enumerate(pieces):
        for p in range(2):
            start = p * len(pieces) * half + (me_ref[0] ^ j) * half
            out_ref[:, pl.ds(pl.multiple_of(start, half), half)] = piece[:, p * half : (p + 1) * half]


TILE = 512


def join_call(kernel, pieces, extra, outs, name):
    rows, width = pieces[0].shape
    me = lax.axis_index("col").astype(jnp.int32).reshape(1)
    return pl.pallas_call(
        functools.partial(kernel, width),
        grid_spec=pltpu.PrefetchScalarGridSpec(
            num_scalar_prefetch=1,
            grid=(rows // TILE,),
            in_specs=[pl.BlockSpec((TILE, width), lambda i, m: (i, 0))] * len(pieces)
            + [pl.BlockSpec(e.shape, lambda i, m: (0, 0)) for e in extra],
            out_specs=[pl.BlockSpec((TILE, o.shape[1]), lambda i, m: (i, 0)) for o in outs],
        ),
        out_shape=outs,
        compiler_params=pltpu.CompilerParams(vmem_limit_bytes=60 * 2**20),
        cost_estimate=FREE,
        name=name,
    )(me, *pieces, *extra)


def join_norm(pieces, gain):
    rows, width = pieces[0].shape
    outs = [jax.ShapeDtypeStruct((rows, width * len(pieces)), bf16), jax.ShapeDtypeStruct((rows, 1), f32)]
    return join_call(norm_kernel, pieces, [gain.reshape(1, -1)], outs, "join_norm")


def join(pieces):
    rows, width = pieces[0].shape
    return join_call(join_kernel, pieces, [], [jax.ShapeDtypeStruct((rows, width * len(pieces)), bf16)], "join")[0]


def dot(a, b, ca=1, cb=0):
    return lax.dot_general(a, b, (((ca,), (cb,)), ((), ())), preferred_element_type=f32)


FREE = pl.CostEstimate(flops=2**20, bytes_accessed=2**18, transcendentals=0)


def tile_call(kernel, arrays, specs, outs, out_specs, grid, name, me=None):
    params = dict(
        compiler_params=pltpu.CompilerParams(vmem_limit_bytes=48 * 2**20), cost_estimate=FREE, name=name
    )
    if me is None:
        return pl.pallas_call(kernel, grid=grid, in_specs=specs, out_specs=out_specs, out_shape=outs, **params)(*arrays)
    grid_spec = pltpu.PrefetchScalarGridSpec(
        num_scalar_prefetch=1, grid=grid, in_specs=specs, out_specs=out_specs
    )
    return pl.pallas_call(kernel, grid_spec=grid_spec, out_shape=outs, **params)(me, *arrays)


def row_tile(width):
    return pl.BlockSpec((TILE, width), lambda i, *_: (i, 0))


def half_tile(width, which):
    return pl.BlockSpec((TILE, width), lambda i, *_: (i, which))


def whole(shape):
    return pl.BlockSpec(shape, lambda i, *_: (0, 0))


def halves_kernel(count, *refs):
    out = refs[-1]
    total = dot(refs[0][...], refs[1][...])
    for i in range(1, count):
        total = total + dot(refs[2 * i][...], refs[2 * i + 1][...])
    out[...] = total.astype(out.dtype)


def halves(left, pairs, dtype=f32):
    rows, half, width = left.shape[0], left.shape[1] // 2, pairs[0][1].shape[1]
    arrays, specs = [], []
    for which, weight in pairs:
        arrays += [left, weight]
        specs += [half_tile(half, which), whole(weight.shape)]
    return tile_call(functools.partial(halves_kernel, len(pairs)), arrays, specs,
                     jax.ShapeDtypeStruct((rows, width), dtype), row_tile(width), (rows // TILE,), "halves")


def both(refs):
    return dot(refs[0][...], refs[2][...]) + dot(refs[1][...], refs[3][...])


def hidden_kernel(*refs):
    gate_ref, up_ref, hidden_ref = refs[4:]
    up = both(refs)
    gate = gate_ref[...].astype(f32)
    up_ref[...] = up.astype(bf16)
    hidden_ref[...] = (gate * sigmoid(gate) * up).astype(bf16)


def both_specs(left, pair):
    half = left.shape[1] // 2
    return [left, left, *pair], [half_tile(half, 0), half_tile(half, 1), whole(pair[0].shape), whole(pair[1].shape)]


def hidden_call(left, pair, gate):
    rows, width = gate.shape
    tile = row_tile(width)
    arrays, specs = both_specs(left, pair)
    outs = [jax.ShapeDtypeStruct((rows, width), bf16)] * 2
    return tile_call(hidden_kernel, arrays + [gate], specs + [tile], outs, [tile, tile], (rows // TILE,), "hidden")


def cots_kernel(*refs):
    gate_ref, up_ref, gate_cot_ref, up_cot_ref, inner_ref = refs[4:]
    cot = both(refs)
    gate, up = gate_ref[...].astype(f32), up_ref[...].astype(f32)
    sig = sigmoid(gate)
    silu = gate * sig
    gate_cot = cot * up * (sig + silu * (1.0 - sig))
    up_cot = cot * silu
    gate_cot_ref[...] = gate_cot.astype(bf16)
    up_cot_ref[...] = up_cot.astype(bf16)
    inner_ref[...] = jnp.sum(gate_cot * gate + up_cot * up, axis=1, keepdims=True)


def cots_call(left, pair, gate, up):
    rows, width = gate.shape
    tile = row_tile(width)
    arrays, specs = both_specs(left, pair)
    outs = [jax.ShapeDtypeStruct((rows, width), bf16)] * 2 + [jax.ShapeDtypeStruct((rows, 1), f32)]
    return tile_call(cots_kernel, arrays + [gate, up], specs + [tile, tile], outs, [tile, tile, row_tile(1)],
                     (rows // TILE,), "cots")


def piece_kernel(count, pieces, has_got, me_ref, *refs):
    outs = refs[-pieces:]
    stride = 1 + 2 * pieces
    for n, out in enumerate(outs):
        width = out.shape[1] // 2
        for p in range(2):
            total = None
            for i in range(count):
                term = dot(refs[stride * i][...], refs[stride * i + 1 + 2 * n + p][...], 1, 1)
                total = term if total is None else total + term
            if has_got:
                total = total + refs[stride * count + n][:, p * width : (p + 1) * width].astype(f32)
            out[:, p * width : (p + 1) * width] = total.astype(out.dtype)


def piece_call(terms, block, js, gots, dtypes):
    rows = terms[0][0].shape[0]
    me = jnp.stack([lax.axis_index("col") ^ j for j in js]).astype(jnp.int32)
    arrays, specs = [], []
    for left, pair in terms:
        arrays.append(left)
        specs.append(row_tile(left.shape[1]))
        for n in range(len(js)):
            arrays += pair
            specs += [pl.BlockSpec((block, w.shape[1]), lambda i, m, n=n: (m[n], 0)) for w in pair]
    has_got = gots[0] is not None
    if has_got:
        arrays += gots
        specs += [row_tile(2 * block)] * len(js)
    kernel = functools.partial(piece_kernel, len(terms), len(js), has_got)
    outs = [jax.ShapeDtypeStruct((rows, 2 * block), dtype) for dtype in dtypes]
    return tile_call(kernel, arrays, specs, outs, [row_tile(2 * block)] * len(js), (rows // TILE,), "piece", me)


def rows_kernel(parts, left_ref, right_ref, *refs):
    total = dot(left_ref[...], right_ref[...], 0, 0)
    gots, out = refs[:-1], refs[-1]
    if not gots:
        out[...] = total.astype(bf16)
    start = 0
    for got, part in zip(gots, parts):

        @pl.when((pl.program_id(0) >= start) & (pl.program_id(0) < start + part))
        def _(got=got):
            out[...] = (total + got[...].astype(f32)).astype(bf16)

        start += part


def rows_call(left, right, first, parts, tile, gots=()):
    rows, width, count = left.shape[0], right.shape[1], sum(parts)
    specs = [pl.BlockSpec((rows, tile), lambda i: (0, first + i)), whole(right.shape)]
    start = 0
    for _, part in zip(gots, parts):
        specs.append(pl.BlockSpec((tile, width), lambda i, s=start, p=part: (jnp.clip(i - s, 0, p - 1), 0)))
        start += part
    out = pl.BlockSpec((tile, width), lambda i: (i, 0))
    return tile_call(functools.partial(rows_kernel, parts), [left, right, *gots], specs,
                     jax.ShapeDtypeStruct((count * tile, width), bf16), out, (count,), "rows")


def parity_groups():
    n = lax.axis_size("row")
    return [list(range(p, n, 2)) for p in range(2)]


def after(x, *earlier):
    return lax.optimization_barrier((x,) + earlier)[0]


def gather_parity(shard):
    return lax.all_gather(shard, "row", axis=0, tiled=True, axis_index_groups=parity_groups())


def scatter_parity(part):
    return lax.psum_scatter(part, "row", scatter_dimension=0, tiled=True, axis_index_groups=parity_groups())


def all_rows(left, right):
    rows, tile, width = left.shape[0], left.shape[1] // 4, right.shape[1]
    odd = (lax.axis_index("row") & 1).astype(jnp.int32).reshape(1)

    def kernel(odd_ref, left_ref, right_ref, out_ref):
        out_ref[...] = dot(left_ref[...], right_ref[...], 0, 0).astype(bf16)

    return tile_call(kernel, [left, right], [pl.BlockSpec((rows, tile), lambda i, m: (0, i)), whole(right.shape)],
                     jax.ShapeDtypeStruct((4 * tile, width), bf16),
                     pl.BlockSpec((tile, width), lambda i, m: (2 * ((i // 2) ^ m[0]) + i % 2, 0)), (4,), "all_rows", odd)


def scatter_rows(part):
    even, odd = parity_groups()
    return lax.psum_scatter(part, "row", scatter_dimension=0, tiled=True, axis_index_groups=[even + odd])


def trade_rows(left, right, parts=(2,)):
    tile = left.shape[1] // 2 // sum(parts)
    sent, first = [], sum(parts)
    for part in parts:
        sent.append(rows_call(left, right, first, (part,), tile))
        first += part
    return sent, [swap(part, "row", 1) for part in sent]


def own_rows(left, right, gots, *earlier):
    first = after(gots[0], *gots[1:], *earlier)
    tile = 512 if len(gots) == 1 else min(got.shape[0] for got in gots)
    return rows_call(left, right, 0, tuple(got.shape[0] // tile for got in gots), tile, [first, *gots[1:]])


def flip(first, second):
    odd = (lax.axis_index("row") & 1) == 1
    return jnp.where(odd, second, first), jnp.where(odd, first, second)


def by_parity(x, chunk):
    lead, width = x.shape
    parts = x.reshape(lead, width // (2 * chunk), 2, chunk)
    first, second = flip(parts[:, :, 0], parts[:, :, 1])
    return jnp.concatenate([first.reshape(lead, width // 2), second.reshape(lead, width // 2)], 1)


def by_place(x, chunk):
    lead, width = x.shape
    shape = (lead, width // (2 * chunk), chunk)
    first, second = flip(x[:, : width // 2].reshape(shape), x[:, width // 2 :].reshape(shape))
    return jnp.stack([first, second], 2).reshape(lead, width)


def per_device(tokens, lengths, norm_in, q_weight, k_weight, v_weight, conv_q, conv_k, conv_v, beta_weight,
               head_gain, out_weight, norm_mid, gate_weight, up_weight, down_weight, cotangent):
    rows, width = tokens.shape
    dh = head_gain.shape[0]
    hd = q_weight.shape[1]
    heads = hd // dh
    ff = gate_weight.shape[1]
    col = lax.axis_index("col")
    feat = lax.axis_size("col") * width
    live = live_column(lengths[0], rows)
    live_low = live.astype(bf16)
    beta_pad = jnp.pad(beta_weight, ((0, 0), (0, 128 - beta_weight.shape[1])))
    in_mine = gather_parity(jnp.concatenate([q_weight, k_weight, v_weight, beta_pad], 1))
    out_mine = gather_parity(out_weight.T)
    gate_mine = gather_parity(gate_weight)
    up_mine = gather_parity(up_weight)
    down_turned = down_weight.T
    down_side = swap(down_turned, "row", 1)
    down_mine = gather_parity(down_turned)
    down_other = gather_parity(down_side)
    conv = jnp.concatenate([conv_q, conv_k, conv_v], 1)
    gain = head_gain.reshape(1, dh)
    gain_in = lax.dynamic_slice_in_dim(norm_in, col * width, width)
    gain_mid = lax.dynamic_slice_in_dim(norm_mid, col * width, width)
    chunk = q_weight.shape[0]
    tokens, cotangent = by_parity(tokens, chunk), by_parity(cotangent, chunk)
    gain_in, gain_mid = by_parity(gain_in[None], chunk), by_parity(gain_mid[None], chunk)
    norm_in, norm_mid = by_parity(norm_in[None], chunk), by_parity(norm_mid[None], chunk)
    tokens32 = tokens.astype(f32)

    block = width // 2

    half = feat // 2
    normed, factor_in = join_norm(spread_cols(tokens), norm_in)
    ffn_cot = join(spread_cols(after(cotangent * live_low, down_side)))
    in_mine = after(in_mine, normed, ffn_cot)
    in_other, out_other = swap(in_mine, "row", 1), swap(out_mine, "row", 1)
    proj = halves(after(normed, out_mine), [(0, in_mine), (1, in_other)])
    gate_mine = after(gate_mine, proj)
    gate_other = swap(gate_mine, "row", 1)
    proj = after(proj, gate_mine)
    out_other = after(out_other, proj)
    w_in, w_out = (in_mine, in_other), (out_mine, out_other)
    mixed, *kept = mixer_forward(proj, conv, gain, heads, dh)
    branch = ColSum([(mixed, w_out)], block)
    sent = branch.send(1)
    sent = branch.send_last(*sent)
    up_mine = after(up_mine, *sent)
    up_other = swap(up_mine, "row", 1)
    middle = tokens32 + live * after(branch.total(), gate_other)
    mid_low = middle.astype(bf16)
    normed_mid, factor_mid = join_norm(spread_cols(mid_low), after(norm_mid, up_mine))
    w_gate, w_up = (gate_mine, gate_other), (up_mine, up_other)
    gate = halves(normed_mid, [(0, gate_mine), (1, gate_other)], bf16)
    up, hidden = hidden_call(after(normed_mid, gate), w_up, gate)
    down_sent = all_rows(ffn_cot, hidden)
    grad_down = scatter_rows(down_sent)
    w_down = after(down_mine, down_sent), after(down_other, down_sent)
    gate_cot, up_cot, inner_mid = cots_call(ffn_cot, w_down, gate, up)
    inner_mid = sum_all(inner_mid.reshape(rows // 128, 128), "col").reshape(rows, 1) / factor_mid
    mid_sum = ColSum([(gate_cot, w_gate), (up_cot, w_up)], block)
    sent = mid_sum.send(1)
    gate_sent, gate_got = trade_rows(after(normed_mid, *sent), gate_cot)
    mid_sum.send_last(inner_mid, gate_sent[0])
    up_sent, up_got = trade_rows(after(normed_mid, mid_sum.base), up_cot)
    mid_sum.got[0] = after(mid_sum.got[0], *up_sent)
    mid_cot = mid_sum.total()

    mid32 = mid_low.astype(f32)
    gmid_part = jnp.sum(mid_cot * mid32 * factor_mid, axis=0)
    middle_cot = cotangent.astype(f32) + factor_mid * gain_mid * mid_cot - mid32 * (factor_mid**3 * inner_mid / feat)
    branch_low = (live * middle_cot).astype(bf16)
    pieces = spread_cols(branch_low)
    gate_rows = own_rows(normed_mid, gate_cot, gate_got, pieces[2])
    grad_gate = scatter_parity(gate_rows)
    branch_cot = join(pieces)
    mixed_cot = halves(branch_cot, [(0, out_mine), (1, out_other)])
    out_sent, out_got = trade_rows(after(branch_cot, mixed_cot), mixed)
    mixed_cot = after(mixed_cot, *out_sent)
    low, gconv, ghead, inner_in = mixer_backward(proj, conv, gain, mixed_cot, kept, heads, dh)
    in_sum = ColSum([(low, w_in)], block)
    sent = in_sum.send(1)
    low_sent, low_got = trade_rows(after(normed, *sent), low)
    inner_in = sum_all(inner_in.reshape(rows // 128, 128), "col").reshape(rows, 1) / factor_in
    in_sum.send_last(inner_in, *low_sent)
    up_rows = own_rows(normed_mid, up_cot, up_got, *out_got, in_sum.base, grad_down)
    grad_up = scatter_parity(up_rows)
    out_rows = own_rows(branch_cot, mixed, out_got, grad_gate, up_rows)
    grad_out = scatter_parity(out_rows)
    in_cot = in_sum.total()
    gin_part = jnp.sum(in_cot * tokens32 * factor_in, axis=0)
    grad_tokens = middle_cot + factor_in * gain_in * in_cot - tokens32 * (factor_in**3 * inner_in / feat)

    def own_cols(part):
        part = by_place(part[None], chunk)[0]
        return lax.dynamic_update_slice_in_dim(jnp.zeros((feat,), f32), part, col * width, 0)

    sizes = [feat, feat, dh]
    wide = sum_all(jnp.concatenate([own_cols(gin_part), own_cols(gmid_part), ghead[0]]).reshape(-1, 128), "col")
    small = jnp.concatenate([wide, gconv.reshape(-1, 128)], 0)
    bits = bits_down(lax.axis_size("row"))
    for bit in bits[:-1]:
        small = small + swap(small, "row", bit)
    low_rows = own_rows(normed, low, low_got, out_rows, grad_up, small, grad_tokens)
    grad_low = scatter_parity(low_rows)
    in_cot = in_sum.total()
    gin_part = jnp.sum(in_cot * tokens32 * factor_in, axis=0)
    grad_tokens = middle_cot + factor_in * gain_in * in_cot - tokens32 * (factor_in**3 * inner_in / feat)

    def own_cols(part):
        part = by_place(part[None], chunk)[0]
        return lax.dynamic_update_slice_in_dim(jnp.zeros((feat,), f32), part, col * width, 0)

    sizes = [feat, feat, dh]
    wide = sum_all(jnp.concatenate([own_cols(gin_part), own_cols(gmid_part), ghead[0]]).reshape(-1, 128), "col")
    small = jnp.concatenate([wide, gconv.reshape(-1, 128)], 0)
    bits = bits_down(lax.axis_size("row"))
    for bit in bits[:-1]:
        small = small + swap(small, "row", bit)
    low_rows = own_rows(normed, low, low_got, out_rows, grad_up, small, grad_tokens)
    grad_low = scatter_parity(low_rows)
    result = ColSum([(hidden, w_down)], block)
    sent = result.send(1, low_rows)
    result.send_last(*sent)
    layer_out = (middle + live * result.total()).astype(bf16)
    small = small + swap(small, "row", bits[-1])
    wide, gconv = small[: wide.shape[0]].reshape(-1), small[wide.shape[0] :].reshape(gconv.shape)
    g_low = grad_low.astype(f32)
    return (
        by_place(layer_out, chunk),
        by_place(grad_tokens, chunk),
        wide[:feat],
        g_low[:, :hd],
        g_low[:, hd : 2 * hd],
        g_low[:, 2 * hd : 3 * hd],
        gconv[:, :hd],
        gconv[:, hd : 2 * hd],
        gconv[:, 2 * hd :],
        g_low[:, 3 * hd : 3 * hd + beta_weight.shape[1]],
        wide[2 * feat :],
        grad_out.astype(f32).T,
        wide[feat : 2 * feat],
        grad_gate.astype(f32),
        grad_up.astype(f32),
        grad_down.astype(f32).T,
    )


def solution(mesh):
    split_both, features, turned = P("row", "col"), P(None, "col"), P("col", "row")
    return jax.shard_map(
        per_device,
        mesh=mesh,
        in_specs=(split_both, P("row"), P(), split_both, split_both, split_both, features, features, features,
                  split_both, P(), turned, P(), split_both, split_both, turned, split_both),
        out_specs=(split_both, split_both, P(), split_both, split_both, split_both, features, features, features,
                   split_both, P(), turned, P(), split_both, split_both, turned),
        check_vma=False,
    )
```

```python
import functools
import jax
import jax.numpy as jnp
from jax import lax
from jax.experimental import pallas as pl
from jax.experimental.pallas import tpu as pltpu
from jax.sharding import PartitionSpec as P
from jax.experimental.layout import Layout, with_layout_constraint

CHUNK = 128
EPS = 1e-6
FREE = pl.CostEstimate(flops=2**20, bytes_accessed=2**18, transcendentals=0)
bf16 = jnp.bfloat16
f32 = jnp.float32


def split(x):
    high = x.astype(bf16)
    return high, (x - high.astype(f32)).astype(bf16)


def mm(a, b, ca=1, cb=0):
    def dg(u, v):
        return lax.dot_general(u, v, (((ca,), (cb,)), ((), ())), preferred_element_type=f32)

    return dg(a[0], b[0]) + (dg(a[0], b[1]) + dg(a[1], b[0]))


def sigmoid(x):
    return 0.5 * jnp.tanh(0.5 * x) + 0.5


def masks(n):
    r = lax.broadcasted_iota(jnp.int32, (n, n), 0)
    c = lax.broadcasted_iota(jnp.int32, (n, n), 1)
    return r, c


def unit_lower_inverse(lows, r, c):
    n = lows[0].shape[0]
    eye = jnp.where(r == c, 1.0, 0.0)
    invs = [eye - jnp.where(r // 2 == c // 2, low, 0.0) for low in lows]
    size = 2
    while size < n:
        mask = (r // (2 * size) == c // (2 * size)) & (r // size != c // size)
        offs = [split(jnp.where(mask, low, 0.0)) for low in lows]
        parts = [split(inv) for inv in invs]
        right = [split(mm(off, part)) for off, part in zip(offs, parts)]
        invs = [inv - mm(part, x) for inv, part, x in zip(invs, parts, right)]
        size *= 2
    return invs


def conv_rows(padded, taps, first):
    out = taps[0:1] * padded[first : first + CHUNK]
    for j in range(1, 4):
        out = out + taps[j : j + 1] * padded[first + j : first + j + CHUNK]
    return out


def fwd_kernel(heads, dh, x_ref, conv_ref, gain_ref, mixed_ref, o_ref, n_ref, t_ref, s_ref, state, halo):
    hd = heads * dh

    @pl.when(pl.program_id(0) == 0)
    def _():
        state[...] = jnp.zeros_like(state)
        halo[...] = jnp.zeros_like(halo)

    r, c = masks(CHUNK)
    each = range(heads)
    acts = []
    for p in range(3):
        for h in each:
            cols = slice(p * hd + h * dh, p * hd + (h + 1) * dh)
            y = conv_rows(jnp.concatenate([halo[:, cols], x_ref[:, cols]], 0), conv_ref[:, cols], 5)
            acts.append(y * sigmoid(y))
    qs = [split(acts[h] * dh ** -0.5) for h in each]
    ks = []
    for h in each:
        k = acts[heads + h]
        ks.append(split(k * lax.rsqrt(jnp.sum(k * k, axis=1, keepdims=True) + EPS)))
    b = [sigmoid(x_ref[:, 3 * hd + h : 3 * hd + h + 1]) for h in each]
    lows = [jnp.where(r > c, b[h] * mm(ks[h], ks[h], 1, 1), 0.0) for h in each]
    invs = unit_lower_inverse(lows, r, c)
    scores = [split(jnp.where(r >= c, mm(qs[h], ks[h], 1, 1), 0.0)) for h in each]
    s = [state[h] for h in each]
    ss = [split(s[h]) for h in each]
    right = [split(b[h] * (acts[2 * heads + h] - mm(ks[h], ss[h]))) for h in each]
    fresh = [mm(split(invs[h]), right[h]) for h in each]
    fs = [split(fresh[h]) for h in each]
    outs = [mm(qs[h], ss[h]) + mm(scores[h], fs[h]) for h in each]
    for h in each:
        state[h] = s[h] + mm(ks[h], fs[h], 0, 0)
        cols = slice(h * dh, (h + 1) * dh)
        s_ref[0, h] = s[h]
        t_ref[0, h] = invs[h]
        n_ref[:, cols] = fresh[h]
        o = outs[h]
        o_ref[:, cols] = o
        norm = lax.rsqrt(jnp.mean(o * o, axis=1, keepdims=True) + EPS)
        mixed_ref[:, cols] = (o * norm * gain_ref[...]).astype(bf16)
    halo[...] = x_ref[CHUNK - 8 :, : 3 * hd]


def bwd_kernel(heads, dh, x_ref, prev_ref, conv_ref, gain_ref, m_ref, o_ref, n_ref, t_ref, s_ref,
               low_ref, gconv_ref, ggain_ref, inner_ref, dstate, ghead):
    hd = heads * dh
    step = pl.program_id(0)

    @pl.when(step == 0)
    def _():
        dstate[...] = jnp.zeros_like(dstate)
        ghead[...] = jnp.zeros_like(ghead)
        gconv_ref[...] = jnp.zeros_like(gconv_ref)
        ggain_ref[...] = jnp.zeros_like(ggain_ref)

    has_prev = jnp.where(step == pl.num_programs(0) - 1, 0.0, 1.0)
    r, c = masks(CHUNK)
    lane = lax.broadcasted_iota(jnp.int32, (CHUNK, 128), 1)
    each = range(heads)
    scale = dh ** -0.5
    cuts = [slice(h * dh, (h + 1) * dh) for h in each]
    ys, sigs = [], []
    for p in range(3):
        for h in each:
            cols = slice(p * hd + h * dh, p * hd + (h + 1) * dh)
            padded = jnp.concatenate([prev_ref[:, cols] * has_prev, x_ref[:, cols]], 0)
            y = conv_rows(padded, conv_ref[:, cols], 5)
            ys.append(y)
            sigs.append(sigmoid(y))
    qs = [split(ys[h] * sigs[h] * scale) for h in each]
    kr = [ys[heads + h] * sigs[heads + h] for h in each]
    kinv = [lax.rsqrt(jnp.sum(kr[h] * kr[h], axis=1, keepdims=True) + EPS) for h in each]
    ks = [split(kr[h] * kinv[h]) for h in each]
    b = [sigmoid(x_ref[:, 3 * hd + h : 3 * hd + h + 1]) for h in each]
    dos = []
    ggain = jnp.zeros((1, dh), f32)
    for h in each:
        o = o_ref[:, cuts[h]]
        mc = m_ref[:, cuts[h]]
        norm = lax.rsqrt(jnp.mean(o * o, axis=1, keepdims=True) + EPS)
        ggain = ggain + jnp.sum(mc * (o * norm), axis=0, keepdims=True)
        dn_ = mc * gain_ref[...]
        do = norm * dn_ - o * (norm * norm * norm * jnp.mean(dn_ * o, axis=1, keepdims=True))
        dos.append(split(do))
    scores = [split(jnp.where(r >= c, mm(qs[h], ks[h], 1, 1), 0.0)) for h in each]
    part = [mm(scores[h], dos[h], 0, 0) for h in each]
    d = [dstate[h] for h in each]
    ds = [split(d[h]) for h in each]
    dfresh = [split(part[h] + mm(ks[h], ds[h])) for h in each]
    db_ = [mm(split(t_ref[0, h]), dfresh[h], 0, 0) for h in each]
    dr = [b[h] * db_[h] for h in each]
    drs = [split(dr[h]) for h in each]
    for h in each:
        dstate[h] = d[h] + (mm(qs[h], dos[h], 0, 0) - mm(ks[h], drs[h], 0, 0))
    ss = [split(s_ref[0, h]) for h in each]
    fs = [split(n_ref[:, cuts[h]]) for h in each]
    resid = [ys[2 * heads + h] * sigs[2 * heads + h] - mm(ks[h], ss[h]) for h in each]
    gram = [mm(ks[h], ks[h], 1, 1) for h in each]
    da = [jnp.where(r > c, -mm(split(db_[h]), fs[h], 1, 1), 0.0) for h in each]
    dsc = [split(jnp.where(r >= c, mm(dos[h], fs[h], 1, 1), 0.0)) for h in each]
    dq = [mm(dos[h], ss[h], 1, 1) + mm(dsc[h], ks[h]) for h in each]
    dgs = [split(b[h] * da[h]) for h in each]
    dk = [mm(dsc[h], qs[h], 0, 0) + mm(fs[h], ds[h], 1, 1) for h in each]
    dk = [dk[h] - mm(drs[h], ss[h], 1, 1) for h in each]
    dk = [dk[h] + (mm(dgs[h], ks[h]) + mm(dgs[h], ks[h], 0, 0)) for h in each]
    beta_low = jnp.zeros((CHUNK, 128), f32)
    inner = jnp.zeros((CHUNK, dh), f32)
    for h in each:
        dbeta = jnp.sum(db_[h] * resid[h], axis=1, keepdims=True) + jnp.sum(da[h] * gram[h], axis=1, keepdims=True)
        beta_low = jnp.where(lane == h, dbeta * b[h] * (1.0 - b[h]), beta_low)
    dkr = [kinv[h] * dk[h] - kr[h] * (kinv[h] * kinv[h] * kinv[h] * jnp.sum(dk[h] * kr[h], axis=1, keepdims=True)) for h in each]
    cots = [dq[h] * scale for h in each] + dkr + dr
    for p in range(3):
        for h in each:
            i = p * heads + h
            cols = slice(p * hd + h * dh, p * hd + (h + 1) * dh)
            g = cots[i] * sigs[i] * (1.0 + ys[i] * (1.0 - sigs[i]))
            taps = conv_ref[:, cols]
            gp = jnp.concatenate([g, ghead[:, cols]], 0)
            padded = jnp.concatenate([prev_ref[:, cols] * has_prev, x_ref[:, cols]], 0)
            out = taps[3:4] * g
            for j in range(3):
                out = out + taps[j : j + 1] * gp[3 - j : 3 - j + CHUNK]
            low_ref[:, cols] = out.astype(bf16)
            inner = inner + out * x_ref[:, cols]
            for j in range(4):
                gconv_ref[j : j + 1, cols] += jnp.sum(g * padded[5 + j : 5 + j + CHUNK], axis=0, keepdims=True)
            ghead[:, cols] = g[0:8]
    low_ref[:, 3 * hd :] = beta_low.astype(bf16)
    inner = inner + beta_low * x_ref[:, 3 * hd :]
    inner_ref[...] = jnp.sum(inner, axis=1, keepdims=True)
    ggain_ref[...] += ggain


def mixer_forward(proj, conv, gain, heads, dh):
    rows, width = proj.shape
    hd = heads * dh
    steps = rows // CHUNK
    square = pl.BlockSpec((1, heads, dh, dh), lambda i: (i, 0, 0, 0))
    wide = pl.BlockSpec((CHUNK, hd), lambda i: (i, 0))
    return pl.pallas_call(
        functools.partial(fwd_kernel, heads, dh),
        grid=(steps,),
        in_specs=[
            pl.BlockSpec((CHUNK, width), lambda i: (i, 0)),
            pl.BlockSpec((4, 3 * hd), lambda i: (0, 0)),
            pl.BlockSpec((1, dh), lambda i: (0, 0)),
        ],
        out_specs=[wide, wide, wide, pl.BlockSpec((1, heads, CHUNK, CHUNK), lambda i: (i, 0, 0, 0)), square],
        out_shape=[
            jax.ShapeDtypeStruct((rows, hd), bf16),
            jax.ShapeDtypeStruct((rows, hd), f32),
            jax.ShapeDtypeStruct((rows, hd), f32),
            jax.ShapeDtypeStruct((steps, heads, CHUNK, CHUNK), f32),
            jax.ShapeDtypeStruct((steps, heads, dh, dh), f32),
        ],
        scratch_shapes=[pltpu.VMEM((heads, dh, dh), f32), pltpu.VMEM((8, 3 * hd), f32)],
        compiler_params=pltpu.CompilerParams(vmem_limit_bytes=60 * 2**20),
        cost_estimate=FREE,
        name="mixer_forward",
    )(proj, conv, gain)


def mixer_backward(proj, conv, gain, mixed_cot, kept, heads, dh):
    o, fresh, inv, states = kept
    rows, width = proj.shape
    hd = heads * dh
    steps = rows // CHUNK
    last = steps - 1
    per = CHUNK // 8
    square = pl.BlockSpec((1, heads, dh, dh), lambda i: (last - i, 0, 0, 0))
    wide = pl.BlockSpec((CHUNK, hd), lambda i: (last - i, 0))
    return pl.pallas_call(
        functools.partial(bwd_kernel, heads, dh),
        grid=(steps,),
        in_specs=[
            pl.BlockSpec((CHUNK, width), lambda i: (last - i, 0)),
            pl.BlockSpec((8, width), lambda i: (jnp.maximum((last - i) * per - 1, 0), 0)),
            pl.BlockSpec((4, 3 * hd), lambda i: (0, 0)),
            pl.BlockSpec((1, dh), lambda i: (0, 0)),
            wide, wide, wide,
            pl.BlockSpec((1, heads, CHUNK, CHUNK), lambda i: (last - i, 0, 0, 0)),
            square,
        ],
        out_specs=[
            pl.BlockSpec((CHUNK, width), lambda i: (last - i, 0)),
            pl.BlockSpec((4, 3 * hd), lambda i: (0, 0)),
            pl.BlockSpec((1, dh), lambda i: (0, 0)),
            pl.BlockSpec((CHUNK, 1), lambda i: (last - i, 0)),
        ],
        out_shape=[
            jax.ShapeDtypeStruct((rows, width), bf16),
            jax.ShapeDtypeStruct((4, 3 * hd), f32),
            jax.ShapeDtypeStruct((1, dh), f32),
            jax.ShapeDtypeStruct((rows, 1), f32),
        ],
        scratch_shapes=[pltpu.VMEM((heads, dh, dh), f32), pltpu.VMEM((8, 3 * hd), f32)],
        compiler_params=pltpu.CompilerParams(vmem_limit_bytes=60 * 2**20),
        cost_estimate=FREE,
        name="mixer_backward",
    )(proj, proj, conv, gain, mixed_cot, o, fresh, inv, states)


def live_column(length, rows):
    return (lax.broadcasted_iota(jnp.int32, (rows, 1), 0) < length).astype(f32)


def swap(x, axis, bit):
    n = lax.axis_size(axis)
    return lax.ppermute(x, axis, [(i, i ^ bit) for i in range(n)])


def bits_down(n):
    bits = []
    while n > 1:
        n //= 2
        bits.append(n)
    return bits


def sum_all(x, axis):
    for bit in bits_down(lax.axis_size(axis)):
        x = x + swap(x, axis, bit)
    return x


def spread_cols(shard):
    n = lax.axis_size("col")
    pieces = {0: shard}
    for bit in bits_down(n):
        for j in list(pieces):
            pieces[j | bit] = swap(pieces[j], "col", bit)
    return [pieces[j] for j in range(n)]


class ColSum:
    def __init__(self, terms, block):
        self.terms, self.block = terms, block
        self.kept, self.got = list(range(lax.axis_size("col"))), {}

    def pieces(self, js, dtypes, earlier):
        (left, pair), rest = self.terms[0], self.terms[1:]
        gots = [self.got.pop(j, None) for j in js]
        return piece_call([(after(left, *earlier), pair)] + rest, self.block, js, gots, dtypes)

    def send(self, bit, *earlier):
        js = [j for j in self.kept if j & bit]
        last = bit > 1 and 2 * bit == lax.axis_size("col")
        sent = list(self.pieces(js + [0] * last, [bf16] * len(js) + [f32] * last, earlier))
        if last:
            self.base = sent.pop()
        for j, low in zip(js, sent):
            got, base = swap(low, "col", bit), j ^ bit
            self.got[base] = got if base not in self.got else self.got[base].astype(f32) + got.astype(f32)
        self.kept = [j for j in self.kept if not j & bit]
        return sent

    def send_last(self, *earlier):
        bit = 2
        while bit < lax.axis_size("col"):
            earlier = self.send(bit, *earlier)
            bit *= 2
        return earlier

    def total(self):
        return self.base + self.got[0].astype(f32)


def norm_kernel(width, me_ref, *refs):
    pieces, (gain_ref, normed_ref, factor_ref) = refs[:-3], refs[-3:]
    total = len(pieces) * width
    values = [p[...].astype(f32) for p in pieces]
    square = values[0] * values[0]
    for v in values[1:]:
        square = square + v * v
    factor = lax.rsqrt(jnp.sum(square, axis=1, keepdims=True) / total + EPS)
    factor_ref[...] = factor
    half = width // 2
    for j, v in enumerate(values):
        for p in range(2):
            start = p * (total // 2) + (me_ref[0] ^ j) * half
            cols = pl.ds(pl.multiple_of(start, half), half)
            normed_ref[:, cols] = (v[:, p * half : (p + 1) * half] * factor * gain_ref[:, cols]).astype(bf16)


def join_kernel(width, me_ref, *refs):
    pieces, out_ref = refs[:-1], refs[-1]
    half = width // 2
    for j, piece in enumerate(pieces):
        for p in range(2):
            start = p * len(pieces) * half + (me_ref[0] ^ j) * half
            out_ref[:, pl.ds(pl.multiple_of(start, half), half)] = piece[:, p * half : (p + 1) * half]


TILE = 512


def join_call(kernel, pieces, extra, outs, name):
    rows, width = pieces[0].shape
    me = lax.axis_index("col").astype(jnp.int32).reshape(1)
    return pl.pallas_call(
        functools.partial(kernel, width),
        grid_spec=pltpu.PrefetchScalarGridSpec(
            num_scalar_prefetch=1,
            grid=(rows // TILE,),
            in_specs=[pl.BlockSpec((TILE, width), lambda i, m: (i, 0))] * len(pieces)
            + [pl.BlockSpec(e.shape, lambda i, m: (0, 0)) for e in extra],
            out_specs=[pl.BlockSpec((TILE, o.shape[1]), lambda i, m: (i, 0)) for o in outs],
        ),
        out_shape=outs,
        compiler_params=pltpu.CompilerParams(vmem_limit_bytes=60 * 2**20),
        cost_estimate=FREE,
        name=name,
    )(me, *pieces, *extra)


def join_norm(pieces, gain):
    rows, width = pieces[0].shape
    outs = [jax.ShapeDtypeStruct((rows, width * len(pieces)), bf16), jax.ShapeDtypeStruct((rows, 1), f32)]
    return join_call(norm_kernel, pieces, [gain.reshape(1, -1)], outs, "join_norm")


def join(pieces):
    rows, width = pieces[0].shape
    return join_call(join_kernel, pieces, [], [jax.ShapeDtypeStruct((rows, width * len(pieces)), bf16)], "join")[0]


def dot(a, b, ca=1, cb=0):
    return lax.dot_general(a, b, (((ca,), (cb,)), ((), ())), preferred_element_type=f32)


FREE = pl.CostEstimate(flops=2**20, bytes_accessed=2**18, transcendentals=0)


def tile_call(kernel, arrays, specs, outs, out_specs, grid, name, me=None):
    params = dict(
        compiler_params=pltpu.CompilerParams(vmem_limit_bytes=48 * 2**20), cost_estimate=FREE, name=name
    )
    if me is None:
        return pl.pallas_call(kernel, grid=grid, in_specs=specs, out_specs=out_specs, out_shape=outs, **params)(*arrays)
    grid_spec = pltpu.PrefetchScalarGridSpec(
        num_scalar_prefetch=1, grid=grid, in_specs=specs, out_specs=out_specs
    )
    return pl.pallas_call(kernel, grid_spec=grid_spec, out_shape=outs, **params)(me, *arrays)


def row_tile(width):
    return pl.BlockSpec((TILE, width), lambda i, *_: (i, 0))


def half_tile(width, which):
    return pl.BlockSpec((TILE, width), lambda i, *_: (i, which))


def whole(shape):
    return pl.BlockSpec(shape, lambda i, *_: (0, 0))


def halves_kernel(count, *refs):
    out = refs[-1]
    total = dot(refs[0][...], refs[1][...])
    for i in range(1, count):
        total = total + dot(refs[2 * i][...], refs[2 * i + 1][...])
    out[...] = total.astype(out.dtype)


def halves(left, pairs, dtype=f32):
    rows, half, width = left.shape[0], left.shape[1] // 2, pairs[0][1].shape[1]
    arrays, specs = [], []
    for which, weight in pairs:
        arrays += [left, weight]
        specs += [half_tile(half, which), whole(weight.shape)]
    return tile_call(functools.partial(halves_kernel, len(pairs)), arrays, specs,
                     jax.ShapeDtypeStruct((rows, width), dtype), row_tile(width), (rows // TILE,), "halves")


def flat(ref):
    value = ref[...]
    return value.reshape(-1, value.shape[-1])


def weight_spec(w, p):
    if w.ndim == 2:
        return whole(w.shape)
    return pl.BlockSpec((w.shape[0], 1) + w.shape[2:], lambda i, *_: (0, p, 0, 0))


def block_spec(w, p, n, block):
    if w.ndim == 2:
        return pl.BlockSpec((block, w.shape[1]), lambda i, m: (m[n], 0))
    return pl.BlockSpec((block // w.shape[2], 1) + w.shape[2:], lambda i, m: (m[n], p, 0, 0))


def both(refs):
    return dot(refs[0][...], flat(refs[2])) + dot(refs[1][...], flat(refs[3]))


def hidden_kernel(*refs):
    gate_ref, up_ref, hidden_ref = refs[4:]
    up = both(refs)
    gate = gate_ref[...].astype(f32)
    up_ref[...] = up.astype(bf16)
    hidden_ref[...] = (gate * sigmoid(gate) * up).astype(bf16)


def both_specs(left, pair):
    half = left.shape[1] // 2
    return [left, left, *pair], [half_tile(half, 0), half_tile(half, 1), weight_spec(pair[0], 0), weight_spec(pair[1], 1)]


def hidden_call(left, pair, gate):
    rows, width = gate.shape
    tile = row_tile(width)
    arrays, specs = both_specs(left, pair)
    outs = [jax.ShapeDtypeStruct((rows, width), bf16)] * 2
    return tile_call(hidden_kernel, arrays + [gate], specs + [tile], outs, [tile, tile], (rows // TILE,), "hidden")


def cots_kernel(*refs):
    gate_ref, up_ref, gate_cot_ref, up_cot_ref, inner_ref = refs[4:]
    cot = both(refs)
    gate, up = gate_ref[...].astype(f32), up_ref[...].astype(f32)
    sig = sigmoid(gate)
    silu = gate * sig
    gate_cot = cot * up * (sig + silu * (1.0 - sig))
    up_cot = cot * silu
    gate_cot_ref[...] = gate_cot.astype(bf16)
    up_cot_ref[...] = up_cot.astype(bf16)
    inner_ref[...] = jnp.sum(gate_cot * gate + up_cot * up, axis=1, keepdims=True)


def cots_call(left, pair, gate, up):
    rows, width = gate.shape
    tile = row_tile(width)
    arrays, specs = both_specs(left, pair)
    outs = [jax.ShapeDtypeStruct((rows, width), bf16)] * 2 + [jax.ShapeDtypeStruct((rows, 1), f32)]
    return tile_call(cots_kernel, arrays + [gate, up], specs + [tile, tile], outs, [tile, tile, row_tile(1)],
                     (rows // TILE,), "cots")


def piece_kernel(count, pieces, has_got, me_ref, *refs):
    outs = refs[-pieces:]
    stride = 1 + 2 * pieces
    for n, out in enumerate(outs):
        width = out.shape[1] // 2
        for p in range(2):
            total = None
            for i in range(count):
                term = dot(refs[stride * i][...], flat(refs[stride * i + 1 + 2 * n + p]), 1, 1)
                total = term if total is None else total + term
            if has_got:
                total = total + refs[stride * count + n][:, p * width : (p + 1) * width].astype(f32)
            out[:, p * width : (p + 1) * width] = total.astype(out.dtype)


def piece_call(terms, block, js, gots, dtypes):
    rows = terms[0][0].shape[0]
    me = jnp.stack([lax.axis_index("col") ^ j for j in js]).astype(jnp.int32)
    arrays, specs = [], []
    for left, pair in terms:
        arrays.append(left)
        specs.append(row_tile(left.shape[1]))
        for n in range(len(js)):
            arrays += pair
            specs += [block_spec(w, p, n, block) for p, w in enumerate(pair)]
    has_got = gots[0] is not None
    if has_got:
        arrays += gots
        specs += [row_tile(2 * block)] * len(js)
    kernel = functools.partial(piece_kernel, len(terms), len(js), has_got)
    outs = [jax.ShapeDtypeStruct((rows, 2 * block), dtype) for dtype in dtypes]
    return tile_call(kernel, arrays, specs, outs, [row_tile(2 * block)] * len(js), (rows // TILE,), "piece", me)


def rows_kernel(parts, left_ref, right_ref, *refs):
    total = dot(left_ref[...], right_ref[...], 0, 0)
    gots, out = refs[:-1], refs[-1]
    if not gots:
        out[...] = total.astype(bf16)
    start = 0
    for got, part in zip(gots, parts):

        @pl.when((pl.program_id(0) >= start) & (pl.program_id(0) < start + part))
        def _(got=got):
            out[...] = (total + got[...].astype(f32)).astype(bf16)

        start += part


def rows_call(left, right, first, parts, tile, gots=()):
    rows, width, count = left.shape[0], right.shape[1], sum(parts)
    specs = [pl.BlockSpec((rows, tile), lambda i: (0, first + i)), whole(right.shape)]
    start = 0
    for _, part in zip(gots, parts):
        specs.append(pl.BlockSpec((tile, width), lambda i, s=start, p=part: (jnp.clip(i - s, 0, p - 1), 0)))
        start += part
    out = pl.BlockSpec((tile, width), lambda i: (i, 0))
    return tile_call(functools.partial(rows_kernel, parts), [left, right, *gots], specs,
                     jax.ShapeDtypeStruct((count * tile, width), bf16), out, (count,), "rows")


def parity_groups():
    n = lax.axis_size("row")
    return [list(range(p, n, 2)) for p in range(2)]


def after(x, *earlier):
    return lax.optimization_barrier((x,) + earlier)[0]


def gather_parity(shard):
    return lax.all_gather(shard, "row", axis=0, tiled=True, axis_index_groups=parity_groups())


def scatter_parity(part):
    return lax.psum_scatter(part, "row", scatter_dimension=0, tiled=True, axis_index_groups=parity_groups())


def all_rows(left, right):
    rows, tile, width = left.shape[0], left.shape[1] // 4, right.shape[1]
    odd = (lax.axis_index("row") & 1).astype(jnp.int32).reshape(1)

    def kernel(odd_ref, left_ref, right_ref, out_ref):
        out_ref[...] = dot(left_ref[...], right_ref[...], 0, 0).astype(bf16)

    return tile_call(kernel, [left, right], [pl.BlockSpec((rows, tile), lambda i, m: (0, i)), whole(right.shape)],
                     jax.ShapeDtypeStruct((4 * tile, width), bf16),
                     pl.BlockSpec((tile, width), lambda i, m: (2 * ((i // 2) ^ m[0]) + i % 2, 0)), (4,), "all_rows", odd)


def scatter_rows(part):
    even, odd = parity_groups()
    return lax.psum_scatter(part, "row", scatter_dimension=0, tiled=True, axis_index_groups=[even + odd])


def trade_rows(left, right, parts=(2,)):
    tile = left.shape[1] // 2 // sum(parts)
    sent, first = [], sum(parts)
    for part in parts:
        sent.append(rows_call(left, right, first, (part,), tile))
        first += part
    return sent, [swap(part, "row", 1) for part in sent]


def own_rows(left, right, gots, *earlier):
    first = after(gots[0], *gots[1:], *earlier)
    tile = 512 if len(gots) == 1 else min(got.shape[0] for got in gots)
    return rows_call(left, right, 0, tuple(got.shape[0] // tile for got in gots), tile, [first, *gots[1:]])


def flip(first, second):
    odd = (lax.axis_index("row") & 1) == 1
    return jnp.where(odd, second, first), jnp.where(odd, first, second)


def by_parity(x, chunk):
    lead, width = x.shape
    parts = x.reshape(lead, width // (2 * chunk), 2, chunk)
    first, second = flip(parts[:, :, 0], parts[:, :, 1])
    return jnp.concatenate([first.reshape(lead, width // 2), second.reshape(lead, width // 2)], 1)


def by_place(x, chunk):
    lead, width = x.shape
    shape = (lead, width // (2 * chunk), chunk)
    first, second = flip(x[:, : width // 2].reshape(shape), x[:, width // 2 :].reshape(shape))
    return jnp.stack([first, second], 2).reshape(lead, width)


def per_device(tokens, lengths, norm_in, q_weight, k_weight, v_weight, conv_q, conv_k, conv_v, beta_weight,
               head_gain, out_weight, norm_mid, gate_weight, up_weight, down_weight, cotangent):
    rows, width = tokens.shape
    dh = head_gain.shape[0]
    hd = q_weight.shape[1]
    heads = hd // dh
    ff = gate_weight.shape[1]
    col = lax.axis_index("col")
    feat = lax.axis_size("col") * width
    live = live_column(lengths[0], rows)
    live_low = live.astype(bf16)
    beta_pad = jnp.pad(beta_weight, ((0, 0), (0, 128 - beta_weight.shape[1])))
    in_mine = gather_parity(jnp.concatenate([q_weight, k_weight, v_weight, beta_pad], 1))
    out_mine = gather_parity(out_weight.T)
    gate_mine = gather_parity(gate_weight)
    up_mine = gather_parity(up_weight)
    down_turned = down_weight.T
    down_side = swap(down_turned, "row", 1)
    down_both = with_layout_constraint(jnp.concatenate([down_turned, down_side], 0), Layout((0, 1)))
    down_rows = with_layout_constraint(gather_parity(down_both), Layout((0, 1))).reshape(-1, 2, *down_turned.shape)
    conv = jnp.concatenate([conv_q, conv_k, conv_v], 1)
    gain = head_gain.reshape(1, dh)
    gain_in = lax.dynamic_slice_in_dim(norm_in, col * width, width)
    gain_mid = lax.dynamic_slice_in_dim(norm_mid, col * width, width)
    chunk = q_weight.shape[0]
    tokens, cotangent = by_parity(tokens, chunk), by_parity(cotangent, chunk)
    gain_in, gain_mid = by_parity(gain_in[None], chunk), by_parity(gain_mid[None], chunk)
    norm_in, norm_mid = by_parity(norm_in[None], chunk), by_parity(norm_mid[None], chunk)
    tokens32 = tokens.astype(f32)

    block = width // 2

    half = feat // 2
    normed, factor_in = join_norm(spread_cols(tokens), norm_in)
    ffn_cot = join(spread_cols(after(cotangent * live_low, down_side)))
    in_mine = after(in_mine, normed, ffn_cot)
    in_other, out_other = swap(in_mine, "row", 1), swap(out_mine, "row", 1)
    proj = halves(after(normed, out_mine), [(0, in_mine), (1, in_other)])
    gate_mine = after(gate_mine, proj)
    gate_other = swap(gate_mine, "row", 1)
    proj = after(proj, gate_mine)
    out_other = after(out_other, proj)
    w_in, w_out = (in_mine, in_other), (out_mine, out_other)
    mixed, *kept = mixer_forward(proj, conv, gain, heads, dh)
    branch = ColSum([(mixed, w_out)], block)
    sent = branch.send(1)
    sent = branch.send_last(*sent)
    up_mine = after(up_mine, *sent)
    up_other = swap(up_mine, "row", 1)
    middle = tokens32 + live * after(branch.total(), gate_other)
    mid_low = middle.astype(bf16)
    normed_mid, factor_mid = join_norm(spread_cols(mid_low), after(norm_mid, up_mine))
    w_gate, w_up = (gate_mine, gate_other), (up_mine, up_other)
    gate = halves(normed_mid, [(0, gate_mine), (1, gate_other)], bf16)
    up, hidden = hidden_call(after(normed_mid, gate), w_up, gate)
    down_sent = all_rows(ffn_cot, hidden)
    grad_down = scatter_rows(down_sent)
    w_down = (after(down_rows, down_sent),) * 2
    gate_cot, up_cot, inner_mid = cots_call(ffn_cot, w_down, gate, up)
    inner_mid = sum_all(inner_mid.reshape(rows // 128, 128), "col").reshape(rows, 1) / factor_mid
    mid_sum = ColSum([(gate_cot, w_gate), (up_cot, w_up)], block)
    sent = mid_sum.send(1)
    gate_sent, gate_got = trade_rows(after(normed_mid, *sent), gate_cot)
    mid_sum.send_last(inner_mid, gate_sent[0])
    up_sent, up_got = trade_rows(after(normed_mid, mid_sum.base), up_cot)
    mid_sum.got[0] = after(mid_sum.got[0], *up_sent)
    mid_cot = mid_sum.total()

    mid32 = mid_low.astype(f32)
    gmid_part = jnp.sum(mid_cot * mid32 * factor_mid, axis=0)
    middle_cot = cotangent.astype(f32) + factor_mid * gain_mid * mid_cot - mid32 * (factor_mid**3 * inner_mid / feat)
    branch_low = (live * middle_cot).astype(bf16)
    pieces = spread_cols(branch_low)
    gate_rows = own_rows(normed_mid, gate_cot, gate_got, pieces[2])
    grad_gate = scatter_parity(gate_rows)
    branch_cot = join(pieces)
    mixed_cot = halves(branch_cot, [(0, out_mine), (1, out_other)])
    out_sent, out_got = trade_rows(after(branch_cot, mixed_cot), mixed)
    mixed_cot = after(mixed_cot, *out_sent)
    low, gconv, ghead, inner_in = mixer_backward(proj, conv, gain, mixed_cot, kept, heads, dh)
    in_sum = ColSum([(low, w_in)], block)
    sent = in_sum.send(1)
    low_sent, low_got = trade_rows(after(normed, *sent), low)
    inner_in = sum_all(inner_in.reshape(rows // 128, 128), "col").reshape(rows, 1) / factor_in
    in_sum.send_last(inner_in, *low_sent)
    up_rows = own_rows(normed_mid, up_cot, up_got, *out_got, in_sum.base, grad_down)
    grad_up = scatter_parity(up_rows)
    out_rows = own_rows(branch_cot, mixed, out_got, grad_gate, up_rows)
    grad_out = scatter_parity(out_rows)
    in_cot = in_sum.total()
    gin_part = jnp.sum(in_cot * tokens32 * factor_in, axis=0)
    grad_tokens = middle_cot + factor_in * gain_in * in_cot - tokens32 * (factor_in**3 * inner_in / feat)

    def own_cols(part):
        part = by_place(part[None], chunk)[0]
        return lax.dynamic_update_slice_in_dim(jnp.zeros((feat,), f32), part, col * width, 0)

    sizes = [feat, feat, dh]
    wide = sum_all(jnp.concatenate([own_cols(gin_part), own_cols(gmid_part), ghead[0]]).reshape(-1, 128), "col")
    small = jnp.concatenate([wide, gconv.reshape(-1, 128)], 0)
    bits = bits_down(lax.axis_size("row"))
    for bit in bits[:-1]:
        small = small + swap(small, "row", bit)
    low_rows = own_rows(normed, low, low_got, out_rows, grad_up, small, grad_tokens)
    grad_low = scatter_parity(low_rows)
    in_cot = in_sum.total()
    gin_part = jnp.sum(in_cot * tokens32 * factor_in, axis=0)
    grad_tokens = middle_cot + factor_in * gain_in * in_cot - tokens32 * (factor_in**3 * inner_in / feat)

    def own_cols(part):
        part = by_place(part[None], chunk)[0]
        return lax.dynamic_update_slice_in_dim(jnp.zeros((feat,), f32), part, col * width, 0)

    sizes = [feat, feat, dh]
    wide = sum_all(jnp.concatenate([own_cols(gin_part), own_cols(gmid_part), ghead[0]]).reshape(-1, 128), "col")
    small = jnp.concatenate([wide, gconv.reshape(-1, 128)], 0)
    bits = bits_down(lax.axis_size("row"))
    for bit in bits[:-1]:
        small = small + swap(small, "row", bit)
    low_rows = own_rows(normed, low, low_got, out_rows, grad_up, small, grad_tokens)
    grad_low = scatter_parity(low_rows)
    result = ColSum([(hidden, w_down)], block)
    sent = result.send(1, low_rows)
    result.send_last(*sent)
    layer_out = (middle + live * result.total()).astype(bf16)
    small = small + swap(small, "row", bits[-1])
    wide, gconv = small[: wide.shape[0]].reshape(-1), small[wide.shape[0] :].reshape(gconv.shape)
    g_low = grad_low.astype(f32)
    return (
        by_place(layer_out, chunk),
        by_place(grad_tokens, chunk),
        wide[:feat],
        g_low[:, :hd],
        g_low[:, hd : 2 * hd],
        g_low[:, 2 * hd : 3 * hd],
        gconv[:, :hd],
        gconv[:, hd : 2 * hd],
        gconv[:, 2 * hd :],
        g_low[:, 3 * hd : 3 * hd + beta_weight.shape[1]],
        wide[2 * feat :],
        grad_out.astype(f32).T,
        wide[feat : 2 * feat],
        grad_gate.astype(f32),
        grad_up.astype(f32),
        grad_down.astype(f32).T,
    )


def solution(mesh):
    split_both, features, turned = P("row", "col"), P(None, "col"), P("col", "row")
    return jax.shard_map(
        per_device,
        mesh=mesh,
        in_specs=(split_both, P("row"), P(), split_both, split_both, split_both, features, features, features,
                  split_both, P(), turned, P(), split_both, split_both, turned, split_both),
        out_specs=(split_both, split_both, P(), split_both, split_both, split_both, features, features, features,
                   split_both, P(), turned, P(), split_both, split_both, turned),
        check_vma=False,
    )
```

```python
import functools
import jax
import jax.numpy as jnp
from jax import lax
from jax.experimental import pallas as pl
from jax.experimental.pallas import tpu as pltpu
from jax.sharding import PartitionSpec as P
from jax.experimental.layout import Layout, with_layout_constraint

CHUNK = 128
EPS = 1e-6
FREE = pl.CostEstimate(flops=2**20, bytes_accessed=2**18, transcendentals=0)
bf16 = jnp.bfloat16
f32 = jnp.float32


def split(x):
    high = x.astype(bf16)
    return high, (x - high.astype(f32)).astype(bf16)


def mm(a, b, ca=1, cb=0):
    def dg(u, v):
        return lax.dot_general(u, v, (((ca,), (cb,)), ((), ())), preferred_element_type=f32)

    return dg(a[0], b[0]) + (dg(a[0], b[1]) + dg(a[1], b[0]))


def sigmoid(x):
    return 0.5 * jnp.tanh(0.5 * x) + 0.5


def masks(n):
    r = lax.broadcasted_iota(jnp.int32, (n, n), 0)
    c = lax.broadcasted_iota(jnp.int32, (n, n), 1)
    return r, c


def unit_lower_inverse(lows, r, c):
    n = lows[0].shape[0]
    eye = jnp.where(r == c, 1.0, 0.0)
    invs = [eye - jnp.where(r // 2 == c // 2, low, 0.0) for low in lows]
    size = 2
    while size < n:
        mask = (r // (2 * size) == c // (2 * size)) & (r // size != c // size)
        offs = [split(jnp.where(mask, low, 0.0)) for low in lows]
        parts = [split(inv) for inv in invs]
        right = [split(mm(off, part)) for off, part in zip(offs, parts)]
        invs = [inv - mm(part, x) for inv, part, x in zip(invs, parts, right)]
        size *= 2
    return invs


def conv_rows(padded, taps, first):
    out = taps[0:1] * padded[first : first + CHUNK]
    for j in range(1, 4):
        out = out + taps[j : j + 1] * padded[first + j : first + j + CHUNK]
    return out


def fwd_kernel(heads, dh, x_ref, conv_ref, gain_ref, mixed_ref, o_ref, n_ref, t_ref, s_ref, state, halo):
    hd = heads * dh

    @pl.when(pl.program_id(0) == 0)
    def _():
        state[...] = jnp.zeros_like(state)
        halo[...] = jnp.zeros_like(halo)

    r, c = masks(CHUNK)
    each = range(heads)
    acts = []
    for p in range(3):
        for h in each:
            cols = slice(p * hd + h * dh, p * hd + (h + 1) * dh)
            y = conv_rows(jnp.concatenate([halo[:, cols], x_ref[:, cols]], 0), conv_ref[:, cols], 5)
            acts.append(y * sigmoid(y))
    qs = [split(acts[h] * dh ** -0.5) for h in each]
    ks = []
    for h in each:
        k = acts[heads + h]
        ks.append(split(k * lax.rsqrt(jnp.sum(k * k, axis=1, keepdims=True) + EPS)))
    b = [sigmoid(x_ref[:, 3 * hd + h : 3 * hd + h + 1]) for h in each]
    lows = [jnp.where(r > c, b[h] * mm(ks[h], ks[h], 1, 1), 0.0) for h in each]
    invs = unit_lower_inverse(lows, r, c)
    scores = [split(jnp.where(r >= c, mm(qs[h], ks[h], 1, 1), 0.0)) for h in each]
    s = [state[h] for h in each]
    ss = [split(s[h]) for h in each]
    right = [split(b[h] * (acts[2 * heads + h] - mm(ks[h], ss[h]))) for h in each]
    fresh = [mm(split(invs[h]), right[h]) for h in each]
    fs = [split(fresh[h]) for h in each]
    outs = [mm(qs[h], ss[h]) + mm(scores[h], fs[h]) for h in each]
    for h in each:
        state[h] = s[h] + mm(ks[h], fs[h], 0, 0)
        cols = slice(h * dh, (h + 1) * dh)
        s_ref[0, h] = s[h]
        t_ref[0, h] = invs[h]
        n_ref[:, cols] = fresh[h]
        o = outs[h]
        o_ref[:, cols] = o
        norm = lax.rsqrt(jnp.mean(o * o, axis=1, keepdims=True) + EPS)
        mixed_ref[:, cols] = (o * norm * gain_ref[...]).astype(bf16)
    halo[...] = x_ref[CHUNK - 8 :, : 3 * hd]


def bwd_kernel(heads, dh, x_ref, prev_ref, conv_ref, gain_ref, m_ref, o_ref, n_ref, t_ref, s_ref,
               low_ref, gconv_ref, ggain_ref, inner_ref, dstate, ghead):
    hd = heads * dh
    step = pl.program_id(0)

    @pl.when(step == 0)
    def _():
        dstate[...] = jnp.zeros_like(dstate)
        ghead[...] = jnp.zeros_like(ghead)
        gconv_ref[...] = jnp.zeros_like(gconv_ref)
        ggain_ref[...] = jnp.zeros_like(ggain_ref)

    has_prev = jnp.where(step == pl.num_programs(0) - 1, 0.0, 1.0)
    r, c = masks(CHUNK)
    lane = lax.broadcasted_iota(jnp.int32, (CHUNK, 128), 1)
    each = range(heads)
    scale = dh ** -0.5
    cuts = [slice(h * dh, (h + 1) * dh) for h in each]
    ys, sigs = [], []
    for p in range(3):
        for h in each:
            cols = slice(p * hd + h * dh, p * hd + (h + 1) * dh)
            padded = jnp.concatenate([prev_ref[:, cols] * has_prev, x_ref[:, cols]], 0)
            y = conv_rows(padded, conv_ref[:, cols], 5)
            ys.append(y)
            sigs.append(sigmoid(y))
    qs = [split(ys[h] * sigs[h] * scale) for h in each]
    kr = [ys[heads + h] * sigs[heads + h] for h in each]
    kinv = [lax.rsqrt(jnp.sum(kr[h] * kr[h], axis=1, keepdims=True) + EPS) for h in each]
    ks = [split(kr[h] * kinv[h]) for h in each]
    b = [sigmoid(x_ref[:, 3 * hd + h : 3 * hd + h + 1]) for h in each]
    dos = []
    ggain = jnp.zeros((1, dh), f32)
    for h in each:
        o = o_ref[:, cuts[h]]
        mc = m_ref[:, cuts[h]]
        norm = lax.rsqrt(jnp.mean(o * o, axis=1, keepdims=True) + EPS)
        ggain = ggain + jnp.sum(mc * (o * norm), axis=0, keepdims=True)
        dn_ = mc * gain_ref[...]
        do = norm * dn_ - o * (norm * norm * norm * jnp.mean(dn_ * o, axis=1, keepdims=True))
        dos.append(split(do))
    scores = [split(jnp.where(r >= c, mm(qs[h], ks[h], 1, 1), 0.0)) for h in each]
    part = [mm(scores[h], dos[h], 0, 0) for h in each]
    d = [dstate[h] for h in each]
    ds = [split(d[h]) for h in each]
    dfresh = [split(part[h] + mm(ks[h], ds[h])) for h in each]
    db_ = [mm(split(t_ref[0, h]), dfresh[h], 0, 0) for h in each]
    dr = [b[h] * db_[h] for h in each]
    drs = [split(dr[h]) for h in each]
    for h in each:
        dstate[h] = d[h] + (mm(qs[h], dos[h], 0, 0) - mm(ks[h], drs[h], 0, 0))
    ss = [split(s_ref[0, h]) for h in each]
    fs = [split(n_ref[:, cuts[h]]) for h in each]
    resid = [ys[2 * heads + h] * sigs[2 * heads + h] - mm(ks[h], ss[h]) for h in each]
    gram = [mm(ks[h], ks[h], 1, 1) for h in each]
    da = [jnp.where(r > c, -mm(split(db_[h]), fs[h], 1, 1), 0.0) for h in each]
    dsc = [split(jnp.where(r >= c, mm(dos[h], fs[h], 1, 1), 0.0)) for h in each]
    dq = [mm(dos[h], ss[h], 1, 1) + mm(dsc[h], ks[h]) for h in each]
    dgs = [split(b[h] * da[h]) for h in each]
    dk = [mm(dsc[h], qs[h], 0, 0) + mm(fs[h], ds[h], 1, 1) for h in each]
    dk = [dk[h] - mm(drs[h], ss[h], 1, 1) for h in each]
    dk = [dk[h] + (mm(dgs[h], ks[h]) + mm(dgs[h], ks[h], 0, 0)) for h in each]
    beta_low = jnp.zeros((CHUNK, 128), f32)
    inner = jnp.zeros((CHUNK, dh), f32)
    for h in each:
        dbeta = jnp.sum(db_[h] * resid[h], axis=1, keepdims=True) + jnp.sum(da[h] * gram[h], axis=1, keepdims=True)
        beta_low = jnp.where(lane == h, dbeta * b[h] * (1.0 - b[h]), beta_low)
    dkr = [kinv[h] * dk[h] - kr[h] * (kinv[h] * kinv[h] * kinv[h] * jnp.sum(dk[h] * kr[h], axis=1, keepdims=True)) for h in each]
    cots = [dq[h] * scale for h in each] + dkr + dr
    for p in range(3):
        for h in each:
            i = p * heads + h
            cols = slice(p * hd + h * dh, p * hd + (h + 1) * dh)
            g = cots[i] * sigs[i] * (1.0 + ys[i] * (1.0 - sigs[i]))
            taps = conv_ref[:, cols]
            gp = jnp.concatenate([g, ghead[:, cols]], 0)
            padded = jnp.concatenate([prev_ref[:, cols] * has_prev, x_ref[:, cols]], 0)
            out = taps[3:4] * g
            for j in range(3):
                out = out + taps[j : j + 1] * gp[3 - j : 3 - j + CHUNK]
            low_ref[:, cols] = out.astype(bf16)
            inner = inner + out * x_ref[:, cols]
            for j in range(4):
                gconv_ref[j : j + 1, cols] += jnp.sum(g * padded[5 + j : 5 + j + CHUNK], axis=0, keepdims=True)
            ghead[:, cols] = g[0:8]
    low_ref[:, 3 * hd :] = beta_low.astype(bf16)
    inner = inner + beta_low * x_ref[:, 3 * hd :]
    inner_ref[...] = jnp.sum(inner, axis=1, keepdims=True)
    ggain_ref[...] += ggain


def mixer_forward(proj, conv, gain, heads, dh):
    rows, width = proj.shape
    hd = heads * dh
    steps = rows // CHUNK
    square = pl.BlockSpec((1, heads, dh, dh), lambda i: (i, 0, 0, 0))
    wide = pl.BlockSpec((CHUNK, hd), lambda i: (i, 0))
    return pl.pallas_call(
        functools.partial(fwd_kernel, heads, dh),
        grid=(steps,),
        in_specs=[
            pl.BlockSpec((CHUNK, width), lambda i: (i, 0)),
            pl.BlockSpec((4, 3 * hd), lambda i: (0, 0)),
            pl.BlockSpec((1, dh), lambda i: (0, 0)),
        ],
        out_specs=[wide, wide, wide, pl.BlockSpec((1, heads, CHUNK, CHUNK), lambda i: (i, 0, 0, 0)), square],
        out_shape=[
            jax.ShapeDtypeStruct((rows, hd), bf16),
            jax.ShapeDtypeStruct((rows, hd), f32),
            jax.ShapeDtypeStruct((rows, hd), f32),
            jax.ShapeDtypeStruct((steps, heads, CHUNK, CHUNK), f32),
            jax.ShapeDtypeStruct((steps, heads, dh, dh), f32),
        ],
        scratch_shapes=[pltpu.VMEM((heads, dh, dh), f32), pltpu.VMEM((8, 3 * hd), f32)],
        compiler_params=pltpu.CompilerParams(vmem_limit_bytes=60 * 2**20),
        cost_estimate=FREE,
        name="mixer_forward",
    )(proj, conv, gain)


def mixer_backward(proj, conv, gain, mixed_cot, kept, heads, dh):
    o, fresh, inv, states = kept
    rows, width = proj.shape
    hd = heads * dh
    steps = rows // CHUNK
    last = steps - 1
    per = CHUNK // 8
    square = pl.BlockSpec((1, heads, dh, dh), lambda i: (last - i, 0, 0, 0))
    wide = pl.BlockSpec((CHUNK, hd), lambda i: (last - i, 0))
    return pl.pallas_call(
        functools.partial(bwd_kernel, heads, dh),
        grid=(steps,),
        in_specs=[
            pl.BlockSpec((CHUNK, width), lambda i: (last - i, 0)),
            pl.BlockSpec((8, width), lambda i: (jnp.maximum((last - i) * per - 1, 0), 0)),
            pl.BlockSpec((4, 3 * hd), lambda i: (0, 0)),
            pl.BlockSpec((1, dh), lambda i: (0, 0)),
            wide, wide, wide,
            pl.BlockSpec((1, heads, CHUNK, CHUNK), lambda i: (last - i, 0, 0, 0)),
            square,
        ],
        out_specs=[
            pl.BlockSpec((CHUNK, width), lambda i: (last - i, 0)),
            pl.BlockSpec((4, 3 * hd), lambda i: (0, 0)),
            pl.BlockSpec((1, dh), lambda i: (0, 0)),
            pl.BlockSpec((CHUNK, 1), lambda i: (last - i, 0)),
        ],
        out_shape=[
            jax.ShapeDtypeStruct((rows, width), bf16),
            jax.ShapeDtypeStruct((4, 3 * hd), f32),
            jax.ShapeDtypeStruct((1, dh), f32),
            jax.ShapeDtypeStruct((rows, 1), f32),
        ],
        scratch_shapes=[pltpu.VMEM((heads, dh, dh), f32), pltpu.VMEM((8, 3 * hd), f32)],
        compiler_params=pltpu.CompilerParams(vmem_limit_bytes=60 * 2**20),
        cost_estimate=FREE,
        name="mixer_backward",
    )(proj, proj, conv, gain, mixed_cot, o, fresh, inv, states)


def live_column(length, rows):
    return (lax.broadcasted_iota(jnp.int32, (rows, 1), 0) < length).astype(f32)


def swap(x, axis, bit):
    n = lax.axis_size(axis)
    return lax.ppermute(x, axis, [(i, i ^ bit) for i in range(n)])


def bits_down(n):
    bits = []
    while n > 1:
        n //= 2
        bits.append(n)
    return bits


def sum_all(x, axis):
    for bit in bits_down(lax.axis_size(axis)):
        x = x + swap(x, axis, bit)
    return x


def spread_cols(shard):
    n = lax.axis_size("col")
    pieces = {0: shard}
    for bit in bits_down(n):
        for j in list(pieces):
            pieces[j | bit] = swap(pieces[j], "col", bit)
    return [pieces[j] for j in range(n)]


class ColSum:
    def __init__(self, terms, block):
        self.terms, self.block = terms, block
        self.kept, self.got = list(range(lax.axis_size("col"))), {}

    def pieces(self, js, dtypes, earlier):
        (left, pair), rest = self.terms[0], self.terms[1:]
        gots = [self.got.pop(j, None) for j in js]
        return piece_call([(after(left, *earlier), pair)] + rest, self.block, js, gots, dtypes)

    def send(self, bit, *earlier):
        js = [j for j in self.kept if j & bit]
        last = bit > 1 and 2 * bit == lax.axis_size("col")
        sent = list(self.pieces(js + [0] * last, [bf16] * len(js) + [f32] * last, earlier))
        if last:
            self.base = sent.pop()
        for j, low in zip(js, sent):
            got, base = swap(low, "col", bit), j ^ bit
            self.got[base] = got if base not in self.got else self.got[base].astype(f32) + got.astype(f32)
        self.kept = [j for j in self.kept if not j & bit]
        return sent

    def send_last(self, *earlier):
        bit = 2
        while bit < lax.axis_size("col"):
            earlier = self.send(bit, *earlier)
            bit *= 2
        return earlier

    def total(self):
        return self.base + self.got[0].astype(f32)


def norm_kernel(width, me_ref, *refs):
    pieces, (gain_ref, normed_ref, factor_ref) = refs[:-3], refs[-3:]
    total = len(pieces) * width
    values = [p[...].astype(f32) for p in pieces]
    square = values[0] * values[0]
    for v in values[1:]:
        square = square + v * v
    factor = lax.rsqrt(jnp.sum(square, axis=1, keepdims=True) / total + EPS)
    factor_ref[...] = factor
    half = width // 2
    for j, v in enumerate(values):
        for p in range(2):
            start = p * (total // 2) + (me_ref[0] ^ j) * half
            cols = pl.ds(pl.multiple_of(start, half), half)
            normed_ref[:, cols] = (v[:, p * half : (p + 1) * half] * factor * gain_ref[:, cols]).astype(bf16)


def join_kernel(width, me_ref, *refs):
    pieces, out_ref = refs[:-1], refs[-1]
    half = width // 2
    for j, piece in enumerate(pieces):
        for p in range(2):
            start = p * len(pieces) * half + (me_ref[0] ^ j) * half
            out_ref[:, pl.ds(pl.multiple_of(start, half), half)] = piece[:, p * half : (p + 1) * half]


TILE = 512


def join_call(kernel, pieces, extra, outs, name):
    rows, width = pieces[0].shape
    me = lax.axis_index("col").astype(jnp.int32).reshape(1)
    return pl.pallas_call(
        functools.partial(kernel, width),
        grid_spec=pltpu.PrefetchScalarGridSpec(
            num_scalar_prefetch=1,
            grid=(rows // TILE,),
            in_specs=[pl.BlockSpec((TILE, width), lambda i, m: (i, 0))] * len(pieces)
            + [pl.BlockSpec(e.shape, lambda i, m: (0, 0)) for e in extra],
            out_specs=[pl.BlockSpec((TILE, o.shape[1]), lambda i, m: (i, 0)) for o in outs],
        ),
        out_shape=outs,
        compiler_params=pltpu.CompilerParams(vmem_limit_bytes=60 * 2**20),
        cost_estimate=FREE,
        name=name,
    )(me, *pieces, *extra)


def join_norm(pieces, gain):
    rows, width = pieces[0].shape
    outs = [jax.ShapeDtypeStruct((rows, width * len(pieces)), bf16), jax.ShapeDtypeStruct((rows, 1), f32)]
    return join_call(norm_kernel, pieces, [gain.reshape(1, -1)], outs, "join_norm")


def join(pieces):
    rows, width = pieces[0].shape
    return join_call(join_kernel, pieces, [], [jax.ShapeDtypeStruct((rows, width * len(pieces)), bf16)], "join")[0]


def dot(a, b, ca=1, cb=0):
    return lax.dot_general(a, b, (((ca,), (cb,)), ((), ())), preferred_element_type=f32)


FREE = pl.CostEstimate(flops=2**20, bytes_accessed=2**18, transcendentals=0)


def tile_call(kernel, arrays, specs, outs, out_specs, grid, name, me=None):
    params = dict(
        compiler_params=pltpu.CompilerParams(vmem_limit_bytes=48 * 2**20), cost_estimate=FREE, name=name
    )
    if me is None:
        return pl.pallas_call(kernel, grid=grid, in_specs=specs, out_specs=out_specs, out_shape=outs, **params)(*arrays)
    grid_spec = pltpu.PrefetchScalarGridSpec(
        num_scalar_prefetch=1, grid=grid, in_specs=specs, out_specs=out_specs
    )
    return pl.pallas_call(kernel, grid_spec=grid_spec, out_shape=outs, **params)(me, *arrays)


def row_tile(width):
    return pl.BlockSpec((TILE, width), lambda i, *_: (i, 0))


def half_tile(width, which):
    return pl.BlockSpec((TILE, width), lambda i, *_: (i, which))


def whole(shape):
    return pl.BlockSpec(shape, lambda i, *_: (0, 0))


def halves_kernel(count, *refs):
    out = refs[-1]
    total = dot(refs[0][...], refs[1][...])
    for i in range(1, count):
        total = total + dot(refs[2 * i][...], refs[2 * i + 1][...])
    out[...] = total.astype(out.dtype)


def halves(left, pairs, dtype=f32):
    rows, half, width = left.shape[0], left.shape[1] // 2, pairs[0][1].shape[1]
    arrays, specs = [], []
    for which, weight in pairs:
        arrays += [left, weight]
        specs += [half_tile(half, which), whole(weight.shape)]
    return tile_call(functools.partial(halves_kernel, len(pairs)), arrays, specs,
                     jax.ShapeDtypeStruct((rows, width), dtype), row_tile(width), (rows // TILE,), "halves")


def flat(ref):
    value = ref[...]
    return value.reshape(-1, value.shape[-1])


def weight_spec(w, p):
    if w.ndim == 2:
        return whole(w.shape)
    return pl.BlockSpec((w.shape[0], 1) + w.shape[2:], lambda i, *_: (0, p, 0, 0))


def block_spec(w, p, n, block):
    if w.ndim == 2:
        return pl.BlockSpec((block, w.shape[1]), lambda i, m: (m[n], 0))
    return pl.BlockSpec((block // w.shape[2], 1) + w.shape[2:], lambda i, m: (m[n], p, 0, 0))


def both(refs):
    return dot(refs[0][...], flat(refs[2])) + dot(refs[1][...], flat(refs[3]))


def hidden_kernel(*refs):
    gate_ref, up_ref, hidden_ref = refs[4:]
    up = both(refs)
    gate = gate_ref[...].astype(f32)
    up_ref[...] = up.astype(bf16)
    hidden_ref[...] = (gate * sigmoid(gate) * up).astype(bf16)


def both_specs(left, pair):
    half = left.shape[1] // 2
    return [left, left, *pair], [half_tile(half, 0), half_tile(half, 1), weight_spec(pair[0], 0), weight_spec(pair[1], 1)]


def hidden_call(left, pair, gate):
    rows, width = gate.shape
    tile = row_tile(width)
    arrays, specs = both_specs(left, pair)
    outs = [jax.ShapeDtypeStruct((rows, width), bf16)] * 2
    return tile_call(hidden_kernel, arrays + [gate], specs + [tile], outs, [tile, tile], (rows // TILE,), "hidden")


def cots_kernel(*refs):
    gate_ref, up_ref, gate_cot_ref, up_cot_ref, inner_ref = refs[4:]
    cot = both(refs)
    gate, up = gate_ref[...].astype(f32), up_ref[...].astype(f32)
    sig = sigmoid(gate)
    silu = gate * sig
    gate_cot = cot * up * (sig + silu * (1.0 - sig))
    up_cot = cot * silu
    gate_cot_ref[...] = gate_cot.astype(bf16)
    up_cot_ref[...] = up_cot.astype(bf16)
    inner_ref[...] = jnp.sum(gate_cot * gate + up_cot * up, axis=1, keepdims=True)


def cots_call(left, pair, gate, up):
    rows, width = gate.shape
    tile = row_tile(width)
    arrays, specs = both_specs(left, pair)
    outs = [jax.ShapeDtypeStruct((rows, width), bf16)] * 2 + [jax.ShapeDtypeStruct((rows, 1), f32)]
    return tile_call(cots_kernel, arrays + [gate, up], specs + [tile, tile], outs, [tile, tile, row_tile(1)],
                     (rows // TILE,), "cots")


def piece_kernel(count, pieces, has_got, me_ref, *refs):
    outs = refs[-pieces:]
    stride = 1 + 2 * pieces
    for n, out in enumerate(outs):
        width = out.shape[1] // 2
        for p in range(2):
            total = None
            for i in range(count):
                term = dot(refs[stride * i][...], flat(refs[stride * i + 1 + 2 * n + p]), 1, 1)
                total = term if total is None else total + term
            if has_got:
                total = total + refs[stride * count + n][:, p * width : (p + 1) * width].astype(f32)
            out[:, p * width : (p + 1) * width] = total.astype(out.dtype)


def piece_call(terms, block, js, gots, dtypes):
    rows = terms[0][0].shape[0]
    me = jnp.stack([lax.axis_index("col") ^ j for j in js]).astype(jnp.int32)
    arrays, specs = [], []
    for left, pair in terms:
        arrays.append(left)
        specs.append(row_tile(left.shape[1]))
        for n in range(len(js)):
            arrays += pair
            specs += [block_spec(w, p, n, block) for p, w in enumerate(pair)]
    has_got = gots[0] is not None
    if has_got:
        arrays += gots
        specs += [row_tile(2 * block)] * len(js)
    kernel = functools.partial(piece_kernel, len(terms), len(js), has_got)
    outs = [jax.ShapeDtypeStruct((rows, 2 * block), dtype) for dtype in dtypes]
    return tile_call(kernel, arrays, specs, outs, [row_tile(2 * block)] * len(js), (rows // TILE,), "piece", me)


def rows_kernel(parts, left_ref, right_ref, *refs):
    total = dot(left_ref[...], right_ref[...], 0, 0)
    gots, out = refs[:-1], refs[-1]
    if not gots:
        out[...] = total.astype(bf16)
    start = 0
    for got, part in zip(gots, parts):

        @pl.when((pl.program_id(0) >= start) & (pl.program_id(0) < start + part))
        def _(got=got):
            out[...] = (total + got[...].astype(f32)).astype(bf16)

        start += part


def rows_call(left, right, first, parts, tile, gots=(), width=None):
    rows, width, count = left.shape[0], width or right.shape[1], sum(parts)
    specs = [pl.BlockSpec((rows, tile), lambda i: (0, first + i)), whole((rows, width))]
    start = 0
    for _, part in zip(gots, parts):
        specs.append(pl.BlockSpec((tile, width), lambda i, s=start, p=part: (jnp.clip(i - s, 0, p - 1), 0)))
        start += part
    out = pl.BlockSpec((tile, width), lambda i: (i, 0))
    return tile_call(functools.partial(rows_kernel, parts), [left, right, *gots], specs,
                     jax.ShapeDtypeStruct((count * tile, width), bf16), out, (count,), "rows")


def parity_groups():
    n = lax.axis_size("row")
    return [list(range(p, n, 2)) for p in range(2)]


def after(x, *earlier):
    return lax.optimization_barrier((x,) + earlier)[0]


def gather_parity(shard):
    return lax.all_gather(shard, "row", axis=0, tiled=True, axis_index_groups=parity_groups())


def scatter_parity(part):
    return lax.psum_scatter(part, "row", scatter_dimension=0, tiled=True, axis_index_groups=parity_groups())


def all_rows(left, right):
    rows, tile, width = left.shape[0], left.shape[1] // 4, right.shape[1]
    odd = (lax.axis_index("row") & 1).astype(jnp.int32).reshape(1)

    def kernel(odd_ref, left_ref, right_ref, out_ref):
        out_ref[...] = dot(left_ref[...], right_ref[...], 0, 0).astype(bf16)

    return tile_call(kernel, [left, right], [pl.BlockSpec((rows, tile), lambda i, m: (0, i)), whole(right.shape)],
                     jax.ShapeDtypeStruct((4 * tile, width), bf16),
                     pl.BlockSpec((tile, width), lambda i, m: (2 * ((i // 2) ^ m[0]) + i % 2, 0)), (4,), "all_rows", odd)


def scatter_rows(part):
    even, odd = parity_groups()
    return lax.psum_scatter(part, "row", scatter_dimension=0, tiled=True, axis_index_groups=[even + odd])


def trade_rows(left, right, parts=(2,), width=None):
    tile = left.shape[1] // 2 // sum(parts)
    sent, first = [], sum(parts)
    for part in parts:
        sent.append(rows_call(left, right, first, (part,), tile, width=width))
        first += part
    return sent, [swap(part, "row", 1) for part in sent]


def got_width(gots):
    return gots[0].shape[1]


def own_rows(left, right, gots, *earlier):
    first = after(gots[0], *gots[1:], *earlier)
    tile = 512 if len(gots) == 1 else min(got.shape[0] for got in gots)
    parts = tuple(got.shape[0] // tile for got in gots)
    return rows_call(left, right, 0, parts, tile, [first, *gots[1:]], got_width(gots))


def flip(first, second):
    odd = (lax.axis_index("row") & 1) == 1
    return jnp.where(odd, second, first), jnp.where(odd, first, second)


def by_parity(x, chunk):
    lead, width = x.shape
    parts = x.reshape(lead, width // (2 * chunk), 2, chunk)
    first, second = flip(parts[:, :, 0], parts[:, :, 1])
    return jnp.concatenate([first.reshape(lead, width // 2), second.reshape(lead, width // 2)], 1)


def by_place(x, chunk):
    lead, width = x.shape
    shape = (lead, width // (2 * chunk), chunk)
    first, second = flip(x[:, : width // 2].reshape(shape), x[:, width // 2 :].reshape(shape))
    return jnp.stack([first, second], 2).reshape(lead, width)


def per_device(tokens, lengths, norm_in, q_weight, k_weight, v_weight, conv_q, conv_k, conv_v, beta_weight,
               head_gain, out_weight, norm_mid, gate_weight, up_weight, down_weight, cotangent):
    rows, width = tokens.shape
    dh = head_gain.shape[0]
    hd = q_weight.shape[1]
    heads = hd // dh
    ff = gate_weight.shape[1]
    col = lax.axis_index("col")
    feat = lax.axis_size("col") * width
    live = live_column(lengths[0], rows)
    live_low = live.astype(bf16)
    beta_pad = jnp.pad(beta_weight, ((0, 0), (0, 128 - beta_weight.shape[1])))
    in_mine = gather_parity(jnp.concatenate([q_weight, k_weight, v_weight, beta_pad], 1))
    out_mine = gather_parity(out_weight.T)
    gate_mine = gather_parity(gate_weight)
    up_mine = gather_parity(up_weight)
    down_turned = down_weight.T
    down_side = swap(down_turned, "row", 1)
    down_both = with_layout_constraint(jnp.concatenate([down_turned, down_side], 0), Layout((0, 1)))
    down_rows = with_layout_constraint(gather_parity(down_both), Layout((0, 1))).reshape(-1, 2, *down_turned.shape)
    conv = jnp.concatenate([conv_q, conv_k, conv_v], 1)
    gain = head_gain.reshape(1, dh)
    gain_in = lax.dynamic_slice_in_dim(norm_in, col * width, width)
    gain_mid = lax.dynamic_slice_in_dim(norm_mid, col * width, width)
    chunk = q_weight.shape[0]
    tokens, cotangent = by_parity(tokens, chunk), by_parity(cotangent, chunk)
    gain_in, gain_mid = by_parity(gain_in[None], chunk), by_parity(gain_mid[None], chunk)
    norm_in, norm_mid = by_parity(norm_in[None], chunk), by_parity(norm_mid[None], chunk)
    tokens32 = tokens.astype(f32)

    block = width // 2

    half = feat // 2
    normed, factor_in = join_norm(spread_cols(tokens), norm_in)
    ffn_cot = join(spread_cols(after(cotangent * live_low, down_side)))
    in_mine = after(in_mine, normed, ffn_cot)
    in_other, out_other = swap(in_mine, "row", 1), swap(out_mine, "row", 1)
    proj = halves(after(normed, out_mine), [(0, in_mine), (1, in_other)])
    gate_mine = after(gate_mine, proj)
    gate_other = swap(gate_mine, "row", 1)
    proj = after(proj, gate_mine)
    out_other = after(out_other, proj)
    w_in, w_out = (in_mine, in_other), (out_mine, out_other)
    mixed, *kept = mixer_forward(proj, conv, gain, heads, dh)
    branch = ColSum([(mixed, w_out)], block)
    sent = branch.send(1)
    sent = branch.send_last(*sent)
    up_mine = after(up_mine, *sent)
    up_other = swap(up_mine, "row", 1)
    middle = tokens32 + live * after(branch.total(), gate_other)
    mid_low = middle.astype(bf16)
    normed_mid, factor_mid = join_norm(spread_cols(mid_low), after(norm_mid, up_mine))
    w_gate, w_up = (gate_mine, gate_other), (up_mine, up_other)
    gate = halves(normed_mid, [(0, gate_mine), (1, gate_other)], bf16)
    up, hidden = hidden_call(after(normed_mid, gate), w_up, gate)
    down_sent = all_rows(ffn_cot, hidden)
    grad_down = scatter_rows(down_sent)
    w_down = (after(down_rows, down_sent),) * 2
    gate_cot, up_cot, inner_mid = cots_call(ffn_cot, w_down, gate, up)
    inner_mid = sum_all(inner_mid.reshape(rows // 128, 128), "col").reshape(rows, 1) / factor_mid
    mid_sum = ColSum([(gate_cot, w_gate), (up_cot, w_up)], block)
    sent = mid_sum.send(1)
    gate_sent, gate_got = trade_rows(after(normed_mid, *sent), gate_cot)
    mid_sum.send_last(inner_mid, gate_sent[0])
    up_sent, up_got = trade_rows(after(normed_mid, mid_sum.base), up_cot)
    mid_sum.got[0] = after(mid_sum.got[0], *up_sent)
    mid_cot = mid_sum.total()

    mid32 = mid_low.astype(f32)
    gmid_part = jnp.sum(mid_cot * mid32 * factor_mid, axis=0)
    middle_cot = cotangent.astype(f32) + factor_mid * gain_mid * mid_cot - mid32 * (factor_mid**3 * inner_mid / feat)
    branch_low = (live * middle_cot).astype(bf16)
    pieces = spread_cols(branch_low)
    gate_rows = own_rows(normed_mid, gate_cot, gate_got, pieces[2])
    grad_gate = scatter_parity(gate_rows)
    branch_cot = join(pieces)
    mixed_cot = halves(branch_cot, [(0, out_mine), (1, out_other)])
    out_sent, out_got = trade_rows(after(branch_cot, mixed_cot), mixed)
    mixed_cot = after(mixed_cot, *out_sent)
    low, gconv, ghead, inner_in = mixer_backward(proj, conv, gain, mixed_cot, kept, heads, dh)
    in_sum = ColSum([(low, w_in)], block)
    sent = in_sum.send(1)
    low_sent, low_got = trade_rows(after(normed, *sent), low, width=3 * hd)
    beta_part = by_place(dot(low[:, 3 * hd :], after(normed, *low_sent), 0, 0)[: beta_weight.shape[1]], chunk)
    inner_in = sum_all(inner_in.reshape(rows // 128, 128), "col").reshape(rows, 1) / factor_in
    in_sum.send_last(inner_in, *low_sent)
    up_rows = own_rows(normed_mid, up_cot, up_got, *out_got, in_sum.base, grad_down)
    grad_up = scatter_parity(up_rows)
    out_rows = own_rows(branch_cot, mixed, out_got, grad_gate, up_rows)
    grad_out = scatter_parity(out_rows)
    in_cot = in_sum.total()
    gin_part = jnp.sum(in_cot * tokens32 * factor_in, axis=0)
    grad_tokens = middle_cot + factor_in * gain_in * in_cot - tokens32 * (factor_in**3 * inner_in / feat)

    def own_cols(part):
        part = by_place(part[None], chunk)[0]
        return lax.dynamic_update_slice_in_dim(jnp.zeros((feat,), f32), part, col * width, 0)

    sizes = [feat, feat, dh]
    wide = sum_all(jnp.concatenate([own_cols(gin_part), own_cols(gmid_part), ghead[0]]).reshape(-1, 128), "col")
    small = jnp.concatenate([wide, gconv.reshape(-1, 128), beta_part.reshape(-1, 128)], 0)
    bits = bits_down(lax.axis_size("row"))
    for bit in bits[:-1]:
        small = small + swap(small, "row", bit)
    low_rows = own_rows(normed, low, low_got, out_rows, grad_up, small, grad_tokens)
    grad_low = scatter_parity(low_rows)
    in_cot = in_sum.total()
    gin_part = jnp.sum(in_cot * tokens32 * factor_in, axis=0)
    grad_tokens = middle_cot + factor_in * gain_in * in_cot - tokens32 * (factor_in**3 * inner_in / feat)

    def own_cols(part):
        part = by_place(part[None], chunk)[0]
        return lax.dynamic_update_slice_in_dim(jnp.zeros((feat,), f32), part, col * width, 0)

    sizes = [feat, feat, dh]
    wide = sum_all(jnp.concatenate([own_cols(gin_part), own_cols(gmid_part), ghead[0]]).reshape(-1, 128), "col")
    small = jnp.concatenate([wide, gconv.reshape(-1, 128), beta_part.reshape(-1, 128)], 0)
    bits = bits_down(lax.axis_size("row"))
    for bit in bits[:-1]:
        small = small + swap(small, "row", bit)
    low_rows = own_rows(normed, low, low_got, out_rows, grad_up, small, grad_tokens)
    grad_low = scatter_parity(low_rows)
    result = ColSum([(hidden, w_down)], block)
    sent = result.send(1, low_rows)
    result.send_last(*sent)
    layer_out = (middle + live * result.total()).astype(bf16)
    small = small + swap(small, "row", bits[-1])
    cuts = [wide.shape[0], wide.shape[0] + gconv.size // 128]
    wide, gconv = small[: cuts[0]].reshape(-1), small[cuts[0] : cuts[1]].reshape(gconv.shape)
    beta_sum = small[cuts[1] :].reshape(beta_part.shape)
    grad_beta = lax.dynamic_slice_in_dim(beta_sum, lax.axis_index("row") * chunk, chunk, 1).T
    g_low = grad_low.astype(f32)
    return (
        by_place(layer_out, chunk),
        by_place(grad_tokens, chunk),
        wide[:feat],
        g_low[:, :hd],
        g_low[:, hd : 2 * hd],
        g_low[:, 2 * hd : 3 * hd],
        gconv[:, :hd],
        gconv[:, hd : 2 * hd],
        gconv[:, 2 * hd :],
        grad_beta,
        wide[2 * feat :],
        grad_out.astype(f32).T,
        wide[feat : 2 * feat],
        grad_gate.astype(f32),
        grad_up.astype(f32),
        grad_down.astype(f32).T,
    )


def solution(mesh):
    split_both, features, turned = P("row", "col"), P(None, "col"), P("col", "row")
    return jax.shard_map(
        per_device,
        mesh=mesh,
        in_specs=(split_both, P("row"), P(), split_both, split_both, split_both, features, features, features,
                  split_both, P(), turned, P(), split_both, split_both, turned, split_both),
        out_specs=(split_both, split_both, P(), split_both, split_both, split_both, features, features, features,
                   split_both, P(), turned, P(), split_both, split_both, turned),
        check_vma=False,
    )
```

```python
import functools
import jax
import jax.numpy as jnp
from jax import lax
from jax.experimental import pallas as pl
from jax.experimental.pallas import tpu as pltpu
from jax.sharding import PartitionSpec as P
from jax.experimental.layout import Layout, with_layout_constraint

CHUNK = 128
EPS = 1e-6
FREE = pl.CostEstimate(flops=2**20, bytes_accessed=2**18, transcendentals=0)
bf16 = jnp.bfloat16
f32 = jnp.float32


def split(x):
    high = x.astype(bf16)
    return high, (x - high.astype(f32)).astype(bf16)


def mm(a, b, ca=1, cb=0):
    def dg(u, v):
        return lax.dot_general(u, v, (((ca,), (cb,)), ((), ())), preferred_element_type=f32)

    return dg(a[0], b[0]) + (dg(a[0], b[1]) + dg(a[1], b[0]))


def sigmoid(x):
    return 0.5 * jnp.tanh(0.5 * x) + 0.5


def masks(n):
    r = lax.broadcasted_iota(jnp.int32, (n, n), 0)
    c = lax.broadcasted_iota(jnp.int32, (n, n), 1)
    return r, c


def unit_lower_inverse(lows, r, c):
    n = lows[0].shape[0]
    eye = jnp.where(r == c, 1.0, 0.0)
    invs = [eye - jnp.where(r // 2 == c // 2, low, 0.0) for low in lows]
    size = 2
    while size < n:
        mask = (r // (2 * size) == c // (2 * size)) & (r // size != c // size)
        offs = [split(jnp.where(mask, low, 0.0)) for low in lows]
        parts = [split(inv) for inv in invs]
        right = [split(mm(off, part)) for off, part in zip(offs, parts)]
        invs = [inv - mm(part, x) for inv, part, x in zip(invs, parts, right)]
        size *= 2
    return invs


def conv_rows(padded, taps, first):
    out = taps[0:1] * padded[first : first + CHUNK]
    for j in range(1, 4):
        out = out + taps[j : j + 1] * padded[first + j : first + j + CHUNK]
    return out


def fwd_kernel(heads, dh, x_ref, conv_ref, gain_ref, mixed_ref, o_ref, n_ref, t_ref, s_ref, state, halo):
    hd = heads * dh

    @pl.when(pl.program_id(0) == 0)
    def _():
        state[...] = jnp.zeros_like(state)
        halo[...] = jnp.zeros_like(halo)

    r, c = masks(CHUNK)
    each = range(heads)
    acts = []
    for p in range(3):
        for h in each:
            cols = slice(p * hd + h * dh, p * hd + (h + 1) * dh)
            y = conv_rows(jnp.concatenate([halo[:, cols], x_ref[:, cols]], 0), conv_ref[:, cols], 5)
            acts.append(y * sigmoid(y))
    qs = [split(acts[h] * dh ** -0.5) for h in each]
    ks = []
    for h in each:
        k = acts[heads + h]
        ks.append(split(k * lax.rsqrt(jnp.sum(k * k, axis=1, keepdims=True) + EPS)))
    b = [sigmoid(x_ref[:, 3 * hd + h : 3 * hd + h + 1]) for h in each]
    lows = [jnp.where(r > c, b[h] * mm(ks[h], ks[h], 1, 1), 0.0) for h in each]
    invs = unit_lower_inverse(lows, r, c)
    scores = [split(jnp.where(r >= c, mm(qs[h], ks[h], 1, 1), 0.0)) for h in each]
    s = [state[h] for h in each]
    ss = [split(s[h]) for h in each]
    right = [split(b[h] * (acts[2 * heads + h] - mm(ks[h], ss[h]))) for h in each]
    fresh = [mm(split(invs[h]), right[h]) for h in each]
    fs = [split(fresh[h]) for h in each]
    outs = [mm(qs[h], ss[h]) + mm(scores[h], fs[h]) for h in each]
    for h in each:
        state[h] = s[h] + mm(ks[h], fs[h], 0, 0)
        cols = slice(h * dh, (h + 1) * dh)
        s_ref[0, h] = s[h]
        t_ref[0, h] = invs[h]
        n_ref[:, cols] = fresh[h]
        o = outs[h]
        o_ref[:, cols] = o
        norm = lax.rsqrt(jnp.mean(o * o, axis=1, keepdims=True) + EPS)
        mixed_ref[:, cols] = (o * norm * gain_ref[...]).astype(bf16)
    halo[...] = x_ref[CHUNK - 8 :, : 3 * hd]


def bwd_kernel(heads, dh, x_ref, prev_ref, conv_ref, gain_ref, m_ref, o_ref, n_ref, t_ref, s_ref,
               low_ref, gconv_ref, ggain_ref, inner_ref, dstate, ghead):
    hd = heads * dh
    step = pl.program_id(0)

    @pl.when(step == 0)
    def _():
        dstate[...] = jnp.zeros_like(dstate)
        ghead[...] = jnp.zeros_like(ghead)
        gconv_ref[...] = jnp.zeros_like(gconv_ref)
        ggain_ref[...] = jnp.zeros_like(ggain_ref)

    has_prev = jnp.where(step == pl.num_programs(0) - 1, 0.0, 1.0)
    r, c = masks(CHUNK)
    lane = lax.broadcasted_iota(jnp.int32, (CHUNK, 128), 1)
    each = range(heads)
    scale = dh ** -0.5
    cuts = [slice(h * dh, (h + 1) * dh) for h in each]
    ys, sigs = [], []
    for p in range(3):
        for h in each:
            cols = slice(p * hd + h * dh, p * hd + (h + 1) * dh)
            padded = jnp.concatenate([prev_ref[:, cols] * has_prev, x_ref[:, cols]], 0)
            y = conv_rows(padded, conv_ref[:, cols], 5)
            ys.append(y)
            sigs.append(sigmoid(y))
    qs = [split(ys[h] * sigs[h] * scale) for h in each]
    kr = [ys[heads + h] * sigs[heads + h] for h in each]
    kinv = [lax.rsqrt(jnp.sum(kr[h] * kr[h], axis=1, keepdims=True) + EPS) for h in each]
    ks = [split(kr[h] * kinv[h]) for h in each]
    b = [sigmoid(x_ref[:, 3 * hd + h : 3 * hd + h + 1]) for h in each]
    dos = []
    ggain = jnp.zeros((1, dh), f32)
    for h in each:
        o = o_ref[:, cuts[h]]
        mc = m_ref[:, cuts[h]]
        norm = lax.rsqrt(jnp.mean(o * o, axis=1, keepdims=True) + EPS)
        ggain = ggain + jnp.sum(mc * (o * norm), axis=0, keepdims=True)
        dn_ = mc * gain_ref[...]
        do = norm * dn_ - o * (norm * norm * norm * jnp.mean(dn_ * o, axis=1, keepdims=True))
        dos.append(split(do))
    scores = [split(jnp.where(r >= c, mm(qs[h], ks[h], 1, 1), 0.0)) for h in each]
    part = [mm(scores[h], dos[h], 0, 0) for h in each]
    d = [dstate[h] for h in each]
    ds = [split(d[h]) for h in each]
    dfresh = [split(part[h] + mm(ks[h], ds[h])) for h in each]
    db_ = [mm(split(t_ref[0, h]), dfresh[h], 0, 0) for h in each]
    dr = [b[h] * db_[h] for h in each]
    drs = [split(dr[h]) for h in each]
    for h in each:
        dstate[h] = d[h] + (mm(qs[h], dos[h], 0, 0) - mm(ks[h], drs[h], 0, 0))
    ss = [split(s_ref[0, h]) for h in each]
    fs = [split(n_ref[:, cuts[h]]) for h in each]
    resid = [ys[2 * heads + h] * sigs[2 * heads + h] - mm(ks[h], ss[h]) for h in each]
    gram = [mm(ks[h], ks[h], 1, 1) for h in each]
    da = [jnp.where(r > c, -mm(split(db_[h]), fs[h], 1, 1), 0.0) for h in each]
    dsc = [split(jnp.where(r >= c, mm(dos[h], fs[h], 1, 1), 0.0)) for h in each]
    dq = [mm(dos[h], ss[h], 1, 1) + mm(dsc[h], ks[h]) for h in each]
    dgs = [split(b[h] * da[h]) for h in each]
    dk = [mm(dsc[h], qs[h], 0, 0) + mm(fs[h], ds[h], 1, 1) for h in each]
    dk = [dk[h] - mm(drs[h], ss[h], 1, 1) for h in each]
    dk = [dk[h] + (mm(dgs[h], ks[h]) + mm(dgs[h], ks[h], 0, 0)) for h in each]
    beta_low = jnp.zeros((CHUNK, 128), f32)
    inner = jnp.zeros((CHUNK, dh), f32)
    for h in each:
        dbeta = jnp.sum(db_[h] * resid[h], axis=1, keepdims=True) + jnp.sum(da[h] * gram[h], axis=1, keepdims=True)
        beta_low = jnp.where(lane == h, dbeta * b[h] * (1.0 - b[h]), beta_low)
    dkr = [kinv[h] * dk[h] - kr[h] * (kinv[h] * kinv[h] * kinv[h] * jnp.sum(dk[h] * kr[h], axis=1, keepdims=True)) for h in each]
    cots = [dq[h] * scale for h in each] + dkr + dr
    for p in range(3):
        for h in each:
            i = p * heads + h
            cols = slice(p * hd + h * dh, p * hd + (h + 1) * dh)
            g = cots[i] * sigs[i] * (1.0 + ys[i] * (1.0 - sigs[i]))
            taps = conv_ref[:, cols]
            gp = jnp.concatenate([g, ghead[:, cols]], 0)
            padded = jnp.concatenate([prev_ref[:, cols] * has_prev, x_ref[:, cols]], 0)
            out = taps[3:4] * g
            for j in range(3):
                out = out + taps[j : j + 1] * gp[3 - j : 3 - j + CHUNK]
            low_ref[:, cols] = out.astype(bf16)
            inner = inner + out * x_ref[:, cols]
            for j in range(4):
                gconv_ref[j : j + 1, cols] += jnp.sum(g * padded[5 + j : 5 + j + CHUNK], axis=0, keepdims=True)
            ghead[:, cols] = g[0:8]
    low_ref[:, 3 * hd :] = beta_low.astype(bf16)
    inner = inner + beta_low * x_ref[:, 3 * hd :]
    inner_ref[...] = jnp.sum(inner, axis=1, keepdims=True)
    ggain_ref[...] += ggain


def mixer_forward(proj, conv, gain, heads, dh):
    rows, width = proj.shape
    hd = heads * dh
    steps = rows // CHUNK
    square = pl.BlockSpec((1, heads, dh, dh), lambda i: (i, 0, 0, 0))
    wide = pl.BlockSpec((CHUNK, hd), lambda i: (i, 0))
    return pl.pallas_call(
        functools.partial(fwd_kernel, heads, dh),
        grid=(steps,),
        in_specs=[
            pl.BlockSpec((CHUNK, width), lambda i: (i, 0)),
            pl.BlockSpec((4, 3 * hd), lambda i: (0, 0)),
            pl.BlockSpec((1, dh), lambda i: (0, 0)),
        ],
        out_specs=[wide, wide, wide, pl.BlockSpec((1, heads, CHUNK, CHUNK), lambda i: (i, 0, 0, 0)), square],
        out_shape=[
            jax.ShapeDtypeStruct((rows, hd), bf16),
            jax.ShapeDtypeStruct((rows, hd), f32),
            jax.ShapeDtypeStruct((rows, hd), f32),
            jax.ShapeDtypeStruct((steps, heads, CHUNK, CHUNK), f32),
            jax.ShapeDtypeStruct((steps, heads, dh, dh), f32),
        ],
        scratch_shapes=[pltpu.VMEM((heads, dh, dh), f32), pltpu.VMEM((8, 3 * hd), f32)],
        compiler_params=pltpu.CompilerParams(vmem_limit_bytes=60 * 2**20),
        cost_estimate=FREE,
        name="mixer_forward",
    )(proj, conv, gain)


def mixer_backward(proj, conv, gain, mixed_cot, kept, heads, dh):
    o, fresh, inv, states = kept
    rows, width = proj.shape
    hd = heads * dh
    steps = rows // CHUNK
    last = steps - 1
    per = CHUNK // 8
    square = pl.BlockSpec((1, heads, dh, dh), lambda i: (last - i, 0, 0, 0))
    wide = pl.BlockSpec((CHUNK, hd), lambda i: (last - i, 0))
    return pl.pallas_call(
        functools.partial(bwd_kernel, heads, dh),
        grid=(steps,),
        in_specs=[
            pl.BlockSpec((CHUNK, width), lambda i: (last - i, 0)),
            pl.BlockSpec((8, width), lambda i: (jnp.maximum((last - i) * per - 1, 0), 0)),
            pl.BlockSpec((4, 3 * hd), lambda i: (0, 0)),
            pl.BlockSpec((1, dh), lambda i: (0, 0)),
            wide, wide, wide,
            pl.BlockSpec((1, heads, CHUNK, CHUNK), lambda i: (last - i, 0, 0, 0)),
            square,
        ],
        out_specs=[
            pl.BlockSpec((CHUNK, width), lambda i: (last - i, 0)),
            pl.BlockSpec((4, 3 * hd), lambda i: (0, 0)),
            pl.BlockSpec((1, dh), lambda i: (0, 0)),
            pl.BlockSpec((CHUNK, 1), lambda i: (last - i, 0)),
        ],
        out_shape=[
            jax.ShapeDtypeStruct((rows, width), bf16),
            jax.ShapeDtypeStruct((4, 3 * hd), f32),
            jax.ShapeDtypeStruct((1, dh), f32),
            jax.ShapeDtypeStruct((rows, 1), f32),
        ],
        scratch_shapes=[pltpu.VMEM((heads, dh, dh), f32), pltpu.VMEM((8, 3 * hd), f32)],
        compiler_params=pltpu.CompilerParams(vmem_limit_bytes=60 * 2**20),
        cost_estimate=FREE,
        name="mixer_backward",
    )(proj, proj, conv, gain, mixed_cot, o, fresh, inv, states)


def live_column(length, rows):
    return (lax.broadcasted_iota(jnp.int32, (rows, 1), 0) < length).astype(f32)


def swap(x, axis, bit):
    n = lax.axis_size(axis)
    return lax.ppermute(x, axis, [(i, i ^ bit) for i in range(n)])


def bits_down(n):
    bits = []
    while n > 1:
        n //= 2
        bits.append(n)
    return bits


def sum_all(x, axis):
    for bit in bits_down(lax.axis_size(axis)):
        x = x + swap(x, axis, bit)
    return x


def spread_cols(shard):
    n = lax.axis_size("col")
    pieces = {0: shard}
    for bit in bits_down(n):
        for j in list(pieces):
            pieces[j | bit] = swap(pieces[j], "col", bit)
    return [pieces[j] for j in range(n)]


class ColSum:
    def __init__(self, terms, block):
        self.terms, self.block = terms, block
        self.kept, self.got = list(range(lax.axis_size("col"))), {}

    def pieces(self, js, dtypes, earlier):
        (left, *pair), rest = self.terms[0], self.terms[1:]
        gots = [self.got.pop(j, None) for j in js]
        return piece_call([(after(left, *earlier), *pair)] + rest, self.block, js, gots, dtypes)

    def send(self, bit, *earlier):
        js = [j for j in self.kept if j & bit]
        last = bit > 1 and 2 * bit == lax.axis_size("col")
        sent = list(self.pieces(js + [0] * last, [bf16] * len(js) + [f32] * last, earlier))
        if last:
            self.base = sent.pop()
        for j, low in zip(js, sent):
            got, base = swap(low, "col", bit), j ^ bit
            self.got[base] = got if base not in self.got else self.got[base].astype(f32) + got.astype(f32)
        self.kept = [j for j in self.kept if not j & bit]
        return sent

    def send_last(self, *earlier):
        bit = 2
        while bit < lax.axis_size("col"):
            earlier = self.send(bit, *earlier)
            bit *= 2
        return earlier

    def total(self):
        return self.base + self.got[0].astype(f32)


def norm_kernel(width, me_ref, *refs):
    pieces, (gain_ref, normed_ref, factor_ref) = refs[:-3], refs[-3:]
    total = len(pieces) * width
    values = [p[...].astype(f32) for p in pieces]
    square = values[0] * values[0]
    for v in values[1:]:
        square = square + v * v
    factor = lax.rsqrt(jnp.sum(square, axis=1, keepdims=True) / total + EPS)
    factor_ref[...] = factor
    half = width // 2
    for j, v in enumerate(values):
        for p in range(2):
            start = p * (total // 2) + (me_ref[0] ^ j) * half
            cols = pl.ds(pl.multiple_of(start, half), half)
            normed_ref[:, cols] = (v[:, p * half : (p + 1) * half] * factor * gain_ref[:, cols]).astype(bf16)


def join_kernel(width, me_ref, *refs):
    pieces, out_ref = refs[:-1], refs[-1]
    half = width // 2
    for j, piece in enumerate(pieces):
        for p in range(2):
            start = p * len(pieces) * half + (me_ref[0] ^ j) * half
            out_ref[:, pl.ds(pl.multiple_of(start, half), half)] = piece[:, p * half : (p + 1) * half]


TILE = 512


def join_call(kernel, pieces, extra, outs, name):
    rows, width = pieces[0].shape
    me = lax.axis_index("col").astype(jnp.int32).reshape(1)
    return pl.pallas_call(
        functools.partial(kernel, width),
        grid_spec=pltpu.PrefetchScalarGridSpec(
            num_scalar_prefetch=1,
            grid=(rows // TILE,),
            in_specs=[pl.BlockSpec((TILE, width), lambda i, m: (i, 0))] * len(pieces)
            + [pl.BlockSpec(e.shape, lambda i, m: (0, 0)) for e in extra],
            out_specs=[pl.BlockSpec((TILE, o.shape[1]), lambda i, m: (i, 0)) for o in outs],
        ),
        out_shape=outs,
        compiler_params=pltpu.CompilerParams(vmem_limit_bytes=60 * 2**20),
        cost_estimate=FREE,
        name=name,
    )(me, *pieces, *extra)


def join_norm(pieces, gain):
    rows, width = pieces[0].shape
    outs = [jax.ShapeDtypeStruct((rows, width * len(pieces)), bf16), jax.ShapeDtypeStruct((rows, 1), f32)]
    return join_call(norm_kernel, pieces, [gain.reshape(1, -1)], outs, "join_norm")


def join(pieces):
    rows, width = pieces[0].shape
    return join_call(join_kernel, pieces, [], [jax.ShapeDtypeStruct((rows, width * len(pieces)), bf16)], "join")[0]


def dot(a, b, ca=1, cb=0):
    return lax.dot_general(a, b, (((ca,), (cb,)), ((), ())), preferred_element_type=f32)


FREE = pl.CostEstimate(flops=2**20, bytes_accessed=2**18, transcendentals=0)


def tile_call(kernel, arrays, specs, outs, out_specs, grid, name, me=None):
    params = dict(
        compiler_params=pltpu.CompilerParams(vmem_limit_bytes=48 * 2**20), cost_estimate=FREE, name=name
    )
    if me is None:
        return pl.pallas_call(kernel, grid=grid, in_specs=specs, out_specs=out_specs, out_shape=outs, **params)(*arrays)
    grid_spec = pltpu.PrefetchScalarGridSpec(
        num_scalar_prefetch=1, grid=grid, in_specs=specs, out_specs=out_specs
    )
    return pl.pallas_call(kernel, grid_spec=grid_spec, out_shape=outs, **params)(me, *arrays)


def row_tile(width):
    return pl.BlockSpec((TILE, width), lambda i, *_: (i, 0))


def half_tile(width, which):
    return pl.BlockSpec((TILE, width), lambda i, *_: (i, which))


def whole(shape):
    return pl.BlockSpec(shape, lambda i, *_: (0, 0))


def halves_kernel(count, *refs):
    out = refs[-1]
    total = dot(refs[0][...], refs[1][...])
    for i in range(1, count):
        total = total + dot(refs[2 * i][...], refs[2 * i + 1][...])
    out[...] = total.astype(out.dtype)


def halves(left, pairs, dtype=f32):
    rows, half, width = left.shape[0], left.shape[1] // 2, pairs[0][1].shape[1]
    arrays, specs = [], []
    for which, weight in pairs:
        arrays += [left, weight]
        specs += [half_tile(half, which), whole(weight.shape)]
    return tile_call(functools.partial(halves_kernel, len(pairs)), arrays, specs,
                     jax.ShapeDtypeStruct((rows, width), dtype), row_tile(width), (rows // TILE,), "halves")


def flat(ref):
    value = ref[...]
    return value.reshape(-1, value.shape[-1])


def weight_spec(w, p):
    if w.ndim == 2:
        return whole(w.shape)
    return pl.BlockSpec((w.shape[0], 1) + w.shape[2:], lambda i, *_: (0, p, 0, 0))


def block_spec(w, p, n, block):
    if w.ndim == 2:
        return pl.BlockSpec((block, w.shape[1]), lambda i, m: (m[n], 0))
    return pl.BlockSpec((block // w.shape[2], 1) + w.shape[2:], lambda i, m: (m[n], p, 0, 0))


def both(refs):
    return dot(refs[0][...], flat(refs[2])) + dot(refs[1][...], flat(refs[3]))


def proj_kernel(*refs):
    cut = refs[2].shape[1]
    for start, first in ((0, 2), (cut, 4)):
        total = dot(refs[0][...], refs[first][...]) + dot(refs[1][...], refs[first + 1][...])
        refs[6][:, start : start + total.shape[1]] = total


def proj_call(left, pair, narrow):
    rows, half, width = left.shape[0], left.shape[1] // 2, pair[0].shape[1] + narrow[0].shape[1]
    arrays = [left, left, *pair, *narrow]
    specs = [half_tile(half, 0), half_tile(half, 1)] + [whole(a.shape) for a in arrays[2:]]
    return tile_call(proj_kernel, arrays, specs, jax.ShapeDtypeStruct((rows, width), f32), row_tile(width),
                     (rows // TILE,), "proj")


def gather_narrow(shard):
    n, row = lax.axis_size("row"), lax.axis_index("row")
    rows, width = shard.shape
    stack = shard.T[None]
    for bit in reversed(bits_down(n)):
        stack = jnp.concatenate([stack, swap(stack, "row", bit)], 0)
    for bit in bits_down(n):
        parts = stack.reshape(n // (2 * bit), 2, bit, width, rows)
        parts = jnp.where((row & bit) != 0, parts[:, ::-1], parts)
        stack = parts.reshape(n, width, rows)
    parts = stack.reshape(n // 2, 2, width, rows).transpose(1, 0, 3, 2).reshape(2, -1, width)
    return flip(*jnp.pad(parts, ((0, 0), (0, 0), (0, 128 - width))))


def hidden_kernel(*refs):
    gate_ref, up_ref, hidden_ref = refs[4:]
    up = both(refs)
    gate = gate_ref[...].astype(f32)
    up_ref[...] = up.astype(bf16)
    hidden_ref[...] = (gate * sigmoid(gate) * up).astype(bf16)


def both_specs(left, pair):
    half = left.shape[1] // 2
    return [left, left, *pair], [half_tile(half, 0), half_tile(half, 1), weight_spec(pair[0], 0), weight_spec(pair[1], 1)]


def hidden_call(left, pair, gate):
    rows, width = gate.shape
    tile = row_tile(width)
    arrays, specs = both_specs(left, pair)
    outs = [jax.ShapeDtypeStruct((rows, width), bf16)] * 2
    return tile_call(hidden_kernel, arrays + [gate], specs + [tile], outs, [tile, tile], (rows // TILE,), "hidden")


def cots_kernel(*refs):
    gate_ref, up_ref, gate_cot_ref, up_cot_ref, inner_ref = refs[4:]
    cot = both(refs)
    gate, up = gate_ref[...].astype(f32), up_ref[...].astype(f32)
    sig = sigmoid(gate)
    silu = gate * sig
    gate_cot = cot * up * (sig + silu * (1.0 - sig))
    up_cot = cot * silu
    gate_cot_ref[...] = gate_cot.astype(bf16)
    up_cot_ref[...] = up_cot.astype(bf16)
    inner_ref[...] = jnp.sum(gate_cot * gate + up_cot * up, axis=1, keepdims=True)


def cots_call(left, pair, gate, up):
    rows, width = gate.shape
    tile = row_tile(width)
    arrays, specs = both_specs(left, pair)
    outs = [jax.ShapeDtypeStruct((rows, width), bf16)] * 2 + [jax.ShapeDtypeStruct((rows, 1), f32)]
    return tile_call(cots_kernel, arrays + [gate, up], specs + [tile, tile], outs, [tile, tile, row_tile(1)],
                     (rows // TILE,), "cots")


def piece_kernel(count, pieces, has_got, me_ref, *refs):
    outs = refs[-pieces:]
    stride = 1 + 2 * pieces
    for n, out in enumerate(outs):
        width = out.shape[1] // 2
        for p in range(2):
            total = None
            for i in range(count):
                term = dot(refs[stride * i][...], flat(refs[stride * i + 1 + 2 * n + p]), 1, 1)
                total = term if total is None else total + term
            if has_got:
                total = total + refs[stride * count + n][:, p * width : (p + 1) * width].astype(f32)
            out[:, p * width : (p + 1) * width] = total.astype(out.dtype)


def piece_call(terms, block, js, gots, dtypes):
    rows = terms[0][0].shape[0]
    me = jnp.stack([lax.axis_index("col") ^ j for j in js]).astype(jnp.int32)
    arrays, specs = [], []
    for left, pair, *place in terms:
        arrays.append(left)
        specs.append(half_tile(pair[0].shape[-1], place[0] if place else 0))
        for n in range(len(js)):
            arrays += pair
            specs += [block_spec(w, p, n, block) for p, w in enumerate(pair)]
    has_got = gots[0] is not None
    if has_got:
        arrays += gots
        specs += [row_tile(2 * block)] * len(js)
    kernel = functools.partial(piece_kernel, len(terms), len(js), has_got)
    outs = [jax.ShapeDtypeStruct((rows, 2 * block), dtype) for dtype in dtypes]
    return tile_call(kernel, arrays, specs, outs, [row_tile(2 * block)] * len(js), (rows // TILE,), "piece", me)


def rows_kernel(parts, left_ref, right_ref, *refs):
    total = dot(left_ref[...], right_ref[...], 0, 0)
    gots, out = refs[:-1], refs[-1]
    if not gots:
        out[...] = total.astype(bf16)
    start = 0
    for got, part in zip(gots, parts):

        @pl.when((pl.program_id(0) >= start) & (pl.program_id(0) < start + part))
        def _(got=got):
            out[...] = (total + got[...].astype(f32)).astype(bf16)

        start += part


def rows_call(left, right, first, parts, tile, gots=(), width=None):
    rows, width, count = left.shape[0], width or right.shape[1], sum(parts)
    specs = [pl.BlockSpec((rows, tile), lambda i: (0, first + i)), whole((rows, width))]
    start = 0
    for _, part in zip(gots, parts):
        specs.append(pl.BlockSpec((tile, width), lambda i, s=start, p=part: (jnp.clip(i - s, 0, p - 1), 0)))
        start += part
    out = pl.BlockSpec((tile, width), lambda i: (i, 0))
    return tile_call(functools.partial(rows_kernel, parts), [left, right, *gots], specs,
                     jax.ShapeDtypeStruct((count * tile, width), bf16), out, (count,), "rows")


def parity_groups():
    n = lax.axis_size("row")
    return [list(range(p, n, 2)) for p in range(2)]


def after(x, *earlier):
    return lax.optimization_barrier((x,) + earlier)[0]


def gather_parity(shard):
    return lax.all_gather(shard, "row", axis=0, tiled=True, axis_index_groups=parity_groups())


def scatter_parity(part):
    return lax.psum_scatter(part, "row", scatter_dimension=0, tiled=True, axis_index_groups=parity_groups())


def all_rows(left, right):
    rows, tile, width = left.shape[0], left.shape[1] // 4, right.shape[1]
    odd = (lax.axis_index("row") & 1).astype(jnp.int32).reshape(1)

    def kernel(odd_ref, left_ref, right_ref, out_ref):
        out_ref[...] = dot(left_ref[...], right_ref[...], 0, 0).astype(bf16)

    return tile_call(kernel, [left, right], [pl.BlockSpec((rows, tile), lambda i, m: (0, i)), whole(right.shape)],
                     jax.ShapeDtypeStruct((4 * tile, width), bf16),
                     pl.BlockSpec((tile, width), lambda i, m: (2 * ((i // 2) ^ m[0]) + i % 2, 0)), (4,), "all_rows", odd)


def scatter_rows(part):
    even, odd = parity_groups()
    return lax.psum_scatter(part, "row", scatter_dimension=0, tiled=True, axis_index_groups=[even + odd])


def trade_rows(left, right, parts=(2,), width=None):
    tile = left.shape[1] // 2 // sum(parts)
    sent, first = [], sum(parts)
    for part in parts:
        sent.append(rows_call(left, right, first, (part,), tile, width=width))
        first += part
    return sent, [swap(part, "row", 1) for part in sent]


def got_width(gots):
    return gots[0].shape[1]


def own_rows(left, right, gots, *earlier):
    first = after(gots[0], *gots[1:], *earlier)
    tile = 512 if len(gots) == 1 else min(got.shape[0] for got in gots)
    parts = tuple(got.shape[0] // tile for got in gots)
    return rows_call(left, right, 0, parts, tile, [first, *gots[1:]], got_width(gots))


def flip(first, second):
    odd = (lax.axis_index("row") & 1) == 1
    return jnp.where(odd, second, first), jnp.where(odd, first, second)


def by_parity(x, chunk):
    lead, width = x.shape
    parts = x.reshape(lead, width // (2 * chunk), 2, chunk)
    first, second = flip(parts[:, :, 0], parts[:, :, 1])
    return jnp.concatenate([first.reshape(lead, width // 2), second.reshape(lead, width // 2)], 1)


def by_place(x, chunk):
    lead, width = x.shape
    shape = (lead, width // (2 * chunk), chunk)
    first, second = flip(x[:, : width // 2].reshape(shape), x[:, width // 2 :].reshape(shape))
    return jnp.stack([first, second], 2).reshape(lead, width)


def per_device(tokens, lengths, norm_in, q_weight, k_weight, v_weight, conv_q, conv_k, conv_v, beta_weight,
               head_gain, out_weight, norm_mid, gate_weight, up_weight, down_weight, cotangent):
    rows, width = tokens.shape
    dh = head_gain.shape[0]
    hd = q_weight.shape[1]
    heads = hd // dh
    ff = gate_weight.shape[1]
    col = lax.axis_index("col")
    feat = lax.axis_size("col") * width
    live = live_column(lengths[0], rows)
    live_low = live.astype(bf16)
    in_mine = gather_parity(jnp.concatenate([q_weight, k_weight, v_weight], 1))
    out_mine = gather_parity(out_weight.T)
    gate_mine = gather_parity(gate_weight)
    up_mine = gather_parity(up_weight)
    down_turned = down_weight.T
    down_side = swap(down_turned, "row", 1)
    down_both = with_layout_constraint(jnp.concatenate([down_turned, down_side], 0), Layout((0, 1)))
    down_rows = with_layout_constraint(gather_parity(down_both), Layout((0, 1))).reshape(-1, 2, *down_turned.shape)
    conv = jnp.concatenate([conv_q, conv_k, conv_v], 1)
    gain = head_gain.reshape(1, dh)
    gain_in = lax.dynamic_slice_in_dim(norm_in, col * width, width)
    gain_mid = lax.dynamic_slice_in_dim(norm_mid, col * width, width)
    chunk = q_weight.shape[0]
    tokens, cotangent = by_parity(tokens, chunk), by_parity(cotangent, chunk)
    gain_in, gain_mid = by_parity(gain_in[None], chunk), by_parity(gain_mid[None], chunk)
    norm_in, norm_mid = by_parity(norm_in[None], chunk), by_parity(norm_mid[None], chunk)
    tokens32 = tokens.astype(f32)

    block = width // 2

    half = feat // 2
    normed, factor_in = join_norm(spread_cols(tokens), norm_in)
    ffn_cot = join(spread_cols(after(cotangent * live_low, down_side)))
    w_beta = gather_narrow(beta_weight)
    in_mine = after(in_mine, normed, ffn_cot, *w_beta)
    in_other, out_other = swap(in_mine, "row", 1), swap(out_mine, "row", 1)
    proj = proj_call(after(normed, out_mine), (in_mine, in_other), w_beta)
    gate_mine = after(gate_mine, proj)
    gate_other = swap(gate_mine, "row", 1)
    proj = after(proj, gate_mine)
    out_other = after(out_other, proj)
    w_in, w_out = (in_mine, in_other), (out_mine, out_other)
    mixed, *kept = mixer_forward(proj, conv, gain, heads, dh)
    branch = ColSum([(mixed, w_out)], block)
    sent = branch.send(1)
    sent = branch.send_last(*sent)
    up_mine = after(up_mine, *sent)
    up_other = swap(up_mine, "row", 1)
    middle = tokens32 + live * after(branch.total(), gate_other)
    mid_low = middle.astype(bf16)
    normed_mid, factor_mid = join_norm(spread_cols(mid_low), after(norm_mid, up_mine))
    w_gate, w_up = (gate_mine, gate_other), (up_mine, up_other)
    gate = halves(normed_mid, [(0, gate_mine), (1, gate_other)], bf16)
    up, hidden = hidden_call(after(normed_mid, gate), w_up, gate)
    down_sent = all_rows(ffn_cot, hidden)
    grad_down = scatter_rows(down_sent)
    w_down = (after(down_rows, down_sent),) * 2
    gate_cot, up_cot, inner_mid = cots_call(ffn_cot, w_down, gate, up)
    inner_mid = sum_all(inner_mid.reshape(rows // 128, 128), "col").reshape(rows, 1) / factor_mid
    mid_sum = ColSum([(gate_cot, w_gate), (up_cot, w_up)], block)
    sent = mid_sum.send(1)
    gate_sent, gate_got = trade_rows(after(normed_mid, *sent), gate_cot)
    mid_sum.send_last(inner_mid, gate_sent[0])
    up_sent, up_got = trade_rows(after(normed_mid, mid_sum.base), up_cot)
    mid_sum.got[0] = after(mid_sum.got[0], *up_sent)
    mid_cot = mid_sum.total()

    mid32 = mid_low.astype(f32)
    gmid_part = jnp.sum(mid_cot * mid32 * factor_mid, axis=0)
    middle_cot = cotangent.astype(f32) + factor_mid * gain_mid * mid_cot - mid32 * (factor_mid**3 * inner_mid / feat)
    branch_low = (live * middle_cot).astype(bf16)
    pieces = spread_cols(branch_low)
    gate_rows = own_rows(normed_mid, gate_cot, gate_got, pieces[2])
    grad_gate = scatter_parity(gate_rows)
    branch_cot = join(pieces)
    mixed_cot = halves(branch_cot, [(0, out_mine), (1, out_other)])
    out_sent, out_got = trade_rows(after(branch_cot, mixed_cot), mixed)
    mixed_cot = after(mixed_cot, *out_sent)
    low, gconv, ghead, inner_in = mixer_backward(proj, conv, gain, mixed_cot, kept, heads, dh)
    in_sum = ColSum([(low, w_in), (low, w_beta, 3 * hd // 128)], block)
    sent = in_sum.send(1)
    low_sent, low_got = trade_rows(after(normed, *sent), low, width=3 * hd)
    beta_part = by_place(dot(low[:, 3 * hd :], after(normed, *low_sent), 0, 0)[: beta_weight.shape[1]], chunk)
    inner_in = sum_all(inner_in.reshape(rows // 128, 128), "col").reshape(rows, 1) / factor_in
    in_sum.send_last(inner_in, *low_sent)
    up_rows = own_rows(normed_mid, up_cot, up_got, *out_got, in_sum.base, grad_down)
    grad_up = scatter_parity(up_rows)
    out_rows = own_rows(branch_cot, mixed, out_got, grad_gate, up_rows)
    grad_out = scatter_parity(out_rows)
    in_cot = in_sum.total()
    gin_part = jnp.sum(in_cot * tokens32 * factor_in, axis=0)
    grad_tokens = middle_cot + factor_in * gain_in * in_cot - tokens32 * (factor_in**3 * inner_in / feat)

    def own_cols(part):
        part = by_place(part[None], chunk)[0]
        return lax.dynamic_update_slice_in_dim(jnp.zeros((feat,), f32), part, col * width, 0)

    sizes = [feat, feat, dh]
    wide = sum_all(jnp.concatenate([own_cols(gin_part), own_cols(gmid_part), ghead[0]]).reshape(-1, 128), "col")
    small = jnp.concatenate([wide, gconv.reshape(-1, 128), beta_part.reshape(-1, 128)], 0)
    bits = bits_down(lax.axis_size("row"))
    for bit in bits[:-1]:
        small = small + swap(small, "row", bit)
    low_rows = own_rows(normed, low, low_got, out_rows, grad_up, small, grad_tokens)
    grad_low = scatter_parity(low_rows)
    in_cot = in_sum.total()
    gin_part = jnp.sum(in_cot * tokens32 * factor_in, axis=0)
    grad_tokens = middle_cot + factor_in * gain_in * in_cot - tokens32 * (factor_in**3 * inner_in / feat)

    def own_cols(part):
        part = by_place(part[None], chunk)[0]
        return lax.dynamic_update_slice_in_dim(jnp.zeros((feat,), f32), part, col * width, 0)

    sizes = [feat, feat, dh]
    wide = sum_all(jnp.concatenate([own_cols(gin_part), own_cols(gmid_part), ghead[0]]).reshape(-1, 128), "col")
    small = jnp.concatenate([wide, gconv.reshape(-1, 128), beta_part.reshape(-1, 128)], 0)
    bits = bits_down(lax.axis_size("row"))
    for bit in bits[:-1]:
        small = small + swap(small, "row", bit)
    low_rows = own_rows(normed, low, low_got, out_rows, grad_up, small, grad_tokens)
    grad_low = scatter_parity(low_rows)
    result = ColSum([(hidden, w_down)], block)
    sent = result.send(1, low_rows)
    result.send_last(*sent)
    layer_out = (middle + live * result.total()).astype(bf16)
    small = small + swap(small, "row", bits[-1])
    cuts = [wide.shape[0], wide.shape[0] + gconv.size // 128]
    wide, gconv = small[: cuts[0]].reshape(-1), small[cuts[0] : cuts[1]].reshape(gconv.shape)
    beta_sum = small[cuts[1] :].reshape(beta_part.shape)
    grad_beta = lax.dynamic_slice_in_dim(beta_sum, lax.axis_index("row") * chunk, chunk, 1).T
    g_low = grad_low.astype(f32)
    return (
        by_place(layer_out, chunk),
        by_place(grad_tokens, chunk),
        wide[:feat],
        g_low[:, :hd],
        g_low[:, hd : 2 * hd],
        g_low[:, 2 * hd : 3 * hd],
        gconv[:, :hd],
        gconv[:, hd : 2 * hd],
        gconv[:, 2 * hd :],
        grad_beta,
        wide[2 * feat :],
        grad_out.astype(f32).T,
        wide[feat : 2 * feat],
        grad_gate.astype(f32),
        grad_up.astype(f32),
        grad_down.astype(f32).T,
    )


def solution(mesh):
    split_both, features, turned = P("row", "col"), P(None, "col"), P("col", "row")
    return jax.shard_map(
        per_device,
        mesh=mesh,
        in_specs=(split_both, P("row"), P(), split_both, split_both, split_both, features, features, features,
                  split_both, P(), turned, P(), split_both, split_both, turned, split_both),
        out_specs=(split_both, split_both, P(), split_both, split_both, split_both, features, features, features,
                   split_both, P(), turned, P(), split_both, split_both, turned),
        check_vma=False,
    )
```
